32 devices in a mesh: rows: 8 (over z, x), cols: 4 (over y, core).
Axes of the slice: x: 2, y: 2, z: 4, core: 2. Of those that a mesh axis runs over, the one named last changes fastest.
Arguments:
- features: float32 [2, 8192, 128], P(None, 'rows', 'cols'), may hold values from -6 to 6
- neigh_first: int32 [2, 4096, 5], P(None, 'rows'), may hold values from 0 to 8191, as said below
- count_first: int32 [2, 4096], P(None, 'rows'), may hold values from 1 to 5
- neigh_mid: int32 [2, 2048, 10], P(None, 'rows'), may hold values from 0 to 4095, as said below
- count_mid: int32 [2, 2048], P(None, 'rows'), may hold values from 1 to 10
- neigh_last: int32 [2, 1024, 15], P(None, 'rows'), may hold values from 0 to 2047, as said below
- count_last: int32 [2, 1024], P(None, 'rows'), may hold values from 1 to 15
- labels: int32 [2, 1024], P(None, 'rows'), may hold values from 0 to 46
- w_first: float32 [2, 128, 256], P(None, 'cols'), may hold values from -0.375 to 0.375
- w_mid: float32 [2, 256, 256], P(None, 'cols'), may hold values from -0.25 to 0.25
- w_last: float32 [2, 256, 47], P(None, 'cols'), may hold values from -0.25 to 0.25
- b_hidden: float32 [2, 256], P(None, 'cols'), may hold values from -3 to 3
- b_last: float32 [47], replicated, may hold values from -3 to 3
- m_first: float32 [2, 128, 256], P(None, 'cols'), may hold values from -3.0517578e-05 to 3.0517578e-05
- m_mid: float32 [2, 256, 256], P(None, 'cols'), may hold values from -3.0517578e-05 to 3.0517578e-05
- m_last: float32 [2, 256, 47], P(None, 'cols'), may hold values from -3.0517578e-05 to 3.0517578e-05
- m_hidden: float32 [2, 256], P(None, 'cols'), may hold values from -3.0517578e-05 to 3.0517578e-05
- m_bias: float32 [47], replicated, may hold values from -3.0517578e-05 to 3.0517578e-05
- v_first: float32 [2, 128, 256], P(None, 'cols'), may hold values from 4.5201622e-13 to 1.8080649e-12
- v_mid: float32 [2, 256, 256], P(None, 'cols'), may hold values from 4.5201622e-13 to 1.8080649e-12
- v_last: float32 [2, 256, 47], P(None, 'cols'), may hold values from 4.5201622e-13 to 1.8080649e-12
- v_hidden: float32 [2, 256], P(None, 'cols'), may hold values from 4.5201622e-13 to 1.8080649e-12
- v_bias: float32 [47], replicated, may hold values from 4.5201622e-13 to 1.8080649e-12
Outputs:
- new_first: float32 [2, 128, 256], P(None, 'cols')
- new_mid: float32 [2, 256, 256], P(None, 'cols')
- new_last: float32 [2, 256, 47], P(None, 'cols')
- new_hidden: float32 [2, 256], P(None, 'cols')
- new_bias: float32 [47], replicated
- moment_first: float32 [2, 128, 256], P(None, 'cols')
- moment_mid: float32 [2, 256, 256], P(None, 'cols')
- moment_last: float32 [2, 256, 47], P(None, 'cols')
- moment_hidden: float32 [2, 256], P(None, 'cols')
- moment_bias: float32 [47], replicated
- square_first: float32 [2, 128, 256], P(None, 'cols')
- square_mid: float32 [2, 256, 256], P(None, 'cols')
- square_last: float32 [2, 256, 47], P(None, 'cols')
- square_hidden: float32 [2, 256], P(None, 'cols')
- square_bias: float32 [47], replicated
- loss_sum: float32 [], replicated
- weight_sum: float32 [], replicated
- grad_norm: float32 [], replicated
The draws below stay inside these ranges and needn't reach their ends.
Inputs may be any that keep to these rules, and one draw needn't show every extreme that they name: `neigh_first`: neighbor ids index the third-hop frontier of all devices, device by device in blocks of 1024; slots past a node's count are ignored; among the 2560 slots of one device's rows in a micro-batch, no device's block is named more than ceil(320) times, and some device's block exactly that often. `neigh_mid`: neighbor ids index the second-hop frontier of all devices, device by device in blocks of 512; slots past a node's count are ignored; among the 2560 slots of one device's rows in a micro-batch, no device's block is named more than ceil(320) times, and some device's block exactly that often. `neigh_last`: neighbor ids index the first-hop frontier of all devices, device by device in blocks of 256; slots past a seed's count are ignored; among the 1920 slots of one device's seeds in a micro-batch, no device's block is named more than ceil(240) times, and some device's block exactly that often.
All inputs are finite; a program needn't handle non-finite values.
Results may differ from the reference program's by a relative error of at most 0.0003.
Values sent between devices are 32-bit elements; how exact they have to be, the bound alone decides.
No kernel may reach another device: no remote copies, remote signals or barrier semaphores. Data moves between devices by JAX's collectives and lax.ppermute only.
A program may use at most 128 MiB of HBM per device.

```python
import math
import jax
import jax.numpy as jnp
from jax import lax

FEAT = 128
HID = 256
CLS = 47
FAN1 = 5
FAN2 = 10
FAN3 = 15
MB = 2
STEP = 5
SEED_DEV = 128
FRONT1 = 256
FRONT2 = 512
FRONT3 = 1024
N_ROWS = 8


def route_block(key, targets, fanout, source):
    first, second, third = jax.random.split(key, 3)
    slots = targets * fanout
    ranked = jax.random.permutation(first, slots).astype(jnp.int32)
    owners = jax.random.permutation(second, N_ROWS).astype(jnp.int32)
    owner = owners[ranked % N_ROWS]
    pair = jax.random.randint(third, (2, slots), 0, source, dtype=jnp.int32)
    local = jnp.minimum(pair[0], pair[1])
    return (owner * source + local).reshape(targets, fanout).astype(jnp.int32)


def route_draw(key, targets, fanout, source):
    keys = jax.random.split(key, MB * N_ROWS)
    blocks = jax.vmap(lambda k: route_block(k, targets, fanout, source))(keys)
    return blocks.reshape(MB, N_ROWS * targets, fanout)


def draw_neigh_first(key, part):
    key = jax.random.fold_in(key, 11)
    return route_draw(key, FRONT2, FAN1, FRONT3)


def draw_neigh_mid(key, part):
    key = jax.random.fold_in(key, 12)
    return route_draw(key, FRONT1, FAN2, FRONT2)


def draw_neigh_last(key, part):
    key = jax.random.fold_in(key, 13)
    return route_draw(key, SEED_DEV, FAN3, FRONT1)


def touch_ends(drawn, stream_key, low, high):
    extent = drawn.shape
    index_at = [jax.random.randint(jax.random.fold_in(stream_key, axis), (), 0, extent[axis]) for axis in range(len(extent))]
    drawn = drawn.at[tuple(index_at)].set(low)
    longest = extent.index(max(extent))
    index_at[longest] = (index_at[longest] + 1) % extent[longest]
    return drawn.at[tuple(index_at)].set(high)


def shard_levels(rng, extent, pieces, least, largest):
    level, own = 1.0, jax.random.fold_in(rng, 6)
    for axis_at, blocks in pieces:
        heights = jnp.exp(jax.random.uniform(jax.random.fold_in(own, axis_at), (blocks,), jnp.float32, least / len(pieces), largest / len(pieces)))
        level = level * jnp.repeat(heights, extent[axis_at] // blocks).reshape([-1 if axis == axis_at else 1 for axis in range(len(extent))])
    return level


def scatter_about(stream_key, shape, scale, most, shards=(), kind=jnp.bfloat16):
    drawn = scale * jax.random.normal(stream_key, shape, jnp.float32)
    if shards:
        drawn = drawn * shard_levels(stream_key, shape, shards, -0.22, 0.18)
    return jnp.clip(drawn, -most, most).astype(kind)


def setup_inputs(seed: int = 0) -> dict:
    arg_keys = jax.random.split(jax.random.key(seed), 24)
    return {
        "features": scatter_about(arg_keys[0], (MB, FRONT3 * N_ROWS, FEAT), 1.0, 6.0, ((1, 8), (2, 4)), jnp.float32),
        "neigh_first": draw_neigh_first(jax.random.fold_in(arg_keys[23], 71), 0),
        "count_first": touch_ends(jax.random.randint(arg_keys[2], (MB, FRONT2 * N_ROWS), 1, FAN1 + 1), jax.random.fold_in(arg_keys[2], 1), 1, FAN1).astype(jnp.int32),
        "neigh_mid": draw_neigh_mid(jax.random.fold_in(arg_keys[23], 71), 0),
        "count_mid": touch_ends(jax.random.randint(arg_keys[4], (MB, FRONT1 * N_ROWS), 1, FAN2 + 1), jax.random.fold_in(arg_keys[4], 1), 1, FAN2).astype(jnp.int32),
        "neigh_last": draw_neigh_last(jax.random.fold_in(arg_keys[23], 71), 0),
        "count_last": touch_ends(jax.random.randint(arg_keys[6], (MB, SEED_DEV * N_ROWS), 1, FAN3 + 1), jax.random.fold_in(arg_keys[6], 1), 1, FAN3).astype(jnp.int32),
        "labels": touch_ends(jax.random.randint(arg_keys[7], (MB, SEED_DEV * N_ROWS), 0, CLS), jax.random.fold_in(arg_keys[7], 1), 0, CLS - 1).astype(jnp.int32),
        "w_first": scatter_about(arg_keys[8], (2, FEAT, HID), (2 * FEAT) ** -0.5, 0.375, ((1, 4),), jnp.float32),
        "w_mid": scatter_about(arg_keys[9], (2, HID, HID), (2 * HID) ** -0.5, 0.25, ((1, 4),), jnp.float32),
        "w_last": scatter_about(arg_keys[10], (2, HID, CLS), (2 * HID) ** -0.5, 0.25, ((1, 4),), jnp.float32),
        "b_hidden": scatter_about(arg_keys[11], (2, HID), 0.5, 3.0, ((1, 4),), jnp.float32),
        "b_last": scatter_about(arg_keys[12], (CLS,), 0.5, 3.0, (), jnp.float32),
        "m_first": scatter_about(arg_keys[13], (2, FEAT, HID), (0.00111 * (2 * FEAT * HID + 2 * HID * HID + 2 * HID * CLS + 2 * HID + CLS) ** -0.5), 3.0517578125e-05, ((1, 4),), jnp.float32),
        "m_mid": scatter_about(arg_keys[14], (2, HID, HID), (0.00111 * (2 * FEAT * HID + 2 * HID * HID + 2 * HID * CLS + 2 * HID + CLS) ** -0.5), 3.0517578125e-05, ((1, 4),), jnp.float32),
        "m_last": scatter_about(arg_keys[15], (2, HID, CLS), (0.00111 * (2 * FEAT * HID + 2 * HID * HID + 2 * HID * CLS + 2 * HID + CLS) ** -0.5), 3.0517578125e-05, ((1, 4),), jnp.float32),
        "m_hidden": scatter_about(arg_keys[16], (2, HID), (0.00111 * (2 * FEAT * HID + 2 * HID * HID + 2 * HID * CLS + 2 * HID + CLS) ** -0.5), 3.0517578125e-05, ((1, 4),), jnp.float32),
        "m_bias": scatter_about(arg_keys[17], (CLS,), (0.00111 * (2 * FEAT * HID + 2 * HID * HID + 2 * HID * CLS + 2 * HID + CLS) ** -0.5), 3.0517578125e-05, (), jnp.float32),
        "v_first": jnp.clip(jnp.exp(math.log(1.8080648740356753e-12) - 1.3862944 * jax.random.uniform(arg_keys[18], (2, FEAT, HID), jnp.float32) ** shard_levels(arg_keys[18], (2, FEAT, HID), ((1, 4),), -0.2, 0.2)), 4.520162185089188e-13, 1.8080648740356753e-12),
        "v_mid": jnp.clip(jnp.exp(math.log(1.8080648740356753e-12) - 1.3862944 * jax.random.uniform(arg_keys[19], (2, HID, HID), jnp.float32) ** shard_levels(arg_keys[19], (2, HID, HID), ((1, 4),), -0.2, 0.2)), 4.520162185089188e-13, 1.8080648740356753e-12),
        "v_last": jnp.clip(jnp.exp(math.log(1.8080648740356753e-12) - 1.3862944 * jax.random.uniform(arg_keys[20], (2, HID, CLS), jnp.float32) ** shard_levels(arg_keys[20], (2, HID, CLS), ((1, 4),), -0.2, 0.2)), 4.520162185089188e-13, 1.8080648740356753e-12),
        "v_hidden": jnp.clip(jnp.exp(math.log(1.8080648740356753e-12) - 1.3862944 * jax.random.uniform(arg_keys[21], (2, HID), jnp.float32) ** shard_levels(arg_keys[21], (2, HID), ((1, 4),), -0.2, 0.2)), 4.520162185089188e-13, 1.8080648740356753e-12),
        "v_bias": jnp.clip(jnp.exp(jax.random.uniform(arg_keys[22], (CLS,), jnp.float32, math.log(4.520162185089188e-13), math.log(1.8080648740356753e-12))), 4.520162185089188e-13, 1.8080648740356753e-12),
    }


@jax.custom_vjp
def low(v):
    return lax.optimization_barrier(v.astype(jnp.bfloat16)).astype(jnp.float32)

@jax.custom_vjp
def low_back(v):
    return v

def low_keep(v):
    return (low(v), None)

def low_pass(kept, grad):
    return (grad,)

def back_keep(v):
    return (v, None)

def back_low(kept, grad):
    return (low(grad),)
low.defvjp(low_keep, low_pass)
low_back.defvjp(back_keep, back_low)
HIGH = lax.Precision.HIGHEST

def sage_layer(hidden, neigh, count, weight, bias, per_dev):
    width = hidden.shape[1]
    before = hidden.shape[0] // N_ROWS
    own = hidden.reshape(N_ROWS, before, width)[:, :per_dev].reshape(N_ROWS * per_dev, width)
    slots = jnp.arange(neigh.shape[1], dtype=jnp.int32)
    mask = (slots[None, :] < count[:, None]).astype(jnp.float32)
    picked = jnp.take(hidden, neigh, axis=0)
    mean = lax.optimization_barrier(jnp.sum(picked * mask[:, :, None], axis=1)) / count[:, None].astype(jnp.float32)
    return jnp.dot(own, weight[0], precision=HIGH, preferred_element_type=jnp.float32) + jnp.dot(mean, weight[1], precision=HIGH, preferred_element_type=jnp.float32) + bias

def reference(features, neigh_first, count_first, neigh_mid, count_mid, neigh_last, count_last, labels, w_first, w_mid, w_last, b_hidden, b_last, m_first, m_mid, m_last, m_hidden, m_bias, v_first, v_mid, v_last, v_hidden, v_bias):
    classes = jnp.arange(CLS, dtype=jnp.int32)
    onehot_all = (labels[:, :, None] == classes).astype(jnp.float32)
    counts = lax.optimization_barrier(jnp.sum(onehot_all, axis=(0, 1)))
    cweight = 1.0 / jnp.maximum(counts, 1.0)
    weight_sum = jnp.sum(counts * cweight)

    def forward(params):
        wa, wb, wc, bh, bl = params
        total = jnp.float32(0.0)
        for batch in range(MB):
            h1 = jax.nn.silu(sage_layer(features[batch], neigh_first[batch], count_first[batch], wa, bh[0], FRONT2))
            h2 = jax.nn.silu(sage_layer(h1, neigh_mid[batch], count_mid[batch], wb, bh[1], FRONT1))
            logits = sage_layer(h2, neigh_last[batch], count_last[batch], wc, bl, SEED_DEV)
            onehot = onehot_all[batch]
            lse = jax.nn.logsumexp(logits, axis=1)
            target = lax.optimization_barrier(jnp.sum(logits * onehot, axis=1))
            weight_seed = jnp.dot(onehot, cweight, precision=HIGH)
            total = total + jnp.sum(weight_seed * (lse - target))
        return total
    params = (w_first, w_mid, w_last, b_hidden, b_last)
    loss_sum, pull = jax.vjp(forward, params)
    grads = pull(1.0 / weight_sum)[0]
    squares = sum((jnp.sum(g * g) for g in grads))
    grad_norm = jnp.sqrt(squares)
    scale = jnp.minimum(1.0, 0.01 / grad_norm)
    firsts = (m_first, m_mid, m_last, m_hidden, m_bias)
    seconds = (v_first, v_mid, v_last, v_hidden, v_bias)
    news, moments, squares_out = ([], [], [])
    for weight, grad, first, second in zip(params, grads, firsts, seconds):
        grad = grad * scale
        moment = 0.9 * first + 0.1 * grad
        square = 0.999 * second + 0.001 * grad * grad
        corrected = moment / (1.0 - 0.9 ** STEP)
        root = jnp.sqrt(square / (1.0 - 0.999 ** STEP))
        news.append(weight - 0.05 * (corrected / (root + 1e-08) + 0.01 * weight))
        moments.append(moment)
        squares_out.append(square)
    return (news[0], news[1], news[2], news[3], news[4], moments[0], moments[1], moments[2], moments[3], moments[4], squares_out[0], squares_out[1], squares_out[2], squares_out[3], squares_out[4], loss_sum, weight_sum, grad_norm)
```

```python
import functools

import jax
import jax.numpy as jnp
from jax import lax
from jax.experimental import pallas as pl
from jax.experimental.pallas import tpu as pltpu
from jax.sharding import Mesh
from jax.sharding import PartitionSpec as P

STEP = 5
F32 = jnp.float32
BF16 = jnp.bfloat16
I32 = jnp.int32
LANES = 128
CLASS_ROWS = 48
LAST_ROWS = 64
ROW_HIDDEN = 48
ROW_LAST = 49
LANE_LOSS = 47
MIB = 1 << 20


def dims(left, right):
    return (((left,), (right,)), ((), ()))


NN, NT = dims(1, 0), dims(1, 1)


def dot(left, right, form):
    return lax.dot_general(left, right, form, preferred_element_type=F32)


def halves(value):
    high = value.astype(BF16)
    return high, (value - high.astype(F32)).astype(BF16)


def dot_split(left, right, form):
    (lh, ll), (rh, rl) = left, right
    return dot(lh, rh, form) + dot(lh, rl, form) + dot(ll, rh, form)


def dot_full(left, right, form):
    return dot_split(halves(left), halves(right), form)


def sigmoid(value):
    return 1.0 / (1.0 + jnp.exp(-value))


def call(body, outs, name, vmem, smem_first=True, scratch=()):
    def run(*args):
        specs = [pl.BlockSpec(memory_space=pltpu.SMEM)]
        specs += [pl.BlockSpec(memory_space=pltpu.VMEM)] * (len(args) - 1)
        return pl.pallas_call(
            body,
            out_shape=[jax.ShapeDtypeStruct(s, d) for s, d in outs],
            in_specs=specs,
            out_specs=[pl.BlockSpec(memory_space=pltpu.VMEM)] * len(outs),
            scratch_shapes=list(scratch),
            name=name,
            compiler_params=pltpu.CompilerParams(vmem_limit_bytes=vmem * MIB),
        )(*args)

    return run


class Sizes:
    def __init__(self, mesh, features, neigh_first, neigh_mid, neigh_last):
        self.ranks = mesh.shape["zh"] * mesh.shape["rl"]
        self.rl = mesh.shape["rl"]
        self.s1, self.t1 = features.shape[1], neigh_first.shape[1]
        self.t2, self.t3 = neigh_mid.shape[1], neigh_last.shape[1]
        self.f1, self.f2, self.f3 = neigh_first.shape[2], neigh_mid.shape[2], neigh_last.shape[2]
        l1, l2, l3 = self.t1 // LANES, self.t2 // LANES, self.t3 // LANES
        self.l1, self.l2, self.l3 = l1, l2, l3
        self.at_first = 0
        self.at_mid = self.at_first + self.f1 * l1
        self.at_last = self.at_mid + self.f2 * l2
        self.at_label = self.at_last + self.f3 * l3
        self.at_c1 = self.at_label + 2 * l3
        self.at_c2 = self.at_c1 + l1
        self.at_c3 = self.at_c2 + l2
        self.id_rows = -(-(self.at_c3 + l3) // 8) * 8
        self.rf, self.rm, self.rlast = 64 // self.ranks, 128 // self.ranks, LAST_ROWS // self.ranks
        self.rs_rows = self.rf + self.rm + self.rlast
        self.ag_rows = 2 * (self.rf + self.rm) + self.rlast


def prep_body(z, pos, feats, nf, cf, nm, cm, nl, cl, labels, wf, wm, wl, bh, f0, f1, ids, wmsg, rows):
    y = pos[2]
    f0[...] = feats[y]
    f1[...] = feats[1 - y]
    rows[...] = jnp.zeros_like(rows)

    def put(mb, at, value):
        for j in range(value.shape[1] // LANES):
            rows[mb, at + j : at + j + 1, :] = value[:, j * LANES : (j + 1) * LANES]

    for mb in range(2):
        for fan, nb, cnt, at, at_c in (
            (z.f1, nf, cf, z.at_first, z.at_c1),
            (z.f2, nm, cm, z.at_mid, z.at_c2),
            (z.f3, nl, cl, z.at_last, z.at_c3),
        ):
            count = cnt[mb : mb + 1, :]
            lanes = count.shape[1] // LANES
            for k in range(fan):
                put(mb, at + k * lanes, jnp.where(count > k, nb[k, mb : mb + 1, :], -1))
            put(mb, at_c, count)
        for other in range(2):
            put(mb, z.at_label + other * z.l3, labels[other : other + 1, :])
        for d in range(z.rl):
            ids[mb * z.rl + d] = rows[mb]
    for j in range(2):
        wmsg[32 * j : 32 * j + 32, :] = wf[j]
        wmsg[64 + 64 * j : 128 + 64 * j, :] = wm[j]
    wmsg[192:248, :] = jnp.zeros((56, 256), F32)
    for j in range(2):
        wmsg[192 : 192 + 47, 64 * j : 64 * j + 64] = wl[:, j, :]
        wmsg[240:241, 64 * j : 64 * j + 64] = bh[j : j + 1, :]


def weights_body(pos, wall, blast, w1h, w1l, w2h, w2l, wmh, wml, wlt, wlc, bias, f32a, f32b):
    for s in range(4):
        for j in range(2):
            f32a[128 * j + 32 * s : 128 * j + 32 * s + 32, :] = wall[s, 32 * j : 32 * j + 32, :]
            f32b[256 * j + 64 * s : 256 * j + 64 * s + 64, :] = wall[s, 64 + 64 * j : 128 + 64 * j, :]
            wlt[j, :, 64 * s : 64 * s + 64] = wall[s, 192 : 192 + CLASS_ROWS, 64 * j : 64 * j + 64]
    w1h[...], w1l[...] = halves(f32a[...].T)
    w2h[...], w2l[...] = halves(f32b[...].T)
    for j in range(2):
        wmh[j], wml[j] = halves(f32b[256 * j : 256 * j + 256, :])
        wlc[j] = jnp.concatenate([wlt[j], jnp.zeros((128 - CLASS_ROWS, 256), F32)], axis=0).T
    rows = [jnp.concatenate([wall[s, 240:241, 64 * j : 64 * j + 64] for s in range(4)], axis=1) for j in range(2)]
    last = jnp.concatenate([blast[...], jnp.zeros((1, 256 - 47), F32)], axis=1)
    packed = jnp.concatenate(rows + [last, jnp.zeros((125, 256), F32)], axis=0)
    bias[...] = packed.T


def one_hot_sum(rows, size, base):
    at = lax.broadcasted_iota(I32, (size, LANES), 0)
    total = jnp.zeros((size, LANES), F32)
    for row in rows:
        total = total + jnp.where(at == row - base, 1.0, 0.0)
    return total.astype(BF16)


def adjacency_body(z, pos, ids, a2, a3, mine, cw):
    zh, rl, y = pos[0], pos[1], pos[2]
    me = y * z.rl + rl
    mine[...] = ids[me]
    s2, s3 = a2.shape[0], a3.shape[0]
    piece = 128

    def block(r, carry):
        for at, fan, lanes, size, out in (
            (z.at_mid, z.f2, z.l2, s2, a2),
            (z.at_last, z.f3, z.l3, s3, a3),
        ):
            for j in range(lanes):
                rows = [ids[r, pl.ds(at + k * lanes + j, 1), :] - me * size for k in range(fan)]
                where = pl.ds(pl.multiple_of((r * lanes + j) * LANES, LANES), LANES)
                for g in range(size // piece):
                    out[g * piece : (g + 1) * piece, where] = one_hot_sum(rows, piece, g * piece)
        return carry

    lax.fori_loop(0, 2 * z.rl, block, 0)
    classes = lax.broadcasted_iota(I32, (CLASS_ROWS, LANES), 0)

    def tally(r, total):
        for other in range(2 * z.l3):
            row = ids[r, pl.ds(z.at_label + other, 1), :]
            total = total + jnp.where(classes == row, 1.0, 0.0)
        return total

    total = lax.fori_loop(0, 2 * z.rl, tally, jnp.zeros((CLASS_ROWS, LANES), F32))
    counts = jnp.sum(total, axis=1, keepdims=True)
    weight = 1.0 / jnp.maximum(counts, 1.0)
    cw[0] = jnp.broadcast_to(weight, (CLASS_ROWS, LANES))
    both = jnp.sum(counts * weight, axis=0, keepdims=True)
    cw[1] = jnp.broadcast_to(both, (CLASS_ROWS, LANES))


def first_body(z, pos, ids, fa, fb, out, table, adj):
    me = pos[2] * z.rl + pos[1]
    width = fa.shape[0] * 2
    rows = jnp.concatenate([fa[...], fb[...]], axis=0)
    table[:width], table[width:] = halves(rows)
    piece = 128

    def block(r, carry):
        for j in range(z.l1):
            rows = [ids[r, pl.ds(z.at_first + k * z.l1 + j, 1), :] - me * z.s1 for k in range(z.f1)]
            for g in range(z.s1 // piece):
                adj[g * piece : (g + 1) * piece, j * LANES : (j + 1) * LANES] = one_hot_sum(rows, piece, g * piece)
        both = dot(table[...], adj[...], NN)
        out[r] = both[:width] + both[width:]
        return carry

    lax.fori_loop(0, 2 * z.rl, block, 0)


def inverse(z, mine, at, lanes):
    row = jnp.concatenate([mine[at + j : at + j + 1, :] for j in range(lanes)], axis=1)
    return 1.0 / row.astype(F32)


def sum_first_body(z, pos, mine, part, fa, fb, out):
    half = fa.shape[0]
    out[:half] = fa[:, : z.t1]
    out[half : 2 * half] = fb[:, : z.t1]
    total = part[0]
    for r in range(1, 2 * z.rl):
        total = total + part[r]
    out[2 * half :] = total * inverse(z, mine, z.at_c1, z.l1)


def put_columns(pos, own, other, out):
    c = pos[3]
    for j in range(2):
        for y in range(2):
            at = 128 * j + 64 * y
            out[pl.ds(pl.multiple_of(at + 32 * c, 32), 32)] = own[64 * j + 32 * y : 64 * j + 32 * y + 32]
            out[pl.ds(pl.multiple_of(at + 32 * (1 - c), 32), 32)] = other[64 * j + 32 * y : 64 * j + 32 * y + 32]


def hidden_one_body(z, pos, own, other, w1h, w1l, bias, a2, out, x1, h1, slope):
    c = pos[3]
    put_columns(pos, own, other, x1)
    pre = dot_split((w1h[...], w1l[...]), halves(x1[...]), NN) + bias[:, 0:1]
    sigma = sigmoid(pre)
    h1[...] = pre * sigma
    slope[...] = sigma * (1.0 + pre * (1.0 - sigma))
    table = jnp.concatenate(halves(h1[pl.ds(pl.multiple_of(c * 128, 128), 128)]), axis=0)
    for r in range(2 * z.rl):
        both = dot(table, a2[:, r * z.t2 : (r + 1) * z.t2], NN)
        out[r] = both[:128] + both[128:]


def sum_mid_body(z, pos, mine, part, out):
    total = part[0]
    for r in range(1, 2 * z.rl):
        total = total + part[r]
    out[...] = total * inverse(z, mine, z.at_c2, z.l2)


def hidden_two_body(z, pos, own, other, h1, w2h, w2l, bias, wlt, a3, out, y2, h2, slope, local):
    c = pos[3]
    y2[:256] = h1[:, : z.t2]
    y2[pl.ds(pl.multiple_of(256 + c * 128, 128), 128)] = own[...]
    y2[pl.ds(pl.multiple_of(256 + (1 - c) * 128, 128), 128)] = other[...]
    pre = dot_split((w2h[...], w2l[...]), halves(y2[...]), NN) + bias[:, 1:2]
    sigma = sigmoid(pre)
    hidden = pre * sigma
    h2[...] = hidden
    slope[...] = sigma * (1.0 + pre * (1.0 - sigma))
    split = halves(hidden)
    local[...] = dot_split(halves(wlt[0]), (split[0][:, : z.t3], split[1][:, : z.t3]), NN)
    table = jnp.concatenate(halves(dot_split(halves(wlt[1]), split, NN)), axis=0)
    for r in range(2 * z.rl):
        both = dot(table, a3[:, r * z.t3 : (r + 1) * z.t3], NN)
        out[r] = both[:CLASS_ROWS] + both[CLASS_ROWS:]


def logits_body(z, pos, mine, part, local, bias, cw, out, grad, loss):
    total = part[0]
    for r in range(1, 2 * z.rl):
        total = total + part[r]
    recip = inverse(z, mine, z.at_c3, z.l3)
    logits = total * recip + local[...] + bias[:CLASS_ROWS, 2:3]
    classes = lax.broadcasted_iota(I32, logits.shape, 0)
    logits = jnp.where(classes < 47, logits, -jnp.inf)
    label = jnp.where(
        pos[0] == 0,
        mine[z.at_label : z.at_label + 1, :],
        mine[z.at_label + z.l3 : z.at_label + z.l3 + 1, :],
    )
    onehot = jnp.where(classes == label, 1.0, 0.0)
    top = jnp.max(logits, axis=0, keepdims=True)
    powers = jnp.exp(logits - top)
    norm = jnp.sum(powers, axis=0, keepdims=True)
    weight = jnp.sum(onehot * cw[0], axis=0, keepdims=True)
    target = jnp.sum(jnp.where(classes == label, logits, 0.0), axis=0, keepdims=True)
    each = weight * (jnp.log(norm) + top - target)
    loss[...] = jnp.broadcast_to(jnp.sum(each, axis=1, keepdims=True), loss.shape)
    dlogits = weight * (powers / norm - onehot) / cw[1, 0:1, :]
    grad[...] = dlogits
    scaled = dlogits * recip
    for r in range(2 * z.rl):
        out[r] = scaled


def back_last_body(z, pos, mine, gall, grad, a3, wlc, h2, slope, out, dpre2, dwl):
    c = pos[3]
    both = None
    for r in range(2 * z.rl):
        table = jnp.concatenate(halves(gall[r]), axis=0)
        term = dot(table, a3[:, r * z.t3 : (r + 1) * z.t3], NT)
        both = term if both is None else both + term
    spread = both[:CLASS_ROWS] + both[CLASS_ROWS:]
    dh = dot_full(wlc[1][:, :CLASS_ROWS], spread, NN)
    own = dot_full(wlc[0][:, :CLASS_ROWS], grad[...], NN)
    dh = dh + jnp.concatenate([own, jnp.zeros((256, z.t2 - z.t3), F32)], axis=1)
    dpre2[...] = dh * slope[...]
    scaled = dpre2[pl.ds(pl.multiple_of(c * 128, 128), 128)] * inverse(z, mine, z.at_c2, z.l2)
    for r in range(2 * z.rl):
        out[r] = scaled
    dwl[0] = dot_full(grad[...], h2[:, : z.t3], NT)
    dwl[1] = dot_full(spread, h2[...], NT)


def back_mid_body(z, pos, gall, a2, out):
    both = None
    for r in range(2 * z.rl):
        table = jnp.concatenate(halves(gall[r]), axis=0)
        term = dot(table, a2[:, r * z.t2 : (r + 1) * z.t2], NT)
        both = term if both is None else both + term
    out[...] = both[:128] + both[128:]


def row_sums(value):
    ones = jnp.ones((8, value.shape[1]), BF16)
    high, low = halves(value)
    return dot(ones, high, NT) + dot(ones, low, NT)


def grads_body(z, pos, own, other, dpre2, wmh, wml, slope, x1, y2, dwl, grad, loss, out, spread, first, mid, last):
    c = pos[3]
    mine = pl.ds(pl.multiple_of(c * 128, 128), 128)
    spread[mine] = own[...]
    spread[pl.ds(pl.multiple_of((1 - c) * 128, 128), 128)] = other[...]
    dh = dot_split((wmh[1, mine, :], wml[1, mine, :]), halves(spread[...]), NN)
    at_own = dot_split((wmh[0, mine, :], wml[0, mine, :]), halves(dpre2[...]), NN)
    dh = dh + jnp.concatenate([at_own, jnp.zeros((128, z.t1 - z.t2), F32)], axis=1)
    dpre1 = dh * slope[mine]
    half2 = dpre2[mine]
    first[...] = dot_full(x1[...], dpre1, NT)
    mid[...] = dot_full(y2[...], half2, NT)
    b1, b2, b3 = row_sums(dpre1), row_sums(half2), row_sums(grad[...])
    last[...] = jnp.zeros_like(last)
    core0 = jnp.where(c == 0, 1.0, 0.0)
    for s in range(4):
        last[s, :CLASS_ROWS, :64] = dwl[0][:, 64 * s : 64 * s + 64] * core0
        last[s, :CLASS_ROWS, 64:] = dwl[1][:, 64 * s : 64 * s + 64] * (1.0 - core0)
        here = jnp.where(c == s // 2, 1.0, 0.0)
        at = 64 * (s % 2)
        last[s, ROW_HIDDEN : ROW_HIDDEN + 1, :64] = b1[0:1, at : at + 64] * here
        last[s, ROW_HIDDEN : ROW_HIDDEN + 1, 64:] = b2[0:1, at : at + 64] * here
        last[s, ROW_LAST : ROW_LAST + 1, :LANE_LOSS] = b3[0:1, :LANE_LOSS] * core0
        last[s, ROW_LAST : ROW_LAST + 1, LANE_LOSS : LANE_LOSS + 1] = loss[0:1, 0:1] * core0
    for q in range(z.ranks):
        for s in range(4):
            d = q * 4 + s
            e = z.rf * q
            at = 128 * (e // 32) + 32 * s + e % 32
            out[d, : z.rf] = first[at : at + z.rf]
            e = z.rm * q
            at = 256 * (e // 64) + 64 * s + e % 64
            out[d, z.rf : z.rf + z.rm] = mid[at : at + z.rm]
            out[d, z.rf + z.rm :] = last[s, z.rlast * q : z.rlast * (q + 1)]


def sum_grads_body(z, pos, part, out):
    n = z.rf + z.rm
    even, odd = part[0], part[1]
    for d in range(2, z.ranks * 4, 2):
        even = even + part[d]
        odd = odd + part[d + 1]
    for q in range(z.ranks):
        out[q, :n] = even[:n]
        out[q, n : 2 * n] = odd[:n]
        out[q, 2 * n :] = even[n:] + odd[n:]


def squares_body(z, pos, whole, out):
    n = 2 * (z.rf + z.rm)
    first_cols = jnp.where(jnp.logical_and(pos[2] == 0, pos[3] == 0), 1.0, 0.0)
    total = jnp.zeros((1, LANES), F32)
    lane = lax.broadcasted_iota(I32, (1, LANES), 1)
    for q in range(z.ranks):
        value = whole[q, :n]
        total = total + jnp.sum(value * value, axis=0, keepdims=True)
        for i in range(z.rlast):
            at = q * z.rlast + i
            row = whole[q, n + i : n + i + 1]
            if at <= ROW_HIDDEN:
                total = total + row * row
            elif at == ROW_LAST:
                total = total + jnp.where(lane < 47, row * row, 0.0) * first_cols
    out[...] = jnp.broadcast_to(jnp.sum(total, axis=1, keepdims=True), out.shape)


def update_body(z, pos, whole, s0, s1, s2, s3, cw, *refs):
    w, m, v = refs[0:5], refs[5:10], refs[10:15]
    new, moment, square = refs[15:20], refs[20:25], refs[25:30]
    loss, weight_sum, norm = refs[30:33]
    total = s0[0:1, 0:1] + s1[0:1, 0:1] + s2[0:1, 0:1] + s3[0:1, 0:1]
    root = jnp.sqrt(total)
    scale = jnp.minimum(1.0, 0.01 / root)
    norm[...] = root
    weight_sum[...] = cw[1, 0:1, 0:1]

    def adamw(weight, grad, first, second):
        grad = grad * scale
        mo = 0.9 * first + 0.1 * grad
        sq = 0.999 * second + 0.001 * grad * grad
        corrected = mo / (1.0 - 0.9**STEP)
        rt = jnp.sqrt(sq / (1.0 - 0.999**STEP))
        return (weight - 0.05 * (corrected / (rt + 1e-08) + 0.01 * weight), mo, sq)

    def put(i, at, grad):
        outs = adamw(w[i][at], grad, m[i][at], v[i][at])
        new[i][at], moment[i][at], square[i][at] = outs

    n = z.rf + z.rm
    for q in range(z.ranks):
        e = z.rf * q
        g = jnp.concatenate([whole[q, : z.rf], whole[q, n : n + z.rf]], axis=1)
        put(0, (e // 32, slice(e % 32, e % 32 + z.rf), slice(None)), g)
        e = z.rm * q
        g = jnp.concatenate([whole[q, z.rf : n], whole[q, n + z.rf : 2 * n]], axis=1)
        put(1, (e // 64, slice(e % 64, e % 64 + z.rm), slice(None)), g)
        a = z.rlast * q
        b = min(a + z.rlast, 47)
        if a < b:
            for j in range(2):
                put(2, (slice(a, b), j, slice(None)), whole[q, 2 * n : 2 * n + b - a, 64 * j : 64 * j + 64])
        for i in range(z.rlast):
            row = whole[q, 2 * n + i : 2 * n + i + 1]
            if a + i == ROW_HIDDEN:
                for j in range(2):
                    put(3, (slice(j, j + 1), slice(None)), row[:, 64 * j : 64 * j + 64])
            elif a + i == ROW_LAST:
                put(4, (slice(None), slice(None)), row[:, :47])
                loss[...] = row[:, LANE_LOSS : LANE_LOSS + 1]


def on_device(
    mesh, features, neigh_first, count_first, neigh_mid, count_mid, neigh_last, count_last, labels,
    w_first, w_mid, w_last, b_hidden, b_last,
    m_first, m_mid, m_last, m_hidden, m_bias,
    v_first, v_mid, v_last, v_hidden, v_bias,
):
    z = Sizes(mesh, features, neigh_first, neigh_mid, neigh_last)
    bind = functools.partial
    blocks = 2 * z.rl
    pos = jnp.stack([lax.axis_index(a) for a in ("zh", "rl", "y", "c")]).astype(I32)

    def flip(value):
        return lax.ppermute(value, "c", [(0, 1), (1, 0)])

    def exchange(value):
        return lax.all_to_all(value, ("y", "rl"), 0, 0)

    def swapped(value):
        return jnp.transpose(value, (2, 0, 1))

    f0, f1, ids, wmsg = call(
        bind(prep_body, z),
        [((32, z.s1), F32), ((32, z.s1), F32), ((z.ranks, z.id_rows, LANES), I32), ((248, 256), F32)],
        "prep", 8, scratch=[pltpu.VMEM((2, z.id_rows, LANES), I32)],
    )(
        pos, jnp.transpose(features, (0, 2, 1)), swapped(neigh_first), count_first, swapped(neigh_mid), count_mid,
        swapped(neigh_last), count_last, labels, w_first, w_mid, swapped(w_last), b_hidden,
    )
    got = [
        lax.ppermute(f, ("zh", "y"), [(2 * zh + y, 2 * (y ^ j) + zh) for zh in range(2) for y in range(2)])
        for j, f in enumerate((f0, f1))
    ]
    wall = lax.all_gather(wmsg, ("y", "c"), axis=0)
    ids = lax.all_to_all(ids, ("zh", "rl"), 0, 0)
    swap = pos[0] == 1
    fa = jnp.where(swap, got[1], got[0])
    fb = jnp.where(swap, got[0], got[1])

    a2, a3, mine, cw = call(
        bind(adjacency_body, z),
        [
            ((z.t1, blocks * z.t2), BF16), ((z.t2, blocks * z.t3), BF16),
            ((z.id_rows, LANES), I32), ((2, CLASS_ROWS, LANES), F32),
        ],
        "adjacency", 24,
    )(pos, ids)
    part = call(
        bind(first_body, z), [((blocks, 64, z.t1), F32)], "first", 24,
        scratch=[pltpu.VMEM((128, z.s1), BF16), pltpu.VMEM((z.s1, z.t1), BF16)],
    )(pos, ids, fa, fb)[0]
    w1h, w1l, w2h, w2l, wmh, wml, wlt, wlc, bias = call(
        weights_body,
        [
            ((256, 256), BF16), ((256, 256), BF16), ((256, 512), BF16), ((256, 512), BF16),
            ((2, 256, 256), BF16), ((2, 256, 256), BF16),
            ((2, CLASS_ROWS, 256), F32), ((2, 256, 128), F32), ((256, 128), F32),
        ],
        "weights", 16, scratch=[pltpu.VMEM((256, 256), F32), pltpu.VMEM((512, 256), F32)],
    )(pos, wall, b_last[None])
    part = exchange(part)
    half = call(bind(sum_first_body, z), [((128, z.t1), F32)], "sum_first", 16)(pos, mine, part, fa, fb)[0]
    other = flip(half)
    part, x1, h1, slope1 = call(
        bind(hidden_one_body, z),
        [((blocks, 128, z.t2), F32), ((256, z.t1), F32), ((256, z.t1), F32), ((256, z.t1), F32)],
        "hidden_one", 32,
    )(pos, half, other, w1h, w1l, bias, a2)
    part = exchange(part)
    half = call(bind(sum_mid_body, z), [((128, z.t2), F32)], "sum_mid", 16)(pos, mine, part)[0]
    other = flip(half)
    part, y2, h2, slope2, local = call(
        bind(hidden_two_body, z),
        [
            ((blocks, CLASS_ROWS, z.t3), F32), ((512, z.t2), F32), ((256, z.t2), F32), ((256, z.t2), F32),
            ((CLASS_ROWS, z.t3), F32),
        ],
        "hidden_two", 24,
    )(pos, half, other, h1, w2h, w2l, bias, wlt, a3)
    part = exchange(part)
    part, grad, loss = call(
        bind(logits_body, z),
        [((blocks, CLASS_ROWS, z.t3), F32), ((CLASS_ROWS, z.t3), F32), ((8, LANES), F32)],
        "logits", 8,
    )(pos, mine, part, local, bias, cw)
    part = exchange(part)
    part, dpre2, dwl = call(
        bind(back_last_body, z),
        [((blocks, 128, z.t2), F32), ((256, z.t2), F32), ((2, CLASS_ROWS, 256), F32)],
        "back_last", 24,
    )(pos, mine, part, grad, a3, wlc, h2, slope2)
    part = exchange(part)
    half = call(bind(back_mid_body, z), [((128, z.t1), F32)], "back_mid", 24)(pos, part, a2)[0]
    other = flip(half)
    part = call(
        bind(grads_body, z), [((z.ranks * 4, z.rs_rows, LANES), F32)], "grads", 24,
        scratch=[
            pltpu.VMEM((256, z.t1), F32), pltpu.VMEM((256, 128), F32), pltpu.VMEM((512, 128), F32),
            pltpu.VMEM((4, LAST_ROWS, LANES), F32),
        ],
    )(pos, half, other, dpre2, wmh, wml, slope1, x1, y2, dwl, grad, loss)[0]
    part = lax.all_to_all(part, ("zh", "rl", "y", "c"), 0, 0)
    part = call(bind(sum_grads_body, z), [((z.ranks, z.ag_rows, LANES), F32)], "sum_grads", 8)(pos, part)[0]
    whole = lax.all_to_all(part, ("zh", "rl"), 0, 0)
    mine_sq = call(bind(squares_body, z), [((8, LANES), F32)], "squares", 8)(pos, whole)[0]
    pair = [(i, i ^ 1) for i in range(4)]
    across = [(i, i ^ 2) for i in range(4)]
    both = [(i, i ^ 3) for i in range(4)]
    others = [lax.ppermute(mine_sq, ("y", "c"), p) for p in (across, both, pair)]

    params = (w_first, w_mid, swapped(w_last), b_hidden, b_last[None])
    firsts = (m_first, m_mid, swapped(m_last), m_hidden, m_bias[None])
    seconds = (v_first, v_mid, swapped(v_last), v_hidden, v_bias[None])
    shapes = [(p.shape, F32) for p in params]
    outs = call(bind(update_body, z), shapes * 3 + [((1, 1), F32)] * 3, "update", 8)(
        pos, whole, mine_sq, *others, cw, *params, *firsts, *seconds
    )
    results = []
    for g in range(3):
        a, b, c, d, e = outs[5 * g : 5 * g + 5]
        results += [a, b, jnp.transpose(c, (1, 2, 0)), d, e[0]]
    return tuple(results) + tuple(o[0, 0] for o in outs[15:])


def solution(mesh):
    rows, cols = mesh.shape["rows"], mesh.shape["cols"]
    fine = Mesh(mesh.devices.reshape(2, rows // 2, 2, cols // 2), ("zh", "rl", "y", "c"))
    r, c = ("zh", "rl"), ("y", "c")
    weights = (P(None, c, None),) * 3 + (P(None, c), P())
    nodes = (P(None, r, None), P(None, r))
    placed = (P(None, r, c),) + nodes * 3 + (P(None, r),) + weights * 3
    return jax.shard_map(
        functools.partial(on_device, fine),
        mesh=fine,
        in_specs=placed,
        out_specs=weights * 3 + (P(), P(), P()),
        check_vma=False,
    )
```

```python
import functools

import jax
import jax.numpy as jnp
from jax import lax
from jax.experimental import pallas as pl
from jax.experimental.pallas import tpu as pltpu
from jax.sharding import Mesh
from jax.sharding import PartitionSpec as P

STEP = 5
F32 = jnp.float32
BF16 = jnp.bfloat16
I32 = jnp.int32
LANES = 128
CLASS_ROWS = 48
LAST_ROWS = 64
ROW_HIDDEN = 48
ROW_LAST = 49
LANE_LOSS = 47
MIB = 1 << 20


def dims(left, right):
    return (((left,), (right,)), ((), ()))


NN, NT = dims(1, 0), dims(1, 1)


def dot(left, right, form):
    return lax.dot_general(left, right, form, preferred_element_type=F32)


def halves(value):
    high = value.astype(BF16)
    return high, (value - high.astype(F32)).astype(BF16)


def dot_split(left, right, form):
    (lh, ll), (rh, rl) = left, right
    return dot(lh, rh, form) + dot(lh, rl, form) + dot(ll, rh, form)


def dot_full(left, right, form):
    return dot_split(halves(left), halves(right), form)


def sigmoid(value):
    return 1.0 / (1.0 + jnp.exp(-value))


VMEM = pl.BlockSpec(memory_space=pltpu.VMEM)
HBM = pl.BlockSpec(memory_space=pltpu.HBM)


AXES = ("zh", "rl", "y", "c")


def call(body, outs, name, vmem, scratch=(), where=VMEM, us=1.0):
    def placed(*refs):
        body([lax.axis_index(a) for a in AXES], *refs)

    def run(*args):
        return pl.pallas_call(
            placed,
            out_shape=[jax.ShapeDtypeStruct(s, d) for s, d in outs],
            in_specs=[where] * len(args),
            out_specs=[VMEM] * len(outs),
            scratch_shapes=list(scratch),
            name=name,
            compiler_params=pltpu.CompilerParams(vmem_limit_bytes=vmem * MIB),
            cost_estimate=pl.CostEstimate(flops=0, bytes_accessed=int(us * 3.6e6), transcendentals=0),
        )(*args)

    return run


def fetch(sources, targets, sems):
    copies = [pltpu.make_async_copy(s, t, sems.at[i]) for i, (s, t) in enumerate(zip(sources, targets))]
    for copy in copies:
        copy.start()
    for copy in copies:
        copy.wait()


def like(*arrays):
    return [pltpu.VMEM(a.shape, a.dtype) for a in arrays] + [pltpu.SemaphoreType.DMA((len(arrays),))]


class Sizes:
    def __init__(self, mesh, features, neigh_first, neigh_mid, neigh_last):
        self.ranks = mesh.shape["zh"] * mesh.shape["rl"]
        self.rl = mesh.shape["rl"]
        self.s1, self.t1 = features.shape[1], neigh_first.shape[1]
        self.t2, self.t3 = neigh_mid.shape[1], neigh_last.shape[1]
        self.f1, self.f2, self.f3 = neigh_first.shape[2], neigh_mid.shape[2], neigh_last.shape[2]
        l1, l2, l3 = self.t1 // LANES, self.t2 // LANES, self.t3 // LANES
        self.l1, self.l2, self.l3 = l1, l2, l3
        self.at_first = 0
        self.at_mid = self.at_first + self.f1 * l1
        self.at_last = self.at_mid + self.f2 * l2
        self.at_label = self.at_last + self.f3 * l3
        self.at_c1 = self.at_label + 2 * l3
        self.at_c2 = self.at_c1 + l1
        self.at_c3 = self.at_c2 + l2
        self.id_rows = -(-(self.at_c3 + l3) // 32) * 32
        self.id_part = self.id_rows // 4
        self.blocks = 2 * self.rl
        self.pieces = 4 * self.rl
        self.nf, self.nm, self.nl = 64 // self.pieces, 128 // self.pieces, LAST_ROWS // self.pieces
        self.half_rows = 4 * (self.nf + self.nm)
        self.sum_rows = 2 * self.half_rows + 4 * self.nl
        self.ag_rows = -(-(2 * (self.nf + self.nm) + self.nl + 1) // 8) * 8
        self.keep_first = self.blocks * self.t1 * self.s1 * 2 <= 8 * MIB


def prep_body(z, pos, *refs):
    ids, f0, f1, wmsg, rows = refs[12:17]
    nf, cf, nm, cm, nl, cl, labels, feats, wf, wm, wl, bh = refs[17:29]
    fetch(refs[:12], refs[17:29], refs[29])

    def put(mb, at, value):
        for j in range(value.shape[1] // LANES):
            rows[mb, at + j : at + j + 1, :] = value[:, j * LANES : (j + 1) * LANES]

    for mb in range(2):
        for fan, nb, cnt, at, at_c in (
            (z.f1, nf, cf, z.at_first, z.at_c1),
            (z.f2, nm, cm, z.at_mid, z.at_c2),
            (z.f3, nl, cl, z.at_last, z.at_c3),
        ):
            count = cnt[mb : mb + 1, :]
            lanes = count.shape[1] // LANES
            for k in range(fan):
                put(mb, at + k * lanes, jnp.where(count > k, nb[k, mb : mb + 1, :], -1))
            put(mb, at_c, count)
        for other in range(2):
            put(mb, z.at_label + other * z.l3, labels[other : other + 1, :])
        end = z.at_c3 + z.l3
        if end < z.id_rows:
            rows[mb, end:, :] = jnp.zeros((z.id_rows - end, LANES), I32)
    part = pl.ds(pl.multiple_of((2 * pos[2] + pos[3]) * z.id_part, 8), z.id_part)
    for mb in range(2):
        mine = rows[mb, part]
        for s in range(4):
            for lead in range(z.rl):
                ids[(2 * s + mb) * z.rl + lead] = mine
    y = pos[2]
    f0[...] = feats[y]
    f1[...] = feats[1 - y]
    for j in range(2):
        wmsg[32 * j : 32 * j + 32, :] = wf[j]
        wmsg[64 + 64 * j : 128 + 64 * j, :] = wm[j]
    wmsg[192:248, :] = jnp.zeros((56, 256), F32)
    for j in range(2):
        wmsg[192 : 192 + 47, 64 * j : 64 * j + 64] = wl[:, j, :]
        wmsg[240:241, 64 * j : 64 * j + 64] = bh[j : j + 1, :]


def weights_body(pos, own, acr, dia, cor, blast, after, w1h, w1l, w2h, w2l, wmh, wml, wlt, wlc, bias, wall, f32a, f32b):
    s = 2 * pos[2] + pos[3]
    for at, part in ((s, own), (s ^ 2, acr), (s ^ 3, dia), (s ^ 1, cor)):
        wall[at] = part[...]
    for s in range(4):
        for j in range(2):
            f32a[128 * j + 32 * s : 128 * j + 32 * s + 32, :] = wall[s, 32 * j : 32 * j + 32, :]
            f32b[256 * j + 64 * s : 256 * j + 64 * s + 64, :] = wall[s, 64 + 64 * j : 128 + 64 * j, :]
            wlt[j, :, 64 * s : 64 * s + 64] = wall[s, 192 : 192 + CLASS_ROWS, 64 * j : 64 * j + 64]
    w1h[...], w1l[...] = halves(f32a[...].T)
    w2h[...], w2l[...] = halves(f32b[...].T)
    for j in range(2):
        wmh[j], wml[j] = halves(f32b[256 * j : 256 * j + 256, :])
        wlc[j] = jnp.concatenate([wlt[j], jnp.zeros((128 - CLASS_ROWS, 256), F32)], axis=0).T
    rows = [jnp.concatenate([wall[s, 240:241, 64 * j : 64 * j + 64] for s in range(4)], axis=1) for j in range(2)]
    last = jnp.concatenate([blast[...], jnp.zeros((1, 256 - 47), F32)], axis=1)
    packed = jnp.concatenate(rows + [last, jnp.zeros((125, 256), F32)], axis=0)
    bias[...] = packed.T


PIECE = 256


def all_rows(z, ids, row, zs):
    first = (row // z.id_part * 2 + zs) * z.rl
    return ids[first : first + z.rl, row % z.id_part, :]


def distinct(z, ids, at, fan, lanes, size, base, local, times):
    for zs in range(2):
        for j in range(lanes):
            rows = [all_rows(z, ids, at + k * lanes + j, zs) for k in range(fan)]
            count = [jnp.ones(rows[0].shape, F32) for _ in range(fan)]
            seen = [None] * fan
            for a in range(fan):
                for b in range(a + 1, fan):
                    same = rows[a] == rows[b]
                    count[a] = count[a] + jnp.where(same, 1.0, 0.0)
                    seen[b] = same if seen[b] is None else jnp.logical_or(seen[b], same)
            for k in range(fan):
                times[zs * lanes + j, k] = count[k]
                rel = rows[k] - base
                for g in range(size // PIECE):
                    inside = jnp.logical_and(rel >= g * PIECE, rel < (g + 1) * PIECE)
                    if seen[k] is not None:
                        inside = jnp.logical_and(inside, jnp.logical_not(seen[k]))
                    local[zs * lanes + j, g * fan + k] = jnp.where(inside, rel - g * PIECE, -1).astype(F32)


def adjacency_block(z, zs, lead, fan, lanes, size, local, times, at, out, column):
    for j in range(lanes):
        row = pl.ds(lead, 1)
        many = [jnp.broadcast_to(times[zs * lanes + j, k, row], (PIECE, LANES)).astype(BF16) for k in range(fan)]
        for g in range(size // PIECE):
            total = jnp.zeros((PIECE, LANES), BF16)
            for k in range(fan):
                name = jnp.broadcast_to(local[zs * lanes + j, g * fan + k, row], (PIECE, LANES)).astype(BF16)
                total = jnp.where(at == name, many[k], total)
            out[g * PIECE : (g + 1) * PIECE, column(j)] = total


def numbers():
    return lax.broadcasted_iota(I32, (PIECE, LANES), 0).astype(F32).astype(BF16)


def tables(z, fan, lanes, size):
    return [
        pltpu.VMEM((2 * lanes, size // PIECE * fan, z.rl, LANES), F32),
        pltpu.VMEM((2 * lanes, fan, z.rl, LANES), F32),
    ]


def adjacency_all(z, ids, first, fan, lanes, size, base, local, times, out):
    distinct(z, ids, first, fan, lanes, size, base, local, times)
    at = numbers()
    for zs in range(2):

        def block(lead, carry):
            def column(j):
                return pl.ds(pl.multiple_of(((zs * z.rl + lead) * lanes + j) * LANES, LANES), LANES)

            adjacency_block(z, zs, lead, fan, lanes, size, local, times, at, out, column)
            return carry

        lax.fori_loop(0, z.rl, block, 0)


def adjacency_first_body(z, pos, ids, a1, local, times):
    me = pos[2] * z.rl + pos[1]
    adjacency_all(z, ids, z.at_first, z.f1, z.l1, z.s1, me * z.s1, local, times, a1)


def class_weights(z, ids):
    classes = lax.broadcasted_iota(I32, (CLASS_ROWS, LANES), 0)
    total = jnp.zeros((CLASS_ROWS, LANES), F32)
    for zs in range(2):
        for other in range(2 * z.l3):
            rows = all_rows(z, ids, z.at_label + other, zs)
            for lead in range(z.rl):
                total = total + jnp.where(classes == rows[lead : lead + 1], 1.0, 0.0)
    counts = jnp.sum(total, axis=1, keepdims=True)
    weight = 1.0 / jnp.maximum(counts, 1.0)
    return weight, jnp.sum(counts * weight, axis=0, keepdims=True)


def adjacency_body(z, pos, ids, a2, a3, small, local2, times2, local3, times3):
    me = pos[2] * z.rl + pos[1]
    for q in range(4):
        small[q * z.id_part : (q + 1) * z.id_part] = ids[2 * q * z.rl + me].astype(F32)
    adjacency_all(z, ids, z.at_mid, z.f2, z.l2, z.t1, me * z.t1, local2, times2, a2)
    adjacency_all(z, ids, z.at_last, z.f3, z.l3, z.t2, me * z.t2, local3, times3, a3)
    weight, total = class_weights(z, ids)
    n = z.id_rows
    small[n : n + CLASS_ROWS] = jnp.broadcast_to(weight, (CLASS_ROWS, LANES))
    small[n + CLASS_ROWS :] = jnp.broadcast_to(total, (8, LANES))


def columns(pos, got0, got1, lanes):
    swap = pos[0] == 1
    a, b = got0[:, :lanes], got1[:, :lanes]
    return jnp.where(swap, b, a), jnp.where(swap, a, b)


def first_table(z, pos, got0, got1, table):
    width = 2 * got0.shape[0]
    rows = jnp.concatenate(columns(pos, got0, got1, z.s1), axis=0)
    table[:width], table[width:] = halves(rows)


def first_kept_body(z, pos, a1, got0, got1, after, out, table):
    first_table(z, pos, got0, got1, table)
    for r in range(z.blocks):
        both = dot(table[...], a1[:, r * z.t1 : (r + 1) * z.t1], NN)
        out[r] = both[: both.shape[0] // 2] + both[both.shape[0] // 2 :]


def first_body(z, pos, ids, got0, got1, after, out, table, adj, local, times):
    me = pos[2] * z.rl + pos[1]
    first_table(z, pos, got0, got1, table)
    width = 2 * got0.shape[0]
    at = numbers()
    distinct(z, ids, z.at_first, z.f1, z.l1, z.s1, me * z.s1, local, times)
    for zs in range(2):

        def block(lead, carry):
            def column(j):
                return slice(j * LANES, (j + 1) * LANES)

            adjacency_block(z, zs, lead, z.f1, z.l1, z.s1, local, times, at, adj, column)
            both = dot(table[...], adj[...], NN)
            out[zs * z.rl + lead] = both[:width] + both[width:]
            return carry

        lax.fori_loop(0, z.rl, block, 0)


def inverse(z, mine, at, lanes):
    row = jnp.concatenate([mine[at + j : at + j + 1, :] for j in range(lanes)], axis=1)
    return 1.0 / row


def sum_first_body(z, pos, mine, part, got0, got1, out):
    half = got0.shape[0]
    out[:half], out[half : 2 * half] = columns(pos, got0, got1, z.t1)
    total = part[0]
    for r in range(1, 2 * z.rl):
        total = total + part[r]
    out[2 * half :] = total * inverse(z, mine, z.at_c1, z.l1)


def put_columns(pos, own, other, out):
    c = pos[3]
    for j in range(2):
        for y in range(2):
            at = 128 * j + 64 * y
            out[pl.ds(pl.multiple_of(at + 32 * c, 32), 32)] = own[64 * j + 32 * y : 64 * j + 32 * y + 32]
            out[pl.ds(pl.multiple_of(at + 32 * (1 - c), 32), 32)] = other[64 * j + 32 * y : 64 * j + 32 * y + 32]


def hidden_one_body(z, pos, own, other, w1h, w1l, bias, a2, out, x1, h1, slope):
    c = pos[3]
    put_columns(pos, own, other, x1)
    pre = dot_split((w1h[...], w1l[...]), halves(x1[...]), NN) + bias[:, 0:1]
    sigma = sigmoid(pre)
    h1[...] = pre * sigma
    slope[...] = sigma * (1.0 + pre * (1.0 - sigma))
    table = jnp.concatenate(halves(h1[pl.ds(pl.multiple_of(c * 128, 128), 128)]), axis=0)
    for r in range(2 * z.rl):
        both = dot(table, a2[:, r * z.t2 : (r + 1) * z.t2], NN)
        out[r] = both[:128] + both[128:]


def sum_mid_body(z, pos, mine, part, out):
    total = part[0]
    for r in range(1, 2 * z.rl):
        total = total + part[r]
    out[...] = total * inverse(z, mine, z.at_c2, z.l2)


def hidden_two_body(z, pos, own, other, h1, w2h, w2l, bias, wlt, a3, out, y2, h2, slope, local):
    c = pos[3]
    y2[:256] = h1[:, : z.t2]
    y2[pl.ds(pl.multiple_of(256 + c * 128, 128), 128)] = own[...]
    y2[pl.ds(pl.multiple_of(256 + (1 - c) * 128, 128), 128)] = other[...]
    pre = dot_split((w2h[...], w2l[...]), halves(y2[...]), NN) + bias[:, 1:2]
    sigma = sigmoid(pre)
    hidden = pre * sigma
    h2[...] = hidden
    slope[...] = sigma * (1.0 + pre * (1.0 - sigma))
    split = halves(hidden)
    local[...] = dot_split(halves(wlt[0]), (split[0][:, : z.t3], split[1][:, : z.t3]), NN)
    for_mean = dot_split(halves(wlt[1]), split, NN)
    table = jnp.concatenate(halves(for_mean), axis=0)
    for r in range(z.blocks):
        both = dot(table, a3[:, r * z.t3 : (r + 1) * z.t3], NN)
        out[r] = both[:CLASS_ROWS] + both[CLASS_ROWS:]


def logits_body(z, pos, mine, part, local, bias, out, grad, loss):
    total = part[0]
    for r in range(1, 2 * z.rl):
        total = total + part[r]
    recip = inverse(z, mine, z.at_c3, z.l3)
    logits = total * recip + local[...] + bias[:CLASS_ROWS, 2:3]
    classes = lax.broadcasted_iota(I32, logits.shape, 0)
    logits = jnp.where(classes < 47, logits, -jnp.inf)
    label = jnp.where(
        pos[0] == 0,
        mine[z.at_label : z.at_label + 1, :],
        mine[z.at_label + z.l3 : z.at_label + z.l3 + 1, :],
    ).astype(I32)
    onehot = jnp.where(classes == label, 1.0, 0.0)
    top = jnp.max(logits, axis=0, keepdims=True)
    powers = jnp.exp(logits - top)
    norm = jnp.sum(powers, axis=0, keepdims=True)
    weight = jnp.sum(onehot * mine[z.id_rows : z.id_rows + CLASS_ROWS], axis=0, keepdims=True)
    target = jnp.sum(jnp.where(classes == label, logits, 0.0), axis=0, keepdims=True)
    each = weight * (jnp.log(norm) + top - target)
    loss[...] = jnp.broadcast_to(jnp.sum(each, axis=1, keepdims=True), loss.shape)
    dlogits = weight * (powers / norm - onehot) / mine[z.id_rows + CLASS_ROWS : z.id_rows + CLASS_ROWS + 1, :]
    grad[...] = dlogits
    scaled = dlogits * recip
    for r in range(2 * z.rl):
        out[r] = scaled


def back_last_body(z, pos, mine, gall, grad, a3, wlc, h2, slope, out, dpre2, dwl):
    both = None
    for r in range(2 * z.rl):
        table = jnp.concatenate(halves(gall[r]), axis=0)
        term = dot(table, a3[:, r * z.t3 : (r + 1) * z.t3], NT)
        both = term if both is None else both + term
    back_last(z, pos, mine, both[:CLASS_ROWS] + both[CLASS_ROWS:], grad, wlc, h2, slope, out, dpre2, dwl)


def back_last(z, pos, mine, spread, grad, wlc, h2, slope, out, dpre2, dwl):
    c = pos[3]
    dh = dot_full(wlc[1][:, :CLASS_ROWS], spread, NN)
    own = dot_full(wlc[0][:, :CLASS_ROWS], grad[...], NN)
    dh = dh + jnp.concatenate([own, jnp.zeros((256, z.t2 - z.t3), F32)], axis=1)
    dpre2[...] = dh * slope[...]
    scaled = dpre2[pl.ds(pl.multiple_of(c * 128, 128), 128)] * inverse(z, mine, z.at_c2, z.l2)
    for r in range(2 * z.rl):
        out[r] = scaled
    dwl[0] = dot_full(grad[...], h2[:, : z.t3], NT)
    dwl[1] = dot_full(spread, h2[...], NT)


def back_mid_body(z, pos, gall, a2, out):
    both = None
    for r in range(2 * z.rl):
        table = jnp.concatenate(halves(gall[r]), axis=0)
        term = dot(table, a2[:, r * z.t2 : (r + 1) * z.t2], NT)
        both = term if both is None else both + term
    out[...] = both[:128] + both[128:]


def row_sums(value):
    ones = jnp.ones((8, value.shape[1]), BF16)
    high, low = halves(value)
    return dot(ones, high, NT) + dot(ones, low, NT)


def grads_body(z, pos, own, other, dpre2, wmh, wml, slope, x1, y2, dwl, grad, loss, out, spread, first, mid, last):
    c = pos[3]
    mine = pl.ds(pl.multiple_of(c * 128, 128), 128)
    spread[mine] = own[...]
    spread[pl.ds(pl.multiple_of((1 - c) * 128, 128), 128)] = other[...]
    dh = dot_split((wmh[1, mine, :], wml[1, mine, :]), halves(spread[...]), NN)
    at_own = dot_split((wmh[0, mine, :], wml[0, mine, :]), halves(dpre2[...]), NN)
    dh = dh + jnp.concatenate([at_own, jnp.zeros((128, z.t1 - z.t2), F32)], axis=1)
    dpre1 = dh * slope[mine]
    half2 = dpre2[mine]
    first[...] = dot_full(x1[...], dpre1, NT)
    mid[...] = dot_full(y2[...], half2, NT)
    b1, b2, b3 = row_sums(dpre1), row_sums(half2), row_sums(grad[...])
    last[...] = jnp.zeros_like(last)
    core0 = jnp.where(c == 0, 1.0, 0.0)
    for s in range(4):
        last[s, :CLASS_ROWS, :64] = dwl[0][:, 64 * s : 64 * s + 64] * core0
        last[s, :CLASS_ROWS, 64:] = dwl[1][:, 64 * s : 64 * s + 64] * (1.0 - core0)
        here = jnp.where(c == s // 2, 1.0, 0.0)
        at = 64 * (s % 2)
        last[s, ROW_HIDDEN : ROW_HIDDEN + 1, :64] = b1[0:1, at : at + 64] * here
        last[s, ROW_HIDDEN : ROW_HIDDEN + 1, 64:] = b2[0:1, at : at + 64] * here
        last[s, ROW_LAST : ROW_LAST + 1, :LANE_LOSS] = b3[0:1, :LANE_LOSS] * core0
        last[s, ROW_LAST : ROW_LAST + 1, LANE_LOSS : LANE_LOSS + 1] = loss[0:1, 0:1] * core0
    n = 4 * (z.nf + z.nm)
    for p in range(z.pieces):
        for s in range(4):
            e = z.nf * p
            at = 128 * (e // 32) + 32 * s + e % 32
            out[p, s * z.nf : (s + 1) * z.nf] = first[at : at + z.nf]
            e = z.nm * p
            at = 256 * (e // 64) + 64 * s + e % 64
            out[p, 4 * z.nf + s * z.nm : 4 * z.nf + (s + 1) * z.nm] = mid[at : at + z.nm]
            out[p, n + s * z.nl : n + (s + 1) * z.nl] = last[s, z.nl * p : z.nl * (p + 1)]


def sum_grads_body(z, pos, part, out):
    n = z.half_rows
    even, odd = part[0], part[1]
    for d in range(2, z.pieces, 2):
        even = even + part[d]
        odd = odd + part[d + 1]
    out[:n] = even[:n]
    out[n : 2 * n] = odd[:n]
    out[2 * n :] = even[n:] + odd[n:]


def share_body(z, pos, own, other, out):
    n, nf, nm, nl = z.half_rows, z.nf, z.nm, z.nl
    total = own[...] + other[...]
    piece = 4 * pos[1] + 2 * pos[2] + pos[3]
    lane = lax.broadcasted_iota(I32, (1, LANES), 1)
    squares = jnp.sum(total[: 2 * n] * total[: 2 * n], axis=0, keepdims=True)
    for s in range(4):
        for i in range(nl):
            row = total[2 * n + s * nl + i : 2 * n + s * nl + i + 1]
            at = piece * nl + i
            squares = squares + jnp.where(at <= ROW_HIDDEN, 1.0, 0.0) * row * row
            if s == 0:
                squares = squares + jnp.where(at == ROW_LAST, 1.0, 0.0) * jnp.where(lane < 47, row * row, 0.0)
    squares = jnp.broadcast_to(jnp.sum(squares, axis=1, keepdims=True), (1, LANES))
    pad = z.ag_rows - 2 * (nf + nm) - nl - 1
    for s in range(4):
        rows = []
        for h in range(2):
            rows.append(total[h * n + s * nf : h * n + (s + 1) * nf])
            rows.append(total[h * n + 4 * nf + s * nm : h * n + 4 * nf + (s + 1) * nm])
        rows += [total[2 * n + s * nl : 2 * n + (s + 1) * nl], squares]
        if pad:
            rows.append(jnp.zeros((pad, LANES), F32))
        rows = jnp.concatenate(rows, axis=0)
        for lead in range(z.rl):
            out[4 * lead + s] = rows


def update_body(z, pos, whole, mine, *refs):
    w, m, v = refs[0:5], refs[5:10], refs[10:15]
    new, moment, square = refs[15:20], refs[20:25], refs[25:30]
    loss, weight_sum, norm = refs[30:33]
    nf, nm, nl = z.nf, z.nm, z.nl
    at = 2 * (nf + nm) + nl
    total = whole[0, at : at + 1, 0:1]
    for p in range(1, z.pieces):
        total = total + whole[p, at : at + 1, 0:1]
    root = jnp.sqrt(total)
    scale = jnp.minimum(1.0, 0.01 / root)
    norm[...] = root
    weight_sum[...] = mine[z.id_rows + CLASS_ROWS : z.id_rows + CLASS_ROWS + 1, 0:1]

    def adamw(weight, grad, first, second):
        grad = grad * scale
        mo = 0.9 * first + 0.1 * grad
        sq = 0.999 * second + 0.001 * grad * grad
        corrected = mo / (1.0 - 0.9**STEP)
        rt = jnp.sqrt(sq / (1.0 - 0.999**STEP))
        return (weight - 0.05 * (corrected / (rt + 1e-08) + 0.01 * weight), mo, sq)

    def put(i, at, grad):
        outs = adamw(w[i][at], grad, m[i][at], v[i][at])
        new[i][at], moment[i][at], square[i][at] = outs

    h = nf + nm
    for p in range(z.pieces):
        e = nf * p
        g = jnp.concatenate([whole[p, :nf], whole[p, h : h + nf]], axis=1)
        put(0, (e // 32, slice(e % 32, e % 32 + nf), slice(None)), g)
        e = nm * p
        g = jnp.concatenate([whole[p, nf:h], whole[p, h + nf : 2 * h]], axis=1)
        put(1, (e // 64, slice(e % 64, e % 64 + nm), slice(None)), g)
        a = nl * p
        b = min(a + nl, 47)
        if a < b:
            for j in range(2):
                put(2, (slice(a, b), j, slice(None)), whole[p, 2 * h : 2 * h + b - a, 64 * j : 64 * j + 64])
        for i in range(nl):
            row = whole[p, 2 * h + i : 2 * h + i + 1]
            if a + i == ROW_HIDDEN:
                for j in range(2):
                    put(3, (slice(j, j + 1), slice(None)), row[:, 64 * j : 64 * j + 64])
            elif a + i == ROW_LAST:
                put(4, (slice(None), slice(None)), row[:, :47])
                loss[...] = row[:, LANE_LOSS : LANE_LOSS + 1]


def on_device(
    mesh, features, neigh_first, count_first, neigh_mid, count_mid, neigh_last, count_last, labels,
    w_first, w_mid, w_last, b_hidden, b_last,
    m_first, m_mid, m_last, m_hidden, m_bias,
    v_first, v_mid, v_last, v_hidden, v_bias,
):
    z = Sizes(mesh, features, neigh_first, neigh_mid, neigh_last)
    bind = functools.partial
    blocks = z.blocks

    def flip(value):
        return lax.ppermute(value, "c", [(0, 1), (1, 0)])

    def exchange(value):
        return lax.all_to_all(value, ("y", "rl"), 0, 0)

    def swapped(value):
        return jnp.transpose(value, (2, 0, 1))

    raw = (
        swapped(neigh_first), count_first, swapped(neigh_mid), count_mid, swapped(neigh_last), count_last, labels,
        jnp.transpose(features, (0, 2, 1)), w_first, w_mid, swapped(w_last), b_hidden,
    )
    ids, f0, f1, wmsg = call(
        bind(prep_body, z),
        [((4 * z.ranks, z.id_part, LANES), I32), ((32, z.s1), F32), ((32, z.s1), F32), ((248, 256), F32)],
        "prep", 58, scratch=[pltpu.VMEM((2, z.id_rows, LANES), I32), *like(*raw)], where=HBM, us=2.0,
    )(*raw)
    got0, got1 = (
        lax.ppermute(f, ("zh", "y"), [(2 * zh + y, 2 * (y ^ j) + zh) for zh in range(2) for y in range(2)])
        for j, f in enumerate((f0, f1))
    )
    across = lax.ppermute(wmsg, "y", [(0, 1), (1, 0)])
    walls = (wmsg, across, flip(across), flip(wmsg))
    ids = lax.all_to_all(ids, ("y", "c", "zh", "rl"), 0, 0)
    a2, a3, mine = call(
        bind(adjacency_body, z),
        [
            ((z.t1, blocks * z.t2), BF16), ((z.t2, blocks * z.t3), BF16),
            ((z.id_rows + CLASS_ROWS + 8, LANES), F32),
        ],
        "adjacency", 8, us=4.0, scratch=tables(z, z.f2, z.l2, z.t1) + tables(z, z.f3, z.l3, z.t2),
    )(ids)
    w1h, w1l, w2h, w2l, wmh, wml, wlt, wlc, bias = call(
        weights_body,
        [
            ((256, 256), BF16), ((256, 256), BF16), ((256, 512), BF16), ((256, 512), BF16),
            ((2, 256, 256), BF16), ((2, 256, 256), BF16),
            ((2, CLASS_ROWS, 256), F32), ((2, 256, 128), F32), ((256, 128), F32),
        ],
        "weights", 8,
        scratch=[pltpu.VMEM((4, 248, 256), F32), pltpu.VMEM((256, 256), F32), pltpu.VMEM((512, 256), F32)],
    )(*walls, b_last[None], mine)
    table = pltpu.VMEM((128, z.s1), BF16)
    sums = [((blocks, 64, z.t1), F32)]
    if z.keep_first:
        a1 = call(
            bind(adjacency_first_body, z), [((z.s1, blocks * z.t1), BF16)], "adjacency_first", 4, us=6.0,
            scratch=tables(z, z.f1, z.l1, z.s1),
        )(ids)[0]
        part = call(bind(first_kept_body, z), sums, "first", 4, us=3.0, scratch=[table])(a1, got0, got1, bias)[0]
    else:
        part = call(
            bind(first_body, z), sums, "first", 16, us=8.0,
            scratch=[table, pltpu.VMEM((z.s1, z.t1), BF16), *tables(z, z.f1, z.l1, z.s1)],
        )(ids, got0, got1, bias)[0]
    part = exchange(part)
    half = call(bind(sum_first_body, z), [((128, z.t1), F32)], "sum_first", 8)(mine, part, got0, got1)[0]
    other = flip(half)
    part, x1, h1, slope1 = call(
        bind(hidden_one_body, z),
        [((blocks, 128, z.t2), F32), ((256, z.t1), F32), ((256, z.t1), F32), ((256, z.t1), F32)],
        "hidden_one", 16,
    )(half, other, w1h, w1l, bias, a2)
    part = exchange(part)
    half = call(bind(sum_mid_body, z), [((128, z.t2), F32)], "sum_mid", 8)(mine, part)[0]
    other = flip(half)
    part, y2, h2, slope2, local = call(
        bind(hidden_two_body, z),
        [
            ((blocks, CLASS_ROWS, z.t3), F32),
            ((512, z.t2), F32), ((256, z.t2), F32), ((256, z.t2), F32), ((CLASS_ROWS, z.t3), F32),
        ],
        "hidden_two", 12,
    )(half, other, h1, w2h, w2l, bias, wlt, a3)
    part = exchange(part)
    backs = [((blocks, 128, z.t2), F32), ((256, z.t2), F32), ((2, CLASS_ROWS, 256), F32)]
    ends = [((CLASS_ROWS, z.t3), F32), ((8, LANES), F32)]
    part, grad, loss = call(bind(logits_body, z), [((blocks, CLASS_ROWS, z.t3), F32), *ends], "logits", 8)(
        mine, part, local, bias
    )
    part = exchange(part)
    part, dpre2, dwl = call(bind(back_last_body, z), backs, "back_last", 12, us=1.5)(
        mine, part, grad, a3, wlc, h2, slope2
    )
    part = exchange(part)
    half = call(bind(back_mid_body, z), [((128, z.t1), F32)], "back_mid", 12)(part, a2)[0]
    other = flip(half)
    part = call(
        bind(grads_body, z), [((z.pieces, 4 * (z.nf + z.nm + z.nl), LANES), F32)], "grads", 12,
        scratch=[
            pltpu.VMEM((256, z.t1), F32), pltpu.VMEM((256, 128), F32), pltpu.VMEM((512, 128), F32),
            pltpu.VMEM((4, LAST_ROWS, LANES), F32),
        ],
    )(half, other, dpre2, wmh, wml, slope1, x1, y2, dwl, grad, loss)[0]
    part = lax.all_to_all(part, ("rl", "y", "c"), 0, 0)
    own = call(bind(sum_grads_body, z), [((z.sum_rows, LANES), F32)], "sum_grads", 8)(part)[0]
    other = lax.ppermute(own, "zh", [(0, 1), (1, 0)])
    part = call(bind(share_body, z), [((z.pieces, z.ag_rows, LANES), F32)], "share", 8)(own, other)[0]
    whole = lax.all_to_all(part, ("rl", "y", "c"), 0, 0)

    params = (w_first, w_mid, swapped(w_last), b_hidden, b_last[None])
    firsts = (m_first, m_mid, swapped(m_last), m_hidden, m_bias[None])
    seconds = (v_first, v_mid, swapped(v_last), v_hidden, v_bias[None])
    shapes = [(p.shape, F32) for p in params]
    state = (*params, *firsts, *seconds)
    outs = call(
        bind(update_body, z), shapes * 3 + [((1, 1), F32)] * 3, "update", 8
    )(whole, mine, *state)
    results = []
    for g in range(3):
        a, b, c, d, e = outs[5 * g : 5 * g + 5]
        results += [a, b, jnp.transpose(c, (1, 2, 0)), d, e[0]]
    return tuple(results) + tuple(o[0, 0] for o in outs[15:])


def solution(mesh):
    rows, cols = mesh.shape["rows"], mesh.shape["cols"]
    fine = Mesh(mesh.devices.reshape(2, rows // 2, 2, cols // 2), ("zh", "rl", "y", "c"))
    r, c = ("zh", "rl"), ("y", "c")
    weights = (P(None, c, None),) * 3 + (P(None, c), P())
    nodes = (P(None, r, None), P(None, r))
    placed = (P(None, r, c),) + nodes * 3 + (P(None, r),) + weights * 3
    return jax.shard_map(
        functools.partial(on_device, fine),
        mesh=fine,
        in_specs=placed,
        out_specs=weights * 3 + (P(), P(), P()),
        check_vma=False,
    )
```

```python
import functools

import jax
import jax.numpy as jnp
from jax import lax
from jax.experimental import pallas as pl
from jax.experimental.pallas import tpu as pltpu
from jax.sharding import Mesh
from jax.sharding import PartitionSpec as P

STEP = 5
F32 = jnp.float32
BF16 = jnp.bfloat16
I32 = jnp.int32
LANES = 128
CLASS_ROWS = 48
LAST_ROWS = 64
ROW_HIDDEN = 48
ROW_LAST = 49
LANE_LOSS = 47
MIB = 1 << 20


def dims(left, right):
    return (((left,), (right,)), ((), ()))


NN, NT = dims(1, 0), dims(1, 1)


def dot(left, right, form):
    return lax.dot_general(left, right, form, preferred_element_type=F32)


def halves(value):
    high = value.astype(BF16)
    return high, (value - high.astype(F32)).astype(BF16)


def dot_split(left, right, form):
    (lh, ll), (rh, rl) = left, right
    return dot(lh, rh, form) + dot(lh, rl, form) + dot(ll, rh, form)


def dot_full(left, right, form):
    return dot_split(halves(left), halves(right), form)


def sigmoid(value):
    return 1.0 / (1.0 + jnp.exp(-value))


VMEM = pl.BlockSpec(memory_space=pltpu.VMEM)
HBM = pl.BlockSpec(memory_space=pltpu.HBM)


AXES = ("zh", "rl", "y", "c")


def call(body, outs, name, vmem, scratch=(), where=VMEM, us=1.0):
    def placed(*refs):
        body([lax.axis_index(a) for a in AXES], *refs)

    def run(*args):
        return pl.pallas_call(
            placed,
            out_shape=[jax.ShapeDtypeStruct(s, d) for s, d in outs],
            in_specs=[where] * len(args),
            out_specs=[VMEM] * len(outs),
            scratch_shapes=list(scratch),
            name=name,
            compiler_params=pltpu.CompilerParams(vmem_limit_bytes=vmem * MIB),
            cost_estimate=pl.CostEstimate(flops=0, bytes_accessed=int(us * 3.6e6), transcendentals=0),
        )(*args)

    return run


def fetch(sources, targets, sems):
    copies = [pltpu.make_async_copy(s, t, sems.at[i]) for i, (s, t) in enumerate(zip(sources, targets))]
    for copy in copies:
        copy.start()
    for copy in copies:
        copy.wait()


def like(*arrays):
    return [pltpu.VMEM(a.shape, a.dtype) for a in arrays] + [pltpu.SemaphoreType.DMA((len(arrays),))]


class Sizes:
    def __init__(self, mesh, features, neigh_first, neigh_mid, neigh_last):
        self.ranks = mesh.shape["zh"] * mesh.shape["rl"]
        self.rl = mesh.shape["rl"]
        self.s1, self.t1 = features.shape[1], neigh_first.shape[1]
        self.t2, self.t3 = neigh_mid.shape[1], neigh_last.shape[1]
        self.f1, self.f2, self.f3 = neigh_first.shape[2], neigh_mid.shape[2], neigh_last.shape[2]
        l1, l2, l3 = self.t1 // LANES, self.t2 // LANES, self.t3 // LANES
        self.l1, self.l2, self.l3 = l1, l2, l3
        self.at_first = 0
        self.at_mid = self.at_first + self.f1 * l1
        self.at_last = self.at_mid + self.f2 * l2
        self.at_label = self.at_last + self.f3 * l3
        self.at_c1 = self.at_label + 2 * l3
        self.at_c2 = self.at_c1 + l1
        self.at_c3 = self.at_c2 + l2
        self.id_rows = -(-(self.at_c3 + l3) // 32) * 32
        self.id_part = self.id_rows // 4
        self.blocks = 2 * self.rl
        self.pieces = 4 * self.rl
        self.nf, self.nm, self.nl = 64 // self.pieces, 128 // self.pieces, LAST_ROWS // self.pieces
        self.half_rows = 4 * (self.nf + self.nm)
        self.sum_rows = 2 * self.half_rows + 4 * self.nl
        self.ag_rows = -(-(2 * (self.nf + self.nm) + self.nl + 1) // 8) * 8
        self.keep_first = self.blocks * self.t1 * self.s1 * 2 <= 8 * MIB


def prep_body(z, pos, *refs):
    ids, f0, f1, wmsg, rows = refs[12:17]
    nf, cf, nm, cm, nl, cl, labels, feats, wf, wm, wl, bh = refs[17:29]
    fetch(refs[:12], refs[17:29], refs[29])

    def put(mb, at, value):
        for j in range(value.shape[1] // LANES):
            rows[mb, at + j : at + j + 1, :] = value[:, j * LANES : (j + 1) * LANES]

    for mb in range(2):
        for fan, nb, cnt, at, at_c in (
            (z.f1, nf, cf, z.at_first, z.at_c1),
            (z.f2, nm, cm, z.at_mid, z.at_c2),
            (z.f3, nl, cl, z.at_last, z.at_c3),
        ):
            count = cnt[mb : mb + 1, :]
            lanes = count.shape[1] // LANES
            for k in range(fan):
                put(mb, at + k * lanes, jnp.where(count > k, nb[k, mb : mb + 1, :], -1))
            put(mb, at_c, count)
        for other in range(2):
            put(mb, z.at_label + other * z.l3, labels[other : other + 1, :])
        end = z.at_c3 + z.l3
        if end < z.id_rows:
            rows[mb, end:, :] = jnp.zeros((z.id_rows - end, LANES), I32)
    part = pl.ds(pl.multiple_of((2 * pos[2] + pos[3]) * z.id_part, 8), z.id_part)
    for mb in range(2):
        mine = rows[mb, part]
        for s in range(4):
            for lead in range(z.rl):
                ids[(2 * s + mb) * z.rl + lead] = mine
    y = pos[2]
    f0[...] = feats[y]
    f1[...] = feats[1 - y]
    for j in range(2):
        wmsg[32 * j : 32 * j + 32, :] = wf[j]
        wmsg[64 + 64 * j : 128 + 64 * j, :] = wm[j]
    wmsg[192:248, :] = jnp.zeros((56, 256), F32)
    for j in range(2):
        wmsg[192 : 192 + 47, 64 * j : 64 * j + 64] = wl[:, j, :]
        wmsg[240:241, 64 * j : 64 * j + 64] = bh[j : j + 1, :]


def held_body(pos, value, after, out):
    out[...] = value[...]


def weights_body(pos, own, acr, dia, cor, blast, after, w1h, w1l, w2h, w2l, wmh, wml, wlt, wlc, bias, wall, f32a, f32b):
    s = 2 * pos[2] + pos[3]
    for at, part in ((s, own), (s ^ 2, acr), (s ^ 3, dia), (s ^ 1, cor)):
        wall[at] = part[...]
    for s in range(4):
        for j in range(2):
            f32a[128 * j + 32 * s : 128 * j + 32 * s + 32, :] = wall[s, 32 * j : 32 * j + 32, :]
            f32b[256 * j + 64 * s : 256 * j + 64 * s + 64, :] = wall[s, 64 + 64 * j : 128 + 64 * j, :]
            wlt[j, :, 64 * s : 64 * s + 64] = wall[s, 192 : 192 + CLASS_ROWS, 64 * j : 64 * j + 64]
    w1h[...], w1l[...] = halves(f32a[...].T)
    w2h[...], w2l[...] = halves(f32b[...].T)
    for j in range(2):
        wmh[j], wml[j] = halves(f32b[256 * j : 256 * j + 256, :])
        wlc[j] = jnp.concatenate([wlt[j], jnp.zeros((128 - CLASS_ROWS, 256), F32)], axis=0).T
    rows = [jnp.concatenate([wall[s, 240:241, 64 * j : 64 * j + 64] for s in range(4)], axis=1) for j in range(2)]
    last = jnp.concatenate([blast[...], jnp.zeros((1, 256 - 47), F32)], axis=1)
    packed = jnp.concatenate(rows + [last, jnp.zeros((125, 256), F32)], axis=0)
    bias[...] = packed.T


PIECE = 256


def all_rows(z, ids, row, zs):
    first = (row // z.id_part * 2 + zs) * z.rl
    return ids[first : first + z.rl, row % z.id_part, :]


def distinct(z, ids, at, fan, lanes, size, base, local, times):
    for zs in range(2):
        for j in range(lanes):
            rows = [all_rows(z, ids, at + k * lanes + j, zs) for k in range(fan)]
            count = [jnp.ones(rows[0].shape, F32) for _ in range(fan)]
            seen = [None] * fan
            for a in range(fan):
                for b in range(a + 1, fan):
                    same = rows[a] == rows[b]
                    count[a] = count[a] + jnp.where(same, 1.0, 0.0)
                    seen[b] = same if seen[b] is None else jnp.logical_or(seen[b], same)
            for k in range(fan):
                times[zs * lanes + j, k] = count[k]
                rel = rows[k] - base
                for g in range(size // PIECE):
                    inside = jnp.logical_and(rel >= g * PIECE, rel < (g + 1) * PIECE)
                    if seen[k] is not None:
                        inside = jnp.logical_and(inside, jnp.logical_not(seen[k]))
                    local[zs * lanes + j, g * fan + k] = jnp.where(inside, rel - g * PIECE, -1).astype(F32)


def adjacency_block(z, zs, lead, fan, lanes, size, local, times, at, out, column):
    for j in range(lanes):
        row = pl.ds(lead, 1)
        many = [jnp.broadcast_to(times[zs * lanes + j, k, row], (PIECE, LANES)).astype(BF16) for k in range(fan)]
        for g in range(size // PIECE):
            total = jnp.zeros((PIECE, LANES), BF16)
            for k in range(fan):
                name = jnp.broadcast_to(local[zs * lanes + j, g * fan + k, row], (PIECE, LANES)).astype(BF16)
                total = jnp.where(at == name, many[k], total)
            out[g * PIECE : (g + 1) * PIECE, column(j)] = total


def numbers():
    return lax.broadcasted_iota(I32, (PIECE, LANES), 0).astype(F32).astype(BF16)


def tables(z, fan, lanes, size):
    return [
        pltpu.VMEM((2 * lanes, size // PIECE * fan, z.rl, LANES), F32),
        pltpu.VMEM((2 * lanes, fan, z.rl, LANES), F32),
    ]


def adjacency_all(z, ids, first, fan, lanes, size, base, local, times, out):
    distinct(z, ids, first, fan, lanes, size, base, local, times)
    at = numbers()
    for zs in range(2):

        def block(lead, carry):
            def column(j):
                return pl.ds(pl.multiple_of(((zs * z.rl + lead) * lanes + j) * LANES, LANES), LANES)

            adjacency_block(z, zs, lead, fan, lanes, size, local, times, at, out, column)
            return carry

        lax.fori_loop(0, z.rl, block, 0)


def adjacency_first_body(z, pos, ids, after0, after1, a1, small, local, times):
    me = pos[2] * z.rl + pos[1]
    for q in range(4):
        small[q * z.id_part : (q + 1) * z.id_part] = ids[2 * q * z.rl + me].astype(F32)
    weight, total = class_weights(z, ids)
    n = z.id_rows
    small[n : n + CLASS_ROWS] = jnp.broadcast_to(weight, (CLASS_ROWS, LANES))
    small[n + CLASS_ROWS :] = jnp.broadcast_to(total, (8, LANES))
    if z.keep_first:
        adjacency_all(z, ids, z.at_first, z.f1, z.l1, z.s1, me * z.s1, local, times, a1)


def adjacency_mid_body(z, pos, ids, after, a2, local, times):
    me = pos[2] * z.rl + pos[1]
    adjacency_all(z, ids, z.at_mid, z.f2, z.l2, z.t1, me * z.t1, local, times, a2)


def adjacency_last_body(z, pos, ids, after, a3, local, times):
    me = pos[2] * z.rl + pos[1]
    adjacency_all(z, ids, z.at_last, z.f3, z.l3, z.t2, me * z.t2, local, times, a3)


def class_weights(z, ids):
    classes = lax.broadcasted_iota(I32, (CLASS_ROWS, LANES), 0)
    total = jnp.zeros((CLASS_ROWS, LANES), F32)
    for zs in range(2):
        for other in range(2 * z.l3):
            rows = all_rows(z, ids, z.at_label + other, zs)
            for lead in range(z.rl):
                total = total + jnp.where(classes == rows[lead : lead + 1], 1.0, 0.0)
    counts = jnp.sum(total, axis=1, keepdims=True)
    weight = 1.0 / jnp.maximum(counts, 1.0)
    return weight, jnp.sum(counts * weight, axis=0, keepdims=True)


def columns(pos, got0, got1, lanes):
    swap = pos[0] == 1
    a, b = got0[:, :lanes], got1[:, :lanes]
    return jnp.where(swap, b, a), jnp.where(swap, a, b)


def first_table(z, pos, got0, got1, table):
    width = 2 * got0.shape[0]
    rows = jnp.concatenate(columns(pos, got0, got1, z.s1), axis=0)
    table[:width], table[width:] = halves(rows)


def first_kept_body(z, pos, a1, got0, got1, after, out, table):
    first_table(z, pos, got0, got1, table)
    for r in range(z.blocks):
        both = dot(table[...], a1[:, r * z.t1 : (r + 1) * z.t1], NN)
        out[r] = both[: both.shape[0] // 2] + both[both.shape[0] // 2 :]


def first_body(z, pos, ids, got0, got1, after, out, table, adj, local, times):
    me = pos[2] * z.rl + pos[1]
    first_table(z, pos, got0, got1, table)
    width = 2 * got0.shape[0]
    at = numbers()
    distinct(z, ids, z.at_first, z.f1, z.l1, z.s1, me * z.s1, local, times)
    for zs in range(2):

        def block(lead, carry):
            def column(j):
                return slice(j * LANES, (j + 1) * LANES)

            adjacency_block(z, zs, lead, z.f1, z.l1, z.s1, local, times, at, adj, column)
            both = dot(table[...], adj[...], NN)
            out[zs * z.rl + lead] = both[:width] + both[width:]
            return carry

        lax.fori_loop(0, z.rl, block, 0)


def inverse(z, mine, at, lanes):
    row = jnp.concatenate([mine[at + j : at + j + 1, :] for j in range(lanes)], axis=1)
    return 1.0 / row


def sum_first_body(z, pos, mine, part, got0, got1, out):
    half = got0.shape[0]
    out[:half], out[half : 2 * half] = columns(pos, got0, got1, z.t1)
    total = part[0]
    for r in range(1, 2 * z.rl):
        total = total + part[r]
    out[2 * half :] = total * inverse(z, mine, z.at_c1, z.l1)


def put_columns(pos, own, other, out):
    c = pos[3]
    for j in range(2):
        for y in range(2):
            at = 128 * j + 64 * y
            out[pl.ds(pl.multiple_of(at + 32 * c, 32), 32)] = own[64 * j + 32 * y : 64 * j + 32 * y + 32]
            out[pl.ds(pl.multiple_of(at + 32 * (1 - c), 32), 32)] = other[64 * j + 32 * y : 64 * j + 32 * y + 32]


def hidden_one_body(z, pos, own, other, w1h, w1l, bias, a2, out, x1, h1, slope):
    c = pos[3]
    put_columns(pos, own, other, x1)
    pre = dot_split((w1h[...], w1l[...]), halves(x1[...]), NN) + bias[:, 0:1]
    sigma = sigmoid(pre)
    h1[...] = pre * sigma
    slope[...] = sigma * (1.0 + pre * (1.0 - sigma))
    table = jnp.concatenate(halves(h1[pl.ds(pl.multiple_of(c * 128, 128), 128)]), axis=0)
    for r in range(2 * z.rl):
        both = dot(table, a2[:, r * z.t2 : (r + 1) * z.t2], NN)
        out[r] = both[:128] + both[128:]


def sum_mid_body(z, pos, mine, part, out):
    total = part[0]
    for r in range(1, 2 * z.rl):
        total = total + part[r]
    out[...] = total * inverse(z, mine, z.at_c2, z.l2)


def hidden_two_body(z, pos, own, other, h1, w2h, w2l, bias, wlt, a3, out, y2, h2, slope, local):
    c = pos[3]
    y2[:256] = h1[:, : z.t2]
    y2[pl.ds(pl.multiple_of(256 + c * 128, 128), 128)] = own[...]
    y2[pl.ds(pl.multiple_of(256 + (1 - c) * 128, 128), 128)] = other[...]
    pre = dot_split((w2h[...], w2l[...]), halves(y2[...]), NN) + bias[:, 1:2]
    sigma = sigmoid(pre)
    hidden = pre * sigma
    h2[...] = hidden
    slope[...] = sigma * (1.0 + pre * (1.0 - sigma))
    split = halves(hidden)
    local[...] = dot_split(halves(wlt[0]), (split[0][:, : z.t3], split[1][:, : z.t3]), NN)
    for_mean = dot_split(halves(wlt[1]), split, NN)
    table = jnp.concatenate(halves(for_mean), axis=0)
    for r in range(z.blocks):
        both = dot(table, a3[:, r * z.t3 : (r + 1) * z.t3], NN)
        out[r] = both[:CLASS_ROWS] + both[CLASS_ROWS:]


def logits_body(z, pos, mine, part, local, bias, out, grad, loss):
    total = part[0]
    for r in range(1, 2 * z.rl):
        total = total + part[r]
    recip = inverse(z, mine, z.at_c3, z.l3)
    logits = total * recip + local[...] + bias[:CLASS_ROWS, 2:3]
    classes = lax.broadcasted_iota(I32, logits.shape, 0)
    logits = jnp.where(classes < 47, logits, -jnp.inf)
    label = jnp.where(
        pos[0] == 0,
        mine[z.at_label : z.at_label + 1, :],
        mine[z.at_label + z.l3 : z.at_label + z.l3 + 1, :],
    ).astype(I32)
    onehot = jnp.where(classes == label, 1.0, 0.0)
    top = jnp.max(logits, axis=0, keepdims=True)
    powers = jnp.exp(logits - top)
    norm = jnp.sum(powers, axis=0, keepdims=True)
    weight = jnp.sum(onehot * mine[z.id_rows : z.id_rows + CLASS_ROWS], axis=0, keepdims=True)
    target = jnp.sum(jnp.where(classes == label, logits, 0.0), axis=0, keepdims=True)
    each = weight * (jnp.log(norm) + top - target)
    loss[...] = jnp.broadcast_to(jnp.sum(each, axis=1, keepdims=True), loss.shape)
    dlogits = weight * (powers / norm - onehot) / mine[z.id_rows + CLASS_ROWS : z.id_rows + CLASS_ROWS + 1, :]
    grad[...] = dlogits
    scaled = dlogits * recip
    for r in range(2 * z.rl):
        out[r] = scaled


def back_last_body(z, pos, mine, gall, grad, a3, wlc, h2, slope, wmh, wml, out, dpre2, dwl):
    both = None
    for r in range(2 * z.rl):
        table = jnp.concatenate(halves(gall[r]), axis=0)
        term = dot(table, a3[:, r * z.t3 : (r + 1) * z.t3], NT)
        both = term if both is None else both + term
    spread = both[:CLASS_ROWS] + both[CLASS_ROWS:]
    dh = dot_full(wlc[1][:, :CLASS_ROWS], spread, NN)
    own = dot_full(wlc[0][:, :CLASS_ROWS], grad[...], NN)
    dh = dh + jnp.concatenate([own, jnp.zeros((256, z.t2 - z.t3), F32)], axis=1)
    dpre2[...] = dh * slope[...]
    rows = pl.ds(pl.multiple_of(pos[3] * 128, 128), 128)
    scaled = dot_split((wmh[1, rows, :], wml[1, rows, :]), halves(dpre2[...]), NN) * inverse(z, mine, z.at_c2, z.l2)
    for r in range(2 * z.rl):
        out[r] = scaled
    dwl[0] = dot_full(grad[...], h2[:, : z.t3], NT)
    dwl[1] = dot_full(spread, h2[...], NT)


def row_sums(value):
    ones = jnp.ones((8, value.shape[1]), BF16)
    high, low = halves(value)
    return dot(ones, high, NT) + dot(ones, low, NT)


def grads_body(z, pos, gall, a2, dpre2, wmh, wml, slope, x1, y2, dwl, grad, loss, out, first, mid, last):
    c = pos[3]
    mine = pl.ds(pl.multiple_of(c * 128, 128), 128)
    both = None
    for r in range(z.blocks):
        table = jnp.concatenate(halves(gall[r]), axis=0)
        term = dot(table, a2[:, r * z.t2 : (r + 1) * z.t2], NT)
        both = term if both is None else both + term
    dh = both[:128] + both[128:]
    at_own = dot_split((wmh[0, mine, :], wml[0, mine, :]), halves(dpre2[...]), NN)
    dh = dh + jnp.concatenate([at_own, jnp.zeros((128, z.t1 - z.t2), F32)], axis=1)
    dpre1 = dh * slope[mine]
    half2 = dpre2[mine]
    first[...] = dot_full(x1[...], dpre1, NT)
    mid[...] = dot_full(y2[...], half2, NT)
    b1, b2, b3 = row_sums(dpre1), row_sums(half2), row_sums(grad[...])
    last[...] = jnp.zeros_like(last)
    core0 = jnp.where(c == 0, 1.0, 0.0)
    for s in range(4):
        last[s, :CLASS_ROWS, :64] = dwl[0][:, 64 * s : 64 * s + 64] * core0
        last[s, :CLASS_ROWS, 64:] = dwl[1][:, 64 * s : 64 * s + 64] * (1.0 - core0)
        here = jnp.where(c == s // 2, 1.0, 0.0)
        at = 64 * (s % 2)
        last[s, ROW_HIDDEN : ROW_HIDDEN + 1, :64] = b1[0:1, at : at + 64] * here
        last[s, ROW_HIDDEN : ROW_HIDDEN + 1, 64:] = b2[0:1, at : at + 64] * here
        last[s, ROW_LAST : ROW_LAST + 1, :LANE_LOSS] = b3[0:1, :LANE_LOSS] * core0
        last[s, ROW_LAST : ROW_LAST + 1, LANE_LOSS : LANE_LOSS + 1] = loss[0:1, 0:1] * core0
    n = 4 * (z.nf + z.nm)
    for p in range(z.pieces):
        for s in range(4):
            e = z.nf * p
            at = 128 * (e // 32) + 32 * s + e % 32
            out[p, s * z.nf : (s + 1) * z.nf] = first[at : at + z.nf]
            e = z.nm * p
            at = 256 * (e // 64) + 64 * s + e % 64
            out[p, 4 * z.nf + s * z.nm : 4 * z.nf + (s + 1) * z.nm] = mid[at : at + z.nm]
            out[p, n + s * z.nl : n + (s + 1) * z.nl] = last[s, z.nl * p : z.nl * (p + 1)]


def sum_grads_body(z, pos, part, out):
    n = z.half_rows
    even, odd = part[0], part[1]
    for d in range(2, z.pieces, 2):
        even = even + part[d]
        odd = odd + part[d + 1]
    out[:n] = even[:n]
    out[n : 2 * n] = odd[:n]
    out[2 * n :] = even[n:] + odd[n:]


def share_body(z, pos, own, other, out):
    n, nf, nm, nl = z.half_rows, z.nf, z.nm, z.nl
    total = own[...] + other[...]
    piece = 4 * pos[1] + 2 * pos[2] + pos[3]
    lane = lax.broadcasted_iota(I32, (1, LANES), 1)
    squares = jnp.sum(total[: 2 * n] * total[: 2 * n], axis=0, keepdims=True)
    for s in range(4):
        for i in range(nl):
            row = total[2 * n + s * nl + i : 2 * n + s * nl + i + 1]
            at = piece * nl + i
            squares = squares + jnp.where(at <= ROW_HIDDEN, 1.0, 0.0) * row * row
            if s == 0:
                squares = squares + jnp.where(at == ROW_LAST, 1.0, 0.0) * jnp.where(lane < 47, row * row, 0.0)
    squares = jnp.broadcast_to(jnp.sum(squares, axis=1, keepdims=True), (1, LANES))
    pad = z.ag_rows - 2 * (nf + nm) - nl - 1
    for s in range(4):
        rows = []
        for h in range(2):
            rows.append(total[h * n + s * nf : h * n + (s + 1) * nf])
            rows.append(total[h * n + 4 * nf + s * nm : h * n + 4 * nf + (s + 1) * nm])
        rows += [total[2 * n + s * nl : 2 * n + (s + 1) * nl], squares]
        if pad:
            rows.append(jnp.zeros((pad, LANES), F32))
        rows = jnp.concatenate(rows, axis=0)
        for lead in range(z.rl):
            out[4 * lead + s] = rows


def update_body(z, pos, whole, mine, *refs):
    w, m, v = refs[0:5], refs[5:10], refs[10:15]
    new, moment, square = refs[15:20], refs[20:25], refs[25:30]
    loss, weight_sum, norm = refs[30:33]
    nf, nm, nl = z.nf, z.nm, z.nl
    at = 2 * (nf + nm) + nl
    total = whole[0, at : at + 1, 0:1]
    for p in range(1, z.pieces):
        total = total + whole[p, at : at + 1, 0:1]
    root = jnp.sqrt(total)
    scale = jnp.minimum(1.0, 0.01 / root)
    norm[...] = root
    weight_sum[...] = mine[z.id_rows + CLASS_ROWS : z.id_rows + CLASS_ROWS + 1, 0:1]

    def adamw(weight, grad, first, second):
        grad = grad * scale
        mo = 0.9 * first + 0.1 * grad
        sq = 0.999 * second + 0.001 * grad * grad
        corrected = mo / (1.0 - 0.9**STEP)
        rt = jnp.sqrt(sq / (1.0 - 0.999**STEP))
        return (weight - 0.05 * (corrected / (rt + 1e-08) + 0.01 * weight), mo, sq)

    def put(i, at, grad):
        outs = adamw(w[i][at], grad, m[i][at], v[i][at])
        new[i][at], moment[i][at], square[i][at] = outs

    h = nf + nm
    for p in range(z.pieces):
        e = nf * p
        g = jnp.concatenate([whole[p, :nf], whole[p, h : h + nf]], axis=1)
        put(0, (e // 32, slice(e % 32, e % 32 + nf), slice(None)), g)
        e = nm * p
        g = jnp.concatenate([whole[p, nf:h], whole[p, h + nf : 2 * h]], axis=1)
        put(1, (e // 64, slice(e % 64, e % 64 + nm), slice(None)), g)
        a = nl * p
        b = min(a + nl, 47)
        if a < b:
            for j in range(2):
                put(2, (slice(a, b), j, slice(None)), whole[p, 2 * h : 2 * h + b - a, 64 * j : 64 * j + 64])
        for i in range(nl):
            row = whole[p, 2 * h + i : 2 * h + i + 1]
            if a + i == ROW_HIDDEN:
                for j in range(2):
                    put(3, (slice(j, j + 1), slice(None)), row[:, 64 * j : 64 * j + 64])
            elif a + i == ROW_LAST:
                put(4, (slice(None), slice(None)), row[:, :47])
                loss[...] = row[:, LANE_LOSS : LANE_LOSS + 1]


def on_device(
    mesh, features, neigh_first, count_first, neigh_mid, count_mid, neigh_last, count_last, labels,
    w_first, w_mid, w_last, b_hidden, b_last,
    m_first, m_mid, m_last, m_hidden, m_bias,
    v_first, v_mid, v_last, v_hidden, v_bias,
):
    z = Sizes(mesh, features, neigh_first, neigh_mid, neigh_last)
    bind = functools.partial
    blocks = z.blocks

    def flip(value):
        return lax.ppermute(value, "c", [(0, 1), (1, 0)])

    def exchange(value):
        return lax.all_to_all(value, ("y", "rl"), 0, 0)

    def swapped(value):
        return jnp.transpose(value, (2, 0, 1))

    raw = (
        swapped(neigh_first), count_first, swapped(neigh_mid), count_mid, swapped(neigh_last), count_last, labels,
        jnp.transpose(features, (0, 2, 1)), w_first, w_mid, swapped(w_last), b_hidden,
    )
    ids, f0, f1, wmsg = call(
        bind(prep_body, z),
        [((4 * z.ranks, z.id_part, LANES), I32), ((32, z.s1), F32), ((32, z.s1), F32), ((248, 256), F32)],
        "prep", 58, scratch=[pltpu.VMEM((2, z.id_rows, LANES), I32), *like(*raw)], where=HBM, us=2.0,
    )(*raw)
    got0, got1 = (
        lax.ppermute(f, ("zh", "y"), [(2 * zh + y, 2 * (y ^ j) + zh) for zh in range(2) for y in range(2)])
        for j, f in enumerate((f0, f1))
    )
    ids = lax.all_to_all(ids, ("y", "c", "zh", "rl"), 0, 0)
    table = pltpu.VMEM((128, z.s1), BF16)
    sums = [((blocks, 64, z.t1), F32)]
    small = ((z.id_rows + CLASS_ROWS + 8, LANES), F32)
    a1, mine = call(
        bind(adjacency_first_body, z), [((z.s1, blocks * z.t1) if z.keep_first else (8, LANES), BF16), small],
        "adjacency_first", 4, us=6.0, scratch=tables(z, z.f1, z.l1, z.s1),
    )(ids, got0, got1)
    w_across = lax.ppermute(wmsg, "y", [(0, 1), (1, 0)])
    w_across = call(held_body, [((248, 256), F32)], "held", 4)(w_across, mine)[0]
    if z.keep_first:
        part = call(bind(first_kept_body, z), sums, "first", 4, us=3.0, scratch=[table])(a1, got0, got1, w_across)[0]
    else:
        part = call(
            bind(first_body, z), sums, "first", 16, us=8.0,
            scratch=[table, pltpu.VMEM((z.s1, z.t1), BF16), *tables(z, z.f1, z.l1, z.s1)],
        )(ids, got0, got1, w_across)[0]
    part = exchange(part)
    half = call(bind(sum_first_body, z), [((128, z.t1), F32)], "sum_first", 8)(mine, part, got0, got1)[0]
    other = flip(half)
    walls = (wmsg, w_across, flip(w_across), flip(wmsg))
    w1h, w1l, w2h, w2l, wmh, wml, wlt, wlc, bias = call(
        weights_body,
        [
            ((256, 256), BF16), ((256, 256), BF16), ((256, 512), BF16), ((256, 512), BF16),
            ((2, 256, 256), BF16), ((2, 256, 256), BF16),
            ((2, CLASS_ROWS, 256), F32), ((2, 256, 128), F32), ((256, 128), F32),
        ],
        "weights", 8,
        scratch=[pltpu.VMEM((4, 248, 256), F32), pltpu.VMEM((256, 256), F32), pltpu.VMEM((512, 256), F32)],
    )(*walls, b_last[None], half)
    a2 = call(
        bind(adjacency_mid_body, z), [((z.t1, blocks * z.t2), BF16)], "adjacency_mid", 4, us=3.0,
        scratch=tables(z, z.f2, z.l2, z.t1),
    )(ids, half)[0]
    part, x1, h1, slope1 = call(
        bind(hidden_one_body, z),
        [((blocks, 128, z.t2), F32), ((256, z.t1), F32), ((256, z.t1), F32), ((256, z.t1), F32)],
        "hidden_one", 16,
    )(half, other, w1h, w1l, bias, a2)
    part = exchange(part)
    half = call(bind(sum_mid_body, z), [((128, z.t2), F32)], "sum_mid", 8)(mine, part)[0]
    other = flip(half)
    a3 = call(
        bind(adjacency_last_body, z), [((z.t2, blocks * z.t3), BF16)], "adjacency_last", 4, us=1.0,
        scratch=tables(z, z.f3, z.l3, z.t2),
    )(ids, half)[0]
    part, y2, h2, slope2, local = call(
        bind(hidden_two_body, z),
        [
            ((blocks, CLASS_ROWS, z.t3), F32),
            ((512, z.t2), F32), ((256, z.t2), F32), ((256, z.t2), F32), ((CLASS_ROWS, z.t3), F32),
        ],
        "hidden_two", 12,
    )(half, other, h1, w2h, w2l, bias, wlt, a3)
    part = exchange(part)
    backs = [((blocks, 128, z.t2), F32), ((256, z.t2), F32), ((2, CLASS_ROWS, 256), F32)]
    ends = [((CLASS_ROWS, z.t3), F32), ((8, LANES), F32)]
    part, grad, loss = call(bind(logits_body, z), [((blocks, CLASS_ROWS, z.t3), F32), *ends], "logits", 8)(
        mine, part, local, bias
    )
    part = exchange(part)
    part, dpre2, dwl = call(bind(back_last_body, z), backs, "back_last", 12, us=1.5)(
        mine, part, grad, a3, wlc, h2, slope2, wmh, wml
    )
    part = exchange(part)
    part = call(
        bind(grads_body, z), [((z.pieces, 4 * (z.nf + z.nm + z.nl), LANES), F32)], "grads", 12,
        scratch=[
            pltpu.VMEM((256, 128), F32), pltpu.VMEM((512, 128), F32),
            pltpu.VMEM((4, LAST_ROWS, LANES), F32),
        ],
    )(part, a2, dpre2, wmh, wml, slope1, x1, y2, dwl, grad, loss)[0]
    part = lax.all_to_all(part, ("rl", "y", "c"), 0, 0)
    own = call(bind(sum_grads_body, z), [((z.sum_rows, LANES), F32)], "sum_grads", 8)(part)[0]
    other = lax.ppermute(own, "zh", [(0, 1), (1, 0)])
    part = call(bind(share_body, z), [((z.pieces, z.ag_rows, LANES), F32)], "share", 8)(own, other)[0]
    whole = lax.all_to_all(part, ("rl", "y", "c"), 0, 0)

    params = (w_first, w_mid, swapped(w_last), b_hidden, b_last[None])
    firsts = (m_first, m_mid, swapped(m_last), m_hidden, m_bias[None])
    seconds = (v_first, v_mid, swapped(v_last), v_hidden, v_bias[None])
    shapes = [(p.shape, F32) for p in params]
    state = (*params, *firsts, *seconds)
    outs = call(
        bind(update_body, z), shapes * 3 + [((1, 1), F32)] * 3, "update", 8
    )(whole, mine, *state)
    results = []
    for g in range(3):
        a, b, c, d, e = outs[5 * g : 5 * g + 5]
        results += [a, b, jnp.transpose(c, (1, 2, 0)), d, e[0]]
    return tuple(results) + tuple(o[0, 0] for o in outs[15:])


def solution(mesh):
    rows, cols = mesh.shape["rows"], mesh.shape["cols"]
    fine = Mesh(mesh.devices.reshape(2, rows // 2, 2, cols // 2), ("zh", "rl", "y", "c"))
    r, c = ("zh", "rl"), ("y", "c")
    weights = (P(None, c, None),) * 3 + (P(None, c), P())
    nodes = (P(None, r, None), P(None, r))
    placed = (P(None, r, c),) + nodes * 3 + (P(None, r),) + weights * 3
    return jax.shard_map(
        functools.partial(on_device, fine),
        mesh=fine,
        in_specs=placed,
        out_specs=weights * 3 + (P(), P(), P()),
        check_vma=False,
    )
```

```python
import functools

import jax
import jax.numpy as jnp
from jax import lax
from jax.experimental import pallas as pl
from jax.experimental.pallas import tpu as pltpu
from jax.sharding import Mesh
from jax.sharding import PartitionSpec as P

STEP = 5
F32 = jnp.float32
BF16 = jnp.bfloat16
I32 = jnp.int32
LANES = 128
CLASS_ROWS = 48
LAST_ROWS = 64
ROW_HIDDEN = 48
ROW_LAST = 50
LANE_LOSS = 47
MIB = 1 << 20


def dims(left, right):
    return (((left,), (right,)), ((), ()))


NN, NT = dims(1, 0), dims(1, 1)


def dot(left, right, form):
    return lax.dot_general(left, right, form, preferred_element_type=F32)


def halves(value):
    high = value.astype(BF16)
    return high, (value - high.astype(F32)).astype(BF16)


def dot_split(left, right, form):
    (lh, ll), (rh, rl) = left, right
    return dot(lh, rh, form) + dot(lh, rl, form) + dot(ll, rh, form)


def dot_full(left, right, form):
    return dot_split(halves(left), halves(right), form)


def sigmoid(value):
    return 1.0 / (1.0 + jnp.exp(-value))


VMEM = pl.BlockSpec(memory_space=pltpu.VMEM)
HBM = pl.BlockSpec(memory_space=pltpu.HBM)


AXES = ("zh", "rl", "y", "c")


def call(body, outs, name, vmem, scratch=(), where=VMEM, us=1.0):
    def placed(*refs):
        body([lax.axis_index(a) for a in AXES], *refs)

    def run(*args):
        return pl.pallas_call(
            placed,
            out_shape=[jax.ShapeDtypeStruct(s, d) for s, d in outs],
            in_specs=[where] * len(args),
            out_specs=[VMEM] * len(outs),
            scratch_shapes=list(scratch),
            name=name,
            compiler_params=pltpu.CompilerParams(vmem_limit_bytes=vmem * MIB),
            cost_estimate=pl.CostEstimate(flops=0, bytes_accessed=int(us * 3.6e6), transcendentals=0),
        )(*args)

    return run


def fetch(sources, targets, sems):
    copies = [pltpu.make_async_copy(s, t, sems.at[i]) for i, (s, t) in enumerate(zip(sources, targets))]
    for copy in copies:
        copy.start()
    for copy in copies:
        copy.wait()


def like(*arrays):
    return [pltpu.VMEM(a.shape, a.dtype) for a in arrays] + [pltpu.SemaphoreType.DMA((len(arrays),))]


class Sizes:
    def __init__(self, mesh, features, neigh_first, neigh_mid, neigh_last):
        self.ranks = mesh.shape["zh"] * mesh.shape["rl"]
        self.rl = mesh.shape["rl"]
        self.s1, self.t1 = features.shape[1], neigh_first.shape[1]
        self.t2, self.t3 = neigh_mid.shape[1], neigh_last.shape[1]
        self.f1, self.f2, self.f3 = neigh_first.shape[2], neigh_mid.shape[2], neigh_last.shape[2]
        l1, l2, l3 = self.t1 // LANES, self.t2 // LANES, self.t3 // LANES
        self.l1, self.l2, self.l3 = l1, l2, l3
        self.at_first = 0
        self.at_mid = self.at_first + self.f1 * l1
        self.at_last = self.at_mid + self.f2 * l2
        self.at_label = self.at_last + self.f3 * l3
        self.at_c1 = self.at_label + 2 * l3
        self.at_c2 = self.at_c1 + l1
        self.at_c3 = self.at_c2 + l2
        self.id_rows = -(-(self.at_c3 + l3) // 32) * 32
        self.id_part = self.id_rows // 4
        self.blocks = 2 * self.rl
        self.nf, self.nm, self.nl = 64 // self.blocks, 128 // self.blocks, LAST_ROWS // self.blocks
        self.pair = self.nl // 2
        self.at_m, self.at_l, self.piece_rows = 4 * self.nf, 4 * (self.nf + self.nm), 4 * (self.nf + self.nm + self.pair)
        self.share_rows = -(-(self.nf + self.nm + self.pair + 1) // 8) * 8


def prep_body(z, pos, *refs):
    ids, f0, f1, wmsg, rows = refs[12:17]
    nf, cf, nm, cm, nl, cl, labels, feats, wf, wm, wl, bh = refs[17:29]
    fetch(refs[:12], refs[17:29], refs[29])

    def put(mb, at, value):
        for j in range(value.shape[1] // LANES):
            rows[mb, at + j : at + j + 1, :] = value[:, j * LANES : (j + 1) * LANES]

    for mb in range(2):
        for fan, nb, cnt, at, at_c in (
            (z.f1, nf, cf, z.at_first, z.at_c1),
            (z.f2, nm, cm, z.at_mid, z.at_c2),
            (z.f3, nl, cl, z.at_last, z.at_c3),
        ):
            count = cnt[mb : mb + 1, :]
            lanes = count.shape[1] // LANES
            for k in range(fan):
                put(mb, at + k * lanes, jnp.where(count > k, nb[k, mb : mb + 1, :], -1))
            put(mb, at_c, count)
        for other in range(2):
            put(mb, z.at_label + other * z.l3, labels[other : other + 1, :])
        end = z.at_c3 + z.l3
        if end < z.id_rows:
            rows[mb, end:, :] = jnp.zeros((z.id_rows - end, LANES), I32)
    part = pl.ds(pl.multiple_of((2 * pos[2] + pos[3]) * z.id_part, 8), z.id_part)
    for mb in range(2):
        mine = rows[mb, part]
        for s in range(4):
            for lead in range(z.rl):
                ids[(2 * s + mb) * z.rl + lead] = mine
    y = pos[2]
    f0[...] = feats[y]
    f1[...] = feats[1 - y]
    for j in range(2):
        wmsg[32 * j : 32 * j + 32, :] = wf[j]
        wmsg[64 + 64 * j : 128 + 64 * j, :] = wm[j]
    wmsg[192:248, :] = jnp.zeros((56, 256), F32)
    for j in range(2):
        wmsg[192 : 192 + 47, 64 * j : 64 * j + 64] = wl[:, j, :]
        wmsg[240:241, 64 * j : 64 * j + 64] = bh[j : j + 1, :]


def weights_body(pos, own, acr, dia, cor, blast, after, w1h, w1l, w2h, w2l, wmh, wml, wlt, wlc, bias, wall, f32a, f32b):
    s = 2 * pos[2] + pos[3]
    for at, part in ((s, own), (s ^ 2, acr), (s ^ 3, dia), (s ^ 1, cor)):
        wall[at] = part[...]
    for s in range(4):
        for j in range(2):
            f32a[128 * j + 32 * s : 128 * j + 32 * s + 32, :] = wall[s, 32 * j : 32 * j + 32, :]
            f32b[256 * j + 64 * s : 256 * j + 64 * s + 64, :] = wall[s, 64 + 64 * j : 128 + 64 * j, :]
            wlt[j, :, 64 * s : 64 * s + 64] = wall[s, 192 : 192 + CLASS_ROWS, 64 * j : 64 * j + 64]
    w1h[...], w1l[...] = halves(f32a[...].T)
    w2h[...], w2l[...] = halves(f32b[...].T)
    for j in range(2):
        wmh[j], wml[j] = halves(f32b[256 * j : 256 * j + 256, :])
        wlc[j] = jnp.concatenate([wlt[j], jnp.zeros((128 - CLASS_ROWS, 256), F32)], axis=0).T
    rows = [jnp.concatenate([wall[s, 240:241, 64 * j : 64 * j + 64] for s in range(4)], axis=1) for j in range(2)]
    last = jnp.concatenate([blast[...], jnp.zeros((1, 256 - 47), F32)], axis=1)
    packed = jnp.concatenate(rows + [last, jnp.zeros((125, 256), F32)], axis=0)
    bias[...] = packed.T


PIECE = 256


def all_rows(z, ids, row, zs):
    first = (row // z.id_part * 2 + zs) * z.rl
    return ids[first : first + z.rl, row % z.id_part, :]


def distinct(z, ids, at, fan, lanes, size, base, local, times):
    for zs in range(2):
        for j in range(lanes):
            rows = [all_rows(z, ids, at + k * lanes + j, zs) for k in range(fan)]
            count = [jnp.ones(rows[0].shape, F32) for _ in range(fan)]
            seen = [None] * fan
            for a in range(fan):
                for b in range(a + 1, fan):
                    same = rows[a] == rows[b]
                    count[a] = count[a] + jnp.where(same, 1.0, 0.0)
                    seen[b] = same if seen[b] is None else jnp.logical_or(seen[b], same)
            for k in range(fan):
                times[zs * lanes + j, k] = count[k]
                rel = rows[k] - base
                for g in range(size // PIECE):
                    inside = jnp.logical_and(rel >= g * PIECE, rel < (g + 1) * PIECE)
                    if seen[k] is not None:
                        inside = jnp.logical_and(inside, jnp.logical_not(seen[k]))
                    local[zs * lanes + j, g * fan + k] = jnp.where(inside, rel - g * PIECE, -1).astype(F32)


def adjacency_block(z, zs, lead, fan, lanes, size, local, times, at, out, column):
    for j in range(lanes):
        row = pl.ds(lead, 1)
        many = [jnp.broadcast_to(times[zs * lanes + j, k, row], (PIECE, LANES)).astype(BF16) for k in range(fan)]
        for g in range(size // PIECE):
            total = jnp.zeros((PIECE, LANES), BF16)
            for k in range(fan):
                name = jnp.broadcast_to(local[zs * lanes + j, g * fan + k, row], (PIECE, LANES)).astype(BF16)
                total = jnp.where(at == name, many[k], total)
            out[g * PIECE : (g + 1) * PIECE, column(j)] = total


def numbers():
    return lax.broadcasted_iota(I32, (PIECE, LANES), 0).astype(F32).astype(BF16)


def tables(z, fan, lanes, size):
    return [
        pltpu.VMEM((2 * lanes, size // PIECE * fan, z.rl, LANES), F32),
        pltpu.VMEM((2 * lanes, fan, z.rl, LANES), F32),
    ]


def adjacency_all(z, ids, first, fan, lanes, size, base, local, times, out):
    distinct(z, ids, first, fan, lanes, size, base, local, times)
    at = numbers()
    for zs in range(2):

        def block(lead, carry):
            def column(j):
                return pl.ds(pl.multiple_of(((zs * z.rl + lead) * lanes + j) * LANES, LANES), LANES)

            adjacency_block(z, zs, lead, fan, lanes, size, local, times, at, out, column)
            return carry

        lax.fori_loop(0, z.rl, block, 0)


def adjacency_first_body(z, pos, ids, adj, small, local, times):
    me = pos[2] * z.rl + pos[1]
    for q in range(4):
        small[q * z.id_part : (q + 1) * z.id_part] = ids[2 * q * z.rl + me].astype(F32)
    weight, total = class_weights(z, ids)
    n = z.id_rows
    small[n : n + CLASS_ROWS] = jnp.broadcast_to(weight, (CLASS_ROWS, LANES))
    small[n + CLASS_ROWS :] = jnp.broadcast_to(total, (8, LANES))
    adjacency_all(z, ids, z.at_first, z.f1, z.l1, z.s1, me * z.s1, local, times, adj)


def adjacency_mid_body(z, pos, ids, after, a2, local, times):
    me = pos[2] * z.rl + pos[1]
    adjacency_all(z, ids, z.at_mid, z.f2, z.l2, z.t1, me * z.t1, local, times, a2)


def adjacency_last_body(z, pos, ids, after, a3, local, times):
    me = pos[2] * z.rl + pos[1]
    adjacency_all(z, ids, z.at_last, z.f3, z.l3, z.t2, me * z.t2, local, times, a3)


def class_weights(z, ids):
    classes = lax.broadcasted_iota(I32, (CLASS_ROWS, LANES), 0)
    total = jnp.zeros((CLASS_ROWS, LANES), F32)
    for zs in range(2):
        for other in range(2 * z.l3):
            rows = all_rows(z, ids, z.at_label + other, zs)
            for lead in range(z.rl):
                total = total + jnp.where(classes == rows[lead : lead + 1], 1.0, 0.0)
    counts = jnp.sum(total, axis=1, keepdims=True)
    weight = 1.0 / jnp.maximum(counts, 1.0)
    return weight, jnp.sum(counts * weight, axis=0, keepdims=True)


def columns(pos, got0, got1, lanes):
    swap = pos[0] == 1
    a, b = got0[:, :lanes], got1[:, :lanes]
    return jnp.where(swap, b, a), jnp.where(swap, a, b)


def first_table(z, pos, got0, got1, table):
    width = 2 * got0.shape[0]
    rows = jnp.concatenate(columns(pos, got0, got1, z.s1), axis=0)
    table[:width], table[width:] = halves(rows)


def first_body(z, pos, adj, got0, got1, after, out, table):
    first_table(z, pos, got0, got1, table)
    for r in range(z.blocks):
        both = dot(table[...], adj[:, r * z.t1 : (r + 1) * z.t1], NN)
        out[r] = both[: both.shape[0] // 2] + both[both.shape[0] // 2 :]


def inverse(z, mine, at, lanes):
    row = jnp.concatenate([mine[at + j : at + j + 1, :] for j in range(lanes)], axis=1)
    return 1.0 / row


def sum_first_body(z, pos, mine, part, got0, got1, out):
    half = got0.shape[0]
    out[:half], out[half : 2 * half] = columns(pos, got0, got1, z.t1)
    total = part[0]
    for r in range(1, 2 * z.rl):
        total = total + part[r]
    out[2 * half :] = total * inverse(z, mine, z.at_c1, z.l1)


def put_columns(pos, own, other, out):
    c = pos[3]
    for j in range(2):
        for y in range(2):
            at = 128 * j + 64 * y
            out[pl.ds(pl.multiple_of(at + 32 * c, 32), 32)] = own[64 * j + 32 * y : 64 * j + 32 * y + 32]
            out[pl.ds(pl.multiple_of(at + 32 * (1 - c), 32), 32)] = other[64 * j + 32 * y : 64 * j + 32 * y + 32]


def hidden_one_body(z, pos, own, other, w1h, w1l, bias, a2, out, x1, h1, slope):
    c = pos[3]
    put_columns(pos, own, other, x1)
    pre = dot_split((w1h[...], w1l[...]), halves(x1[...]), NN) + bias[:, 0:1]
    sigma = sigmoid(pre)
    h1[...] = pre * sigma
    slope[...] = sigma * (1.0 + pre * (1.0 - sigma))
    table = jnp.concatenate(halves(h1[pl.ds(pl.multiple_of(c * 128, 128), 128)]), axis=0)
    for r in range(2 * z.rl):
        both = dot(table, a2[:, r * z.t2 : (r + 1) * z.t2], NN)
        out[r] = both[:128] + both[128:]


def sum_mid_body(z, pos, mine, part, out):
    total = part[0]
    for r in range(1, 2 * z.rl):
        total = total + part[r]
    out[...] = total * inverse(z, mine, z.at_c2, z.l2)


def hidden_two_body(z, pos, own, other, h1, w2h, w2l, bias, wlt, a3, out, y2, h2, slope, local):
    c = pos[3]
    y2[:256] = h1[:, : z.t2]
    y2[pl.ds(pl.multiple_of(256 + c * 128, 128), 128)] = own[...]
    y2[pl.ds(pl.multiple_of(256 + (1 - c) * 128, 128), 128)] = other[...]
    pre = dot_split((w2h[...], w2l[...]), halves(y2[...]), NN) + bias[:, 1:2]
    sigma = sigmoid(pre)
    hidden = pre * sigma
    h2[...] = hidden
    slope[...] = sigma * (1.0 + pre * (1.0 - sigma))
    split = halves(hidden)
    local[...] = dot_split(halves(wlt[0]), (split[0][:, : z.t3], split[1][:, : z.t3]), NN)
    for_mean = dot_split(halves(wlt[1]), split, NN)
    table = jnp.concatenate(halves(for_mean), axis=0)
    for r in range(z.blocks):
        both = dot(table, a3[:, r * z.t3 : (r + 1) * z.t3], NN)
        out[r] = both[:CLASS_ROWS] + both[CLASS_ROWS:]


def logits_body(z, pos, mine, part, local, bias, out, grad, loss):
    total = part[0]
    for r in range(1, 2 * z.rl):
        total = total + part[r]
    recip = inverse(z, mine, z.at_c3, z.l3)
    logits = total * recip + local[...] + bias[:CLASS_ROWS, 2:3]
    classes = lax.broadcasted_iota(I32, logits.shape, 0)
    logits = jnp.where(classes < 47, logits, -jnp.inf)
    label = jnp.where(
        pos[0] == 0,
        mine[z.at_label : z.at_label + 1, :],
        mine[z.at_label + z.l3 : z.at_label + z.l3 + 1, :],
    ).astype(I32)
    onehot = jnp.where(classes == label, 1.0, 0.0)
    top = jnp.max(logits, axis=0, keepdims=True)
    powers = jnp.exp(logits - top)
    norm = jnp.sum(powers, axis=0, keepdims=True)
    weight = jnp.sum(onehot * mine[z.id_rows : z.id_rows + CLASS_ROWS], axis=0, keepdims=True)
    target = jnp.sum(jnp.where(classes == label, logits, 0.0), axis=0, keepdims=True)
    each = weight * (jnp.log(norm) + top - target)
    loss[...] = jnp.broadcast_to(jnp.sum(each, axis=1, keepdims=True), loss.shape)
    dlogits = weight * (powers / norm - onehot) / mine[z.id_rows + CLASS_ROWS : z.id_rows + CLASS_ROWS + 1, :]
    grad[...] = dlogits
    scaled = dlogits * recip
    for r in range(2 * z.rl):
        out[r] = scaled


def back_last_body(z, pos, mine, gall, grad, a3, wlc, h2, slope, wmh, wml, out, dpre2, dwl):
    both = None
    for r in range(2 * z.rl):
        table = jnp.concatenate(halves(gall[r]), axis=0)
        term = dot(table, a3[:, r * z.t3 : (r + 1) * z.t3], NT)
        both = term if both is None else both + term
    spread = both[:CLASS_ROWS] + both[CLASS_ROWS:]
    dh = dot_full(wlc[1][:, :CLASS_ROWS], spread, NN)
    own = dot_full(wlc[0][:, :CLASS_ROWS], grad[...], NN)
    dh = dh + jnp.concatenate([own, jnp.zeros((256, z.t2 - z.t3), F32)], axis=1)
    dpre2[...] = dh * slope[...]
    rows = pl.ds(pl.multiple_of(pos[3] * 128, 128), 128)
    scaled = dot_split((wmh[1, rows, :], wml[1, rows, :]), halves(dpre2[...]), NN) * inverse(z, mine, z.at_c2, z.l2)
    for r in range(2 * z.rl):
        out[r] = scaled
    dwl[0] = dot_full(grad[...], h2[:, : z.t3], NT)
    dwl[1] = dot_full(spread, h2[...], NT)


def row_sums(value):
    ones = jnp.ones((8, value.shape[1]), BF16)
    high, low = halves(value)
    return dot(ones, high, NT) + dot(ones, low, NT)


def grads_body(z, pos, gall, a2, dpre2, wmh, wml, slope, x1, y2, dwl, grad, loss, out, first, mid, last):
    c = pos[3]
    mine = pl.ds(pl.multiple_of(c * 128, 128), 128)
    both = None
    for r in range(z.blocks):
        table = jnp.concatenate(halves(gall[r]), axis=0)
        term = dot(table, a2[:, r * z.t2 : (r + 1) * z.t2], NT)
        both = term if both is None else both + term
    dh = both[:128] + both[128:]
    at_own = dot_split((wmh[0, mine, :], wml[0, mine, :]), halves(dpre2[...]), NN)
    dh = dh + jnp.concatenate([at_own, jnp.zeros((128, z.t1 - z.t2), F32)], axis=1)
    dpre1 = dh * slope[mine]
    half2 = dpre2[mine]
    first[...] = dot_full(x1[...], dpre1, NT)
    mid[...] = dot_full(y2[...], half2, NT)
    b1, b2, b3 = row_sums(dpre1), row_sums(half2), row_sums(grad[...])
    last[...] = jnp.zeros_like(last)
    core0 = jnp.where(c == 0, 1.0, 0.0)
    for s in range(4):
        last[s, :CLASS_ROWS, :64] = dwl[c, :, 64 * s : 64 * s + 64]
        here = jnp.where(c == s // 2, 1.0, 0.0)
        at = 64 * (s % 2)
        last[s, ROW_HIDDEN : ROW_HIDDEN + 1, :64] = b1[0:1, at : at + 64] * here
        last[s, ROW_HIDDEN + 1 : ROW_HIDDEN + 2, :64] = b2[0:1, at : at + 64] * here
        last[s, ROW_LAST : ROW_LAST + 1, :LANE_LOSS] = b3[0:1, :LANE_LOSS] * core0
        last[s, ROW_LAST : ROW_LAST + 1, LANE_LOSS : LANE_LOSS + 1] = loss[0:1, 0:1] * core0
    for p in range(z.blocks):
        for s in range(4):
            e = z.nf * p
            at = 128 * (e // 32) + 32 * s + e % 32
            out[p, s * z.nf : (s + 1) * z.nf] = first[at : at + z.nf]
            e = z.nm * p
            at = 256 * (e // 64) + 64 * s + e % 64
            out[p, z.at_m + s * z.nm : z.at_m + (s + 1) * z.nm] = mid[at : at + z.nm]
            e = z.nl * p
            two = [last[s, e + h * z.pair : e + (h + 1) * z.pair, :64] for h in range(2)]
            out[p, z.at_l + s * z.pair : z.at_l + (s + 1) * z.pair] = jnp.concatenate(two, axis=1)


def sum_grads_body(z, pos, part, out):
    total = part[0]
    for r in range(1, z.blocks):
        total = total + part[r]
    out[...] = total


def share_body(z, pos, own, other, out):
    nf, nm, pair = z.nf, z.nm, z.pair
    total = own[...] + other[...]
    piece = pos[2] * z.rl + pos[1]
    lane = lax.broadcasted_iota(I32, (1, LANES), 1)
    squares = jnp.sum(total[: z.at_l] * total[: z.at_l], axis=0, keepdims=True)
    for s in range(4):
        for i in range(pair):
            row = total[z.at_l + s * pair + i : z.at_l + s * pair + i + 1]
            at = piece * z.nl + i + jnp.where(lane < 64, 0, pair)
            keep = at < ROW_LAST
            if s == 0:
                keep = jnp.logical_or(keep, jnp.logical_and(at == ROW_LAST, lane % 64 < 47))
            squares = squares + jnp.where(keep, row * row, 0.0)
    squares = jnp.broadcast_to(jnp.sum(squares, axis=1, keepdims=True), (1, LANES))
    pad = z.share_rows - nf - nm - pair - 1
    for s in range(4):
        rows = [
            total[s * nf : (s + 1) * nf],
            total[z.at_m + s * nm : z.at_m + (s + 1) * nm],
            total[z.at_l + s * pair : z.at_l + (s + 1) * pair],
            squares,
        ]
        if pad:
            rows.append(jnp.zeros((pad, LANES), F32))
        rows = jnp.concatenate(rows, axis=0)
        for lead in range(z.rl):
            out[4 * lead + s] = rows


def update_body(z, pos, whole, mine, *refs):
    w, m, v = refs[0:5], refs[5:10], refs[10:15]
    new, moment, square = refs[15:20], refs[20:25], refs[25:30]
    loss, weight_sum, norm = refs[30:33]
    nf, nm, nl, pair = z.nf, z.nm, z.nl, z.pair
    h = nf + nm
    total = whole[0, h + pair : h + pair + 1, 0:1]
    for p in range(1, 4 * z.rl):
        total = total + whole[p, h + pair : h + pair + 1, 0:1]
    root = jnp.sqrt(total)
    scale = jnp.minimum(1.0, 0.01 / root)
    norm[...] = root
    weight_sum[...] = mine[z.id_rows + CLASS_ROWS : z.id_rows + CLASS_ROWS + 1, 0:1]

    def adamw(weight, grad, first, second):
        grad = grad * scale
        mo = 0.9 * first + 0.1 * grad
        sq = 0.999 * second + 0.001 * grad * grad
        corrected = mo / (1.0 - 0.9**STEP)
        rt = jnp.sqrt(sq / (1.0 - 0.999**STEP))
        return (weight - 0.05 * (corrected / (rt + 1e-08) + 0.01 * weight), mo, sq)

    def put(i, at, grad):
        outs = adamw(w[i][at], grad, m[i][at], v[i][at])
        new[i][at], moment[i][at], square[i][at] = outs

    def source(p, c):
        return 4 * (p % z.rl) + 2 * (p // z.rl) + c

    def class_row(row, c):
        p, i = row // nl, row % nl
        at, lane = h + i % pair, 64 * (i // pair)
        return whole[source(p, c), at : at + 1, lane : lane + 64]

    for p in range(z.blocks):
        a, b = source(p, 0), source(p, 1)
        e = nf * p
        g = jnp.concatenate([whole[a, :nf], whole[b, :nf]], axis=1)
        put(0, (e // 32, slice(e % 32, e % 32 + nf), slice(None)), g)
        e = nm * p
        g = jnp.concatenate([whole[a, nf:h], whole[b, nf:h]], axis=1)
        put(1, (e // 64, slice(e % 64, e % 64 + nm), slice(None)), g)
        for j, src in enumerate((a, b)):
            for half in range(2):
                at = nl * p + half * pair
                end = min(at + pair, 47)
                if at < end:
                    g = whole[src, h : h + end - at, 64 * half : 64 * half + 64]
                    put(2, (slice(at, end), j, slice(None)), g)
    for j in range(2):
        g = jnp.where(pos[2] == 0, class_row(ROW_HIDDEN + j, 0), class_row(ROW_HIDDEN + j, 1))
        put(3, (slice(j, j + 1), slice(None)), g)
    row = class_row(ROW_LAST, 0)
    put(4, (slice(None), slice(None)), row[:, :47])
    loss[...] = row[:, LANE_LOSS : LANE_LOSS + 1]


def on_device(
    mesh, features, neigh_first, count_first, neigh_mid, count_mid, neigh_last, count_last, labels,
    w_first, w_mid, w_last, b_hidden, b_last,
    m_first, m_mid, m_last, m_hidden, m_bias,
    v_first, v_mid, v_last, v_hidden, v_bias,
):
    z = Sizes(mesh, features, neigh_first, neigh_mid, neigh_last)
    bind = functools.partial
    blocks = z.blocks

    def flip(value):
        return lax.ppermute(value, "c", [(0, 1), (1, 0)])

    def exchange(value):
        return lax.all_to_all(value, ("y", "rl"), 0, 0)

    def swapped(value):
        return jnp.transpose(value, (2, 0, 1))

    raw = (
        swapped(neigh_first), count_first, swapped(neigh_mid), count_mid, swapped(neigh_last), count_last, labels,
        jnp.transpose(features, (0, 2, 1)), w_first, w_mid, swapped(w_last), b_hidden,
    )
    ids, f0, f1, wmsg = call(
        bind(prep_body, z),
        [((4 * z.ranks, z.id_part, LANES), I32), ((32, z.s1), F32), ((32, z.s1), F32), ((248, 256), F32)],
        "prep", 58, scratch=[pltpu.VMEM((2, z.id_rows, LANES), I32), *like(*raw)], where=HBM, us=2.0,
    )(*raw)
    got0, got1 = (
        lax.ppermute(f, ("zh", "y"), [(2 * zh + y, 2 * (y ^ j) + zh) for zh in range(2) for y in range(2)])
        for j, f in enumerate((f0, f1))
    )
    ids = lax.all_to_all(ids, ("y", "c", "zh", "rl"), 0, 0)
    w_across = lax.ppermute(wmsg, "y", [(0, 1), (1, 0)])
    a1, mine = call(
        bind(adjacency_first_body, z),
        [((z.s1, blocks * z.t1), BF16), ((z.id_rows + CLASS_ROWS + 8, LANES), F32)], "adjacency_first", 4 + blocks,
        us=6.0, scratch=tables(z, z.f1, z.l1, z.s1),
    )(ids)
    part = call(
        bind(first_body, z), [((blocks, 64, z.t1), F32)], "first", 4 + blocks, scratch=[pltpu.VMEM((128, z.s1), BF16)],
    )(a1, got0, got1, w_across)[0]
    part = exchange(part)
    half = call(bind(sum_first_body, z), [((128, z.t1), F32)], "sum_first", 8)(mine, part, got0, got1)[0]
    other = flip(half)
    walls = (wmsg, w_across, flip(w_across), flip(wmsg))
    w1h, w1l, w2h, w2l, wmh, wml, wlt, wlc, bias = call(
        weights_body,
        [
            ((256, 256), BF16), ((256, 256), BF16), ((256, 512), BF16), ((256, 512), BF16),
            ((2, 256, 256), BF16), ((2, 256, 256), BF16),
            ((2, CLASS_ROWS, 256), F32), ((2, 256, 128), F32), ((256, 128), F32),
        ],
        "weights", 8,
        scratch=[pltpu.VMEM((4, 248, 256), F32), pltpu.VMEM((256, 256), F32), pltpu.VMEM((512, 256), F32)],
    )(*walls, b_last[None], half)
    a2 = call(
        bind(adjacency_mid_body, z), [((z.t1, blocks * z.t2), BF16)], "adjacency_mid", 4, us=3.0,
        scratch=tables(z, z.f2, z.l2, z.t1),
    )(ids, half)[0]
    part, x1, h1, slope1 = call(
        bind(hidden_one_body, z),
        [((blocks, 128, z.t2), F32), ((256, z.t1), F32), ((256, z.t1), F32), ((256, z.t1), F32)],
        "hidden_one", 16,
    )(half, other, w1h, w1l, bias, a2)
    part = exchange(part)
    half = call(bind(sum_mid_body, z), [((128, z.t2), F32)], "sum_mid", 8)(mine, part)[0]
    other = flip(half)
    a3 = call(
        bind(adjacency_last_body, z), [((z.t2, blocks * z.t3), BF16)], "adjacency_last", 4, us=1.0,
        scratch=tables(z, z.f3, z.l3, z.t2),
    )(ids, half)[0]
    part, y2, h2, slope2, local = call(
        bind(hidden_two_body, z),
        [
            ((blocks, CLASS_ROWS, z.t3), F32),
            ((512, z.t2), F32), ((256, z.t2), F32), ((256, z.t2), F32), ((CLASS_ROWS, z.t3), F32),
        ],
        "hidden_two", 12,
    )(half, other, h1, w2h, w2l, bias, wlt, a3)
    part = exchange(part)
    backs = [((blocks, 128, z.t2), F32), ((256, z.t2), F32), ((2, CLASS_ROWS, 256), F32)]
    ends = [((CLASS_ROWS, z.t3), F32), ((8, LANES), F32)]
    part, grad, loss = call(bind(logits_body, z), [((blocks, CLASS_ROWS, z.t3), F32), *ends], "logits", 8)(
        mine, part, local, bias
    )
    part = exchange(part)
    part, dpre2, dwl = call(bind(back_last_body, z), backs, "back_last", 12, us=1.5)(
        mine, part, grad, a3, wlc, h2, slope2, wmh, wml
    )
    part = exchange(part)
    part = call(
        bind(grads_body, z), [((blocks, z.piece_rows, LANES), F32)], "grads", 12,
        scratch=[
            pltpu.VMEM((256, 128), F32), pltpu.VMEM((512, 128), F32),
            pltpu.VMEM((4, LAST_ROWS, LANES), F32),
        ],
    )(part, a2, dpre2, wmh, wml, slope1, x1, y2, dwl, grad, loss)[0]
    part = exchange(part)
    own = call(bind(sum_grads_body, z), [((z.piece_rows, LANES), F32)], "sum_grads", 8)(part)[0]
    other = lax.ppermute(own, "zh", [(0, 1), (1, 0)])
    part = call(bind(share_body, z), [((4 * z.rl, z.share_rows, LANES), F32)], "share", 8)(own, other)[0]
    whole = lax.all_to_all(part, ("rl", "y", "c"), 0, 0)

    params = (w_first, w_mid, swapped(w_last), b_hidden, b_last[None])
    firsts = (m_first, m_mid, swapped(m_last), m_hidden, m_bias[None])
    seconds = (v_first, v_mid, swapped(v_last), v_hidden, v_bias[None])
    shapes = [(p.shape, F32) for p in params]
    state = (*params, *firsts, *seconds)
    outs = call(
        bind(update_body, z), shapes * 3 + [((1, 1), F32)] * 3, "update", 8
    )(whole, mine, *state)
    results = []
    for g in range(3):
        a, b, c, d, e = outs[5 * g : 5 * g + 5]
        results += [a, b, jnp.transpose(c, (1, 2, 0)), d, e[0]]
    return tuple(results) + tuple(o[0, 0] for o in outs[15:])


def solution(mesh):
    rows, cols = mesh.shape["rows"], mesh.shape["cols"]
    fine = Mesh(mesh.devices.reshape(2, rows // 2, 2, cols // 2), ("zh", "rl", "y", "c"))
    r, c = ("zh", "rl"), ("y", "c")
    weights = (P(None, c, None),) * 3 + (P(None, c), P())
    nodes = (P(None, r, None), P(None, r))
    placed = (P(None, r, c),) + nodes * 3 + (P(None, r),) + weights * 3
    return jax.shard_map(
        functools.partial(on_device, fine),
        mesh=fine,
        in_specs=placed,
        out_specs=weights * 3 + (P(), P(), P()),
        check_vma=False,
    )
```

```python
import functools

import jax
import jax.numpy as jnp
from jax import lax
from jax.experimental import pallas as pl
from jax.experimental.pallas import tpu as pltpu
from jax.sharding import Mesh
from jax.sharding import PartitionSpec as P

STEP = 5
F32 = jnp.float32
BF16 = jnp.bfloat16
I32 = jnp.int32
LANES = 128
CLASS_ROWS = 48
LAST_ROWS = 64
ROW_HIDDEN = 48
ROW_LAST = 50
LANE_LOSS = 47
MIB = 1 << 20


def dims(left, right):
    return (((left,), (right,)), ((), ()))


NN, NT = dims(1, 0), dims(1, 1)


def dot(left, right, form):
    return lax.dot_general(left, right, form, preferred_element_type=F32)


def halves(value):
    high = value.astype(BF16)
    return high, (value - high.astype(F32)).astype(BF16)


def dot_split(left, right, form):
    (lh, ll), (rh, rl) = left, right
    return dot(lh, rh, form) + dot(lh, rl, form) + dot(ll, rh, form)


def dot_full(left, right, form):
    return dot_split(halves(left), halves(right), form)


def sigmoid(value):
    return 1.0 / (1.0 + jnp.exp(-value))


VMEM = pl.BlockSpec(memory_space=pltpu.VMEM)
HBM = pl.BlockSpec(memory_space=pltpu.HBM)


AXES = ("zh", "rl", "y", "c")


def call(body, outs, name, vmem, scratch=(), where=VMEM, us=1.0):
    def placed(*refs):
        body([lax.axis_index(a) for a in AXES], *refs)

    def run(*args):
        return pl.pallas_call(
            placed,
            out_shape=[jax.ShapeDtypeStruct(s, d) for s, d in outs],
            in_specs=[where] * len(args),
            out_specs=[VMEM] * len(outs),
            scratch_shapes=list(scratch),
            name=name,
            compiler_params=pltpu.CompilerParams(vmem_limit_bytes=vmem * MIB),
            cost_estimate=pl.CostEstimate(flops=0, bytes_accessed=int(us * 3.6e6), transcendentals=0),
        )(*args)

    return run


def fetch(sources, targets, sems):
    copies = [pltpu.make_async_copy(s, t, sems.at[i]) for i, (s, t) in enumerate(zip(sources, targets))]
    for copy in copies:
        copy.start()
    for copy in copies:
        copy.wait()


def like(*arrays):
    return [pltpu.VMEM(a.shape, a.dtype) for a in arrays] + [pltpu.SemaphoreType.DMA((len(arrays),))]


class Sizes:
    def __init__(self, mesh, features, neigh_first, neigh_mid, neigh_last):
        self.ranks = mesh.shape["zh"] * mesh.shape["rl"]
        self.rl = mesh.shape["rl"]
        self.s1, self.t1 = features.shape[1], neigh_first.shape[1]
        self.t2, self.t3 = neigh_mid.shape[1], neigh_last.shape[1]
        self.f1, self.f2, self.f3 = neigh_first.shape[2], neigh_mid.shape[2], neigh_last.shape[2]
        l1, l2, l3 = self.t1 // LANES, self.t2 // LANES, self.t3 // LANES
        self.l1, self.l2, self.l3 = l1, l2, l3
        self.at_first = 0
        self.at_mid = self.at_first + self.f1 * l1
        self.at_last = self.at_mid + self.f2 * l2
        self.at_label = self.at_last + self.f3 * l3
        self.at_c1 = self.at_label + 2 * l3
        self.at_c2 = self.at_c1 + l1
        self.at_c3 = self.at_c2 + l2
        self.id_rows = -(-(self.at_c3 + l3) // 32) * 32
        self.id_part = self.id_rows // 4
        self.blocks = 2 * self.rl
        self.nf, self.nm, self.nl = 64 // self.blocks, 128 // self.blocks, LAST_ROWS // self.blocks
        self.pair = self.nl // 2
        self.at_m, self.at_l, self.piece_rows = 4 * self.nf, 4 * (self.nf + self.nm), 4 * (self.nf + self.nm + self.pair)
        self.share_rows = -(-(self.nf + self.nm + self.pair + 1) // 8) * 8


def ids_body(z, pos, *refs):
    ids, rows = refs[7:9]
    nf, cf, nm, cm, nl, cl, labels = refs[9:16]
    fetch(refs[:7], refs[9:16], refs[16])

    def put(mb, at, value):
        for j in range(value.shape[1] // LANES):
            rows[mb, at + j : at + j + 1, :] = value[:, j * LANES : (j + 1) * LANES]

    for mb in range(2):
        for fan, nb, cnt, at, at_c in (
            (z.f1, nf, cf, z.at_first, z.at_c1),
            (z.f2, nm, cm, z.at_mid, z.at_c2),
            (z.f3, nl, cl, z.at_last, z.at_c3),
        ):
            count = cnt[mb : mb + 1, :]
            lanes = count.shape[1] // LANES
            for k in range(fan):
                put(mb, at + k * lanes, jnp.where(count > k, nb[k, mb : mb + 1, :], -1))
            put(mb, at_c, count)
        for other in range(2):
            put(mb, z.at_label + other * z.l3, labels[other : other + 1, :])
        end = z.at_c3 + z.l3
        if end < z.id_rows:
            rows[mb, end:, :] = jnp.zeros((z.id_rows - end, LANES), I32)
    part = pl.ds(pl.multiple_of((2 * pos[2] + pos[3]) * z.id_part, 8), z.id_part)
    for mb in range(2):
        mine = rows[mb, part]
        for s in range(4):
            for lead in range(z.rl):
                ids[(2 * s + mb) * z.rl + lead] = mine


def prep_body(z, pos, *refs):
    f0, f1, wmsg = refs[5:8]
    feats, wf, wm, wl, bh = refs[8:13]
    fetch(refs[:5], refs[8:13], refs[13])
    y = pos[2]
    f0[...] = feats[y]
    f1[...] = feats[1 - y]
    for j in range(2):
        wmsg[32 * j : 32 * j + 32, :] = wf[j]
        wmsg[64 + 64 * j : 128 + 64 * j, :] = wm[j]
    wmsg[192:248, :] = jnp.zeros((56, 256), F32)
    for j in range(2):
        wmsg[192 : 192 + 47, 64 * j : 64 * j + 64] = wl[:, j, :]
        wmsg[240:241, 64 * j : 64 * j + 64] = bh[j : j + 1, :]


def weights_body(pos, own, acr, dia, cor, blast, after, w1h, w1l, w2h, w2l, wmh, wml, wlt, wlc, bias, wall, f32a, f32b):
    s = 2 * pos[2] + pos[3]
    for at, part in ((s, own), (s ^ 2, acr), (s ^ 3, dia), (s ^ 1, cor)):
        wall[at] = part[...]
    for s in range(4):
        for j in range(2):
            f32a[128 * j + 32 * s : 128 * j + 32 * s + 32, :] = wall[s, 32 * j : 32 * j + 32, :]
            f32b[256 * j + 64 * s : 256 * j + 64 * s + 64, :] = wall[s, 64 + 64 * j : 128 + 64 * j, :]
            wlt[j, :, 64 * s : 64 * s + 64] = wall[s, 192 : 192 + CLASS_ROWS, 64 * j : 64 * j + 64]
    w1h[...], w1l[...] = halves(f32a[...].T)
    w2h[...], w2l[...] = halves(f32b[...].T)
    for j in range(2):
        wmh[j], wml[j] = halves(f32b[256 * j : 256 * j + 256, :])
        wlc[j] = jnp.concatenate([wlt[j], jnp.zeros((128 - CLASS_ROWS, 256), F32)], axis=0).T
    rows = [jnp.concatenate([wall[s, 240:241, 64 * j : 64 * j + 64] for s in range(4)], axis=1) for j in range(2)]
    last = jnp.concatenate([blast[...], jnp.zeros((1, 256 - 47), F32)], axis=1)
    packed = jnp.concatenate(rows + [last, jnp.zeros((125, 256), F32)], axis=0)
    bias[...] = packed.T


PIECE = 256


def all_rows(z, ids, row, zs):
    first = (row // z.id_part * 2 + zs) * z.rl
    return ids[first : first + z.rl, row % z.id_part, :]


def distinct(z, ids, at, fan, lanes, size, base, local, times):
    for zs in range(2):
        for j in range(lanes):
            rows = [all_rows(z, ids, at + k * lanes + j, zs) for k in range(fan)]
            count = [jnp.ones(rows[0].shape, F32) for _ in range(fan)]
            seen = [None] * fan
            for a in range(fan):
                for b in range(a + 1, fan):
                    same = rows[a] == rows[b]
                    count[a] = count[a] + jnp.where(same, 1.0, 0.0)
                    seen[b] = same if seen[b] is None else jnp.logical_or(seen[b], same)
            for k in range(fan):
                times[zs * lanes + j, k] = count[k]
                rel = rows[k] - base
                for g in range(size // PIECE):
                    inside = jnp.logical_and(rel >= g * PIECE, rel < (g + 1) * PIECE)
                    if seen[k] is not None:
                        inside = jnp.logical_and(inside, jnp.logical_not(seen[k]))
                    local[zs * lanes + j, g * fan + k] = jnp.where(inside, rel - g * PIECE, -1).astype(F32)


def adjacency_block(z, zs, lead, fan, lanes, size, local, times, at, out, column):
    for j in range(lanes):
        row = pl.ds(lead, 1)
        many = [jnp.broadcast_to(times[zs * lanes + j, k, row], (PIECE, LANES)).astype(BF16) for k in range(fan)]
        for g in range(size // PIECE):
            total = jnp.zeros((PIECE, LANES), BF16)
            for k in range(fan):
                name = jnp.broadcast_to(local[zs * lanes + j, g * fan + k, row], (PIECE, LANES)).astype(BF16)
                total = jnp.where(at == name, many[k], total)
            out[g * PIECE : (g + 1) * PIECE, column(j)] = total


def numbers():
    return lax.broadcasted_iota(I32, (PIECE, LANES), 0).astype(F32).astype(BF16)


def tables(z, fan, lanes, size):
    return [
        pltpu.VMEM((2 * lanes, size // PIECE * fan, z.rl, LANES), F32),
        pltpu.VMEM((2 * lanes, fan, z.rl, LANES), F32),
    ]


def adjacency_all(z, ids, first, fan, lanes, size, base, local, times, out):
    distinct(z, ids, first, fan, lanes, size, base, local, times)
    at = numbers()
    for zs in range(2):

        def block(lead, carry):
            def column(j):
                return pl.ds(pl.multiple_of(((zs * z.rl + lead) * lanes + j) * LANES, LANES), LANES)

            adjacency_block(z, zs, lead, fan, lanes, size, local, times, at, out, column)
            return carry

        lax.fori_loop(0, z.rl, block, 0)


def adjacency_first_body(z, pos, ids, adj, small, local, times):
    me = pos[2] * z.rl + pos[1]
    for q in range(4):
        small[q * z.id_part : (q + 1) * z.id_part] = ids[2 * q * z.rl + me].astype(F32)
    weight, total = class_weights(z, ids)
    n = z.id_rows
    small[n : n + CLASS_ROWS] = jnp.broadcast_to(weight, (CLASS_ROWS, LANES))
    small[n + CLASS_ROWS :] = jnp.broadcast_to(total, (8, LANES))
    adjacency_all(z, ids, z.at_first, z.f1, z.l1, z.s1, me * z.s1, local, times, adj)


def adjacency_mid_body(z, pos, ids, after, a2, local, times):
    me = pos[2] * z.rl + pos[1]
    adjacency_all(z, ids, z.at_mid, z.f2, z.l2, z.t1, me * z.t1, local, times, a2)


def adjacency_last_body(z, pos, ids, after, a3, local, times):
    me = pos[2] * z.rl + pos[1]
    adjacency_all(z, ids, z.at_last, z.f3, z.l3, z.t2, me * z.t2, local, times, a3)


def class_weights(z, ids):
    classes = lax.broadcasted_iota(I32, (CLASS_ROWS, LANES), 0)
    total = jnp.zeros((CLASS_ROWS, LANES), F32)
    for zs in range(2):
        for other in range(2 * z.l3):
            rows = all_rows(z, ids, z.at_label + other, zs)
            for lead in range(z.rl):
                total = total + jnp.where(classes == rows[lead : lead + 1], 1.0, 0.0)
    counts = jnp.sum(total, axis=1, keepdims=True)
    weight = 1.0 / jnp.maximum(counts, 1.0)
    return weight, jnp.sum(counts * weight, axis=0, keepdims=True)


def columns(pos, got0, got1, lanes):
    swap = pos[0] == 1
    a, b = got0[:, :lanes], got1[:, :lanes]
    return jnp.where(swap, b, a), jnp.where(swap, a, b)


def first_table(z, pos, got0, got1, table):
    width = 2 * got0.shape[0]
    rows = jnp.concatenate(columns(pos, got0, got1, z.s1), axis=0)
    table[:width], table[width:] = halves(rows)


def first_body(z, pos, adj, got0, got1, after, out, table):
    first_table(z, pos, got0, got1, table)
    for r in range(z.blocks):
        both = dot(table[...], adj[:, r * z.t1 : (r + 1) * z.t1], NN)
        out[r] = both[: both.shape[0] // 2] + both[both.shape[0] // 2 :]


def inverse(z, mine, at, lanes):
    row = jnp.concatenate([mine[at + j : at + j + 1, :] for j in range(lanes)], axis=1)
    return 1.0 / row


def sum_first_body(z, pos, mine, part, got0, got1, out):
    half = got0.shape[0]
    out[:half], out[half : 2 * half] = columns(pos, got0, got1, z.t1)
    total = part[0]
    for r in range(1, 2 * z.rl):
        total = total + part[r]
    out[2 * half :] = total * inverse(z, mine, z.at_c1, z.l1)


def put_columns(pos, own, other, out):
    c = pos[3]
    for j in range(2):
        for y in range(2):
            at = 128 * j + 64 * y
            out[pl.ds(pl.multiple_of(at + 32 * c, 32), 32)] = own[64 * j + 32 * y : 64 * j + 32 * y + 32]
            out[pl.ds(pl.multiple_of(at + 32 * (1 - c), 32), 32)] = other[64 * j + 32 * y : 64 * j + 32 * y + 32]


def hidden_one_body(z, pos, own, other, w1h, w1l, bias, a2, out, x1, h1, slope):
    c = pos[3]
    put_columns(pos, own, other, x1)
    pre = dot_split((w1h[...], w1l[...]), halves(x1[...]), NN) + bias[:, 0:1]
    sigma = sigmoid(pre)
    h1[...] = pre * sigma
    slope[...] = sigma * (1.0 + pre * (1.0 - sigma))
    table = jnp.concatenate(halves(h1[pl.ds(pl.multiple_of(c * 128, 128), 128)]), axis=0)
    for r in range(2 * z.rl):
        both = dot(table, a2[:, r * z.t2 : (r + 1) * z.t2], NN)
        out[r] = both[:128] + both[128:]


def sum_mid_body(z, pos, mine, part, out):
    total = part[0]
    for r in range(1, 2 * z.rl):
        total = total + part[r]
    out[...] = total * inverse(z, mine, z.at_c2, z.l2)


def hidden_two_body(z, pos, own, other, h1, w2h, w2l, bias, wlt, a3, out, y2, h2, slope, local):
    c = pos[3]
    y2[:256] = h1[:, : z.t2]
    y2[pl.ds(pl.multiple_of(256 + c * 128, 128), 128)] = own[...]
    y2[pl.ds(pl.multiple_of(256 + (1 - c) * 128, 128), 128)] = other[...]
    pre = dot_split((w2h[...], w2l[...]), halves(y2[...]), NN) + bias[:, 1:2]
    sigma = sigmoid(pre)
    hidden = pre * sigma
    h2[...] = hidden
    slope[...] = sigma * (1.0 + pre * (1.0 - sigma))
    split = halves(hidden)
    local[...] = dot_split(halves(wlt[0]), (split[0][:, : z.t3], split[1][:, : z.t3]), NN)
    for_mean = dot_split(halves(wlt[1]), split, NN)
    table = jnp.concatenate(halves(for_mean), axis=0)
    for r in range(z.blocks):
        both = dot(table, a3[:, r * z.t3 : (r + 1) * z.t3], NN)
        out[r] = both[:CLASS_ROWS] + both[CLASS_ROWS:]


def logits_body(z, pos, mine, part, local, bias, out, grad, loss):
    total = part[0]
    for r in range(1, 2 * z.rl):
        total = total + part[r]
    recip = inverse(z, mine, z.at_c3, z.l3)
    logits = total * recip + local[...] + bias[:CLASS_ROWS, 2:3]
    classes = lax.broadcasted_iota(I32, logits.shape, 0)
    logits = jnp.where(classes < 47, logits, -jnp.inf)
    label = jnp.where(
        pos[0] == 0,
        mine[z.at_label : z.at_label + 1, :],
        mine[z.at_label + z.l3 : z.at_label + z.l3 + 1, :],
    ).astype(I32)
    onehot = jnp.where(classes == label, 1.0, 0.0)
    top = jnp.max(logits, axis=0, keepdims=True)
    powers = jnp.exp(logits - top)
    norm = jnp.sum(powers, axis=0, keepdims=True)
    weight = jnp.sum(onehot * mine[z.id_rows : z.id_rows + CLASS_ROWS], axis=0, keepdims=True)
    target = jnp.sum(jnp.where(classes == label, logits, 0.0), axis=0, keepdims=True)
    each = weight * (jnp.log(norm) + top - target)
    loss[...] = jnp.broadcast_to(jnp.sum(each, axis=1, keepdims=True), loss.shape)
    dlogits = weight * (powers / norm - onehot) / mine[z.id_rows + CLASS_ROWS : z.id_rows + CLASS_ROWS + 1, :]
    grad[...] = dlogits
    scaled = dlogits * recip
    for r in range(2 * z.rl):
        out[r] = scaled


def back_last_body(z, pos, mine, gall, grad, a3, wlc, h2, slope, wmh, wml, out, dpre2, dwl):
    both = None
    for r in range(2 * z.rl):
        table = jnp.concatenate(halves(gall[r]), axis=0)
        term = dot(table, a3[:, r * z.t3 : (r + 1) * z.t3], NT)
        both = term if both is None else both + term
    spread = both[:CLASS_ROWS] + both[CLASS_ROWS:]
    dh = dot_full(wlc[1][:, :CLASS_ROWS], spread, NN)
    own = dot_full(wlc[0][:, :CLASS_ROWS], grad[...], NN)
    dh = dh + jnp.concatenate([own, jnp.zeros((256, z.t2 - z.t3), F32)], axis=1)
    dpre2[...] = dh * slope[...]
    rows = pl.ds(pl.multiple_of(pos[3] * 128, 128), 128)
    scaled = dot_split((wmh[1, rows, :], wml[1, rows, :]), halves(dpre2[...]), NN) * inverse(z, mine, z.at_c2, z.l2)
    for r in range(2 * z.rl):
        out[r] = scaled
    dwl[0] = dot_full(grad[...], h2[:, : z.t3], NT)
    dwl[1] = dot_full(spread, h2[...], NT)


def row_sums(value):
    ones = jnp.ones((8, value.shape[1]), BF16)
    high, low = halves(value)
    return dot(ones, high, NT) + dot(ones, low, NT)


def grads_body(z, pos, gall, a2, dpre2, wmh, wml, slope, x1, y2, dwl, grad, loss, out, first, mid, last):
    c = pos[3]
    mine = pl.ds(pl.multiple_of(c * 128, 128), 128)
    both = None
    for r in range(z.blocks):
        table = jnp.concatenate(halves(gall[r]), axis=0)
        term = dot(table, a2[:, r * z.t2 : (r + 1) * z.t2], NT)
        both = term if both is None else both + term
    dh = both[:128] + both[128:]
    at_own = dot_split((wmh[0, mine, :], wml[0, mine, :]), halves(dpre2[...]), NN)
    dh = dh + jnp.concatenate([at_own, jnp.zeros((128, z.t1 - z.t2), F32)], axis=1)
    dpre1 = dh * slope[mine]
    half2 = dpre2[mine]
    first[...] = dot_full(x1[...], dpre1, NT)
    mid[...] = dot_full(y2[...], half2, NT)
    b1, b2, b3 = row_sums(dpre1), row_sums(half2), row_sums(grad[...])
    last[...] = jnp.zeros_like(last)
    core0 = jnp.where(c == 0, 1.0, 0.0)
    for s in range(4):
        last[s, :CLASS_ROWS, :64] = dwl[c, :, 64 * s : 64 * s + 64]
        here = jnp.where(c == s // 2, 1.0, 0.0)
        at = 64 * (s % 2)
        last[s, ROW_HIDDEN : ROW_HIDDEN + 1, :64] = b1[0:1, at : at + 64] * here
        last[s, ROW_HIDDEN + 1 : ROW_HIDDEN + 2, :64] = b2[0:1, at : at + 64] * here
        last[s, ROW_LAST : ROW_LAST + 1, :LANE_LOSS] = b3[0:1, :LANE_LOSS] * core0
        last[s, ROW_LAST : ROW_LAST + 1, LANE_LOSS : LANE_LOSS + 1] = loss[0:1, 0:1] * core0
    for p in range(z.blocks):
        for s in range(4):
            e = z.nf * p
            at = 128 * (e // 32) + 32 * s + e % 32
            out[p, s * z.nf : (s + 1) * z.nf] = first[at : at + z.nf]
            e = z.nm * p
            at = 256 * (e // 64) + 64 * s + e % 64
            out[p, z.at_m + s * z.nm : z.at_m + (s + 1) * z.nm] = mid[at : at + z.nm]
            e = z.nl * p
            two = [last[s, e + h * z.pair : e + (h + 1) * z.pair, :64] for h in range(2)]
            out[p, z.at_l + s * z.pair : z.at_l + (s + 1) * z.pair] = jnp.concatenate(two, axis=1)


def sum_grads_body(z, pos, part, out):
    total = part[0]
    for r in range(1, z.blocks):
        total = total + part[r]
    out[...] = total


def share_body(z, pos, own, other, out):
    nf, nm, pair = z.nf, z.nm, z.pair
    total = own[...] + other[...]
    piece = pos[2] * z.rl + pos[1]
    lane = lax.broadcasted_iota(I32, (1, LANES), 1)
    squares = jnp.sum(total[: z.at_l] * total[: z.at_l], axis=0, keepdims=True)
    for s in range(4):
        for i in range(pair):
            row = total[z.at_l + s * pair + i : z.at_l + s * pair + i + 1]
            at = piece * z.nl + i + jnp.where(lane < 64, 0, pair)
            keep = at < ROW_LAST
            if s == 0:
                keep = jnp.logical_or(keep, jnp.logical_and(at == ROW_LAST, lane % 64 < 47))
            squares = squares + jnp.where(keep, row * row, 0.0)
    squares = jnp.broadcast_to(jnp.sum(squares, axis=1, keepdims=True), (1, LANES))
    pad = z.share_rows - nf - nm - pair - 1
    for s in range(4):
        rows = [
            total[s * nf : (s + 1) * nf],
            total[z.at_m + s * nm : z.at_m + (s + 1) * nm],
            total[z.at_l + s * pair : z.at_l + (s + 1) * pair],
            squares,
        ]
        if pad:
            rows.append(jnp.zeros((pad, LANES), F32))
        rows = jnp.concatenate(rows, axis=0)
        for lead in range(z.rl):
            out[4 * lead + s] = rows


def update_body(z, pos, whole, mine, *refs):
    w, m, v = refs[0:5], refs[5:10], refs[10:15]
    new, moment, square = refs[15:20], refs[20:25], refs[25:30]
    loss, weight_sum, norm = refs[30:33]
    nf, nm, nl, pair = z.nf, z.nm, z.nl, z.pair
    h = nf + nm
    total = whole[0, h + pair : h + pair + 1, 0:1]
    for p in range(1, 4 * z.rl):
        total = total + whole[p, h + pair : h + pair + 1, 0:1]
    root = jnp.sqrt(total)
    scale = jnp.minimum(1.0, 0.01 / root)
    norm[...] = root
    weight_sum[...] = mine[z.id_rows + CLASS_ROWS : z.id_rows + CLASS_ROWS + 1, 0:1]

    def adamw(weight, grad, first, second):
        grad = grad * scale
        mo = 0.9 * first + 0.1 * grad
        sq = 0.999 * second + 0.001 * grad * grad
        corrected = mo / (1.0 - 0.9**STEP)
        rt = jnp.sqrt(sq / (1.0 - 0.999**STEP))
        return (weight - 0.05 * (corrected / (rt + 1e-08) + 0.01 * weight), mo, sq)

    def put(i, at, grad):
        outs = adamw(w[i][at], grad, m[i][at], v[i][at])
        new[i][at], moment[i][at], square[i][at] = outs

    def source(p, c):
        return 4 * (p % z.rl) + 2 * (p // z.rl) + c

    def class_row(row, c):
        p, i = row // nl, row % nl
        at, lane = h + i % pair, 64 * (i // pair)
        return whole[source(p, c), at : at + 1, lane : lane + 64]

    for p in range(z.blocks):
        a, b = source(p, 0), source(p, 1)
        e = nf * p
        g = jnp.concatenate([whole[a, :nf], whole[b, :nf]], axis=1)
        put(0, (e // 32, slice(e % 32, e % 32 + nf), slice(None)), g)
        e = nm * p
        g = jnp.concatenate([whole[a, nf:h], whole[b, nf:h]], axis=1)
        put(1, (e // 64, slice(e % 64, e % 64 + nm), slice(None)), g)
        for j, src in enumerate((a, b)):
            for half in range(2):
                at = nl * p + half * pair
                end = min(at + pair, 47)
                if at < end:
                    g = whole[src, h : h + end - at, 64 * half : 64 * half + 64]
                    put(2, (slice(at, end), j, slice(None)), g)
    for j in range(2):
        g = jnp.where(pos[2] == 0, class_row(ROW_HIDDEN + j, 0), class_row(ROW_HIDDEN + j, 1))
        put(3, (slice(j, j + 1), slice(None)), g)
    row = class_row(ROW_LAST, 0)
    put(4, (slice(None), slice(None)), row[:, :47])
    loss[...] = row[:, LANE_LOSS : LANE_LOSS + 1]


def on_device(
    mesh, features, neigh_first, count_first, neigh_mid, count_mid, neigh_last, count_last, labels,
    w_first, w_mid, w_last, b_hidden, b_last,
    m_first, m_mid, m_last, m_hidden, m_bias,
    v_first, v_mid, v_last, v_hidden, v_bias,
):
    z = Sizes(mesh, features, neigh_first, neigh_mid, neigh_last)
    bind = functools.partial
    blocks = z.blocks

    def flip(value):
        return lax.ppermute(value, "c", [(0, 1), (1, 0)])

    def exchange(value):
        return lax.all_to_all(value, ("y", "rl"), 0, 0)

    def swapped(value):
        return jnp.transpose(value, (2, 0, 1))

    raw = (
        swapped(neigh_first), count_first, swapped(neigh_mid), count_mid, swapped(neigh_last), count_last, labels,
    )
    ids = call(
        bind(ids_body, z), [((4 * z.ranks, z.id_part, LANES), I32)], "ids", 58,
        scratch=[pltpu.VMEM((2, z.id_rows, LANES), I32), *like(*raw)], where=HBM,
    )(*raw)[0]
    raw = (jnp.transpose(features, (0, 2, 1)), w_first, w_mid, swapped(w_last), b_hidden)
    f0, f1, wmsg = call(
        bind(prep_body, z), [((32, z.s1), F32), ((32, z.s1), F32), ((248, 256), F32)], "prep", 58, scratch=like(*raw),
        where=HBM,
    )(*raw)
    got0, got1 = (
        lax.ppermute(f, ("zh", "y"), [(2 * zh + y, 2 * (y ^ j) + zh) for zh in range(2) for y in range(2)])
        for j, f in enumerate((f0, f1))
    )
    ids = lax.all_to_all(ids, ("y", "c", "zh", "rl"), 0, 0)
    w_across = lax.ppermute(wmsg, "y", [(0, 1), (1, 0)])
    a1, mine = call(
        bind(adjacency_first_body, z),
        [
            ((z.s1, blocks * z.t1), BF16), ((z.id_rows + CLASS_ROWS + 8, LANES), F32),
        ],
        "adjacency_first", 4 + blocks, us=6.0, scratch=tables(z, z.f1, z.l1, z.s1),
    )(ids)
    part = call(
        bind(first_body, z), [((blocks, 64, z.t1), F32)], "first", 4 + blocks, scratch=[pltpu.VMEM((128, z.s1), BF16)],
    )(a1, got0, got1, w_across)[0]
    part = exchange(part)
    half = call(bind(sum_first_body, z), [((128, z.t1), F32)], "sum_first", 8)(mine, part, got0, got1)[0]
    other = flip(half)
    walls = (wmsg, w_across, flip(w_across), flip(wmsg))
    w1h, w1l, w2h, w2l, wmh, wml, wlt, wlc, bias = call(
        weights_body,
        [
            ((256, 256), BF16), ((256, 256), BF16), ((256, 512), BF16), ((256, 512), BF16),
            ((2, 256, 256), BF16), ((2, 256, 256), BF16),
            ((2, CLASS_ROWS, 256), F32), ((2, 256, 128), F32), ((256, 128), F32),
        ],
        "weights", 8,
        scratch=[pltpu.VMEM((4, 248, 256), F32), pltpu.VMEM((256, 256), F32), pltpu.VMEM((512, 256), F32)],
    )(*walls, b_last[None], half)
    a2 = call(
        bind(adjacency_mid_body, z), [((z.t1, blocks * z.t2), BF16)], "adjacency_mid", 4, us=3.0,
        scratch=tables(z, z.f2, z.l2, z.t1),
    )(ids, half)[0]
    part, x1, h1, slope1 = call(
        bind(hidden_one_body, z),
        [((blocks, 128, z.t2), F32), ((256, z.t1), F32), ((256, z.t1), F32), ((256, z.t1), F32)],
        "hidden_one", 16,
    )(half, other, w1h, w1l, bias, a2)
    part = exchange(part)
    half = call(bind(sum_mid_body, z), [((128, z.t2), F32)], "sum_mid", 8)(mine, part)[0]
    other = flip(half)
    a3 = call(
        bind(adjacency_last_body, z), [((z.t2, blocks * z.t3), BF16)], "adjacency_last", 4, us=1.0,
        scratch=tables(z, z.f3, z.l3, z.t2),
    )(ids, half)[0]
    part, y2, h2, slope2, local = call(
        bind(hidden_two_body, z),
        [
            ((blocks, CLASS_ROWS, z.t3), F32),
            ((512, z.t2), F32), ((256, z.t2), F32), ((256, z.t2), F32), ((CLASS_ROWS, z.t3), F32),
        ],
        "hidden_two", 12,
    )(half, other, h1, w2h, w2l, bias, wlt, a3)
    part = exchange(part)
    backs = [((blocks, 128, z.t2), F32), ((256, z.t2), F32), ((2, CLASS_ROWS, 256), F32)]
    ends = [((CLASS_ROWS, z.t3), F32), ((8, LANES), F32)]
    part, grad, loss = call(bind(logits_body, z), [((blocks, CLASS_ROWS, z.t3), F32), *ends], "logits", 8)(
        mine, part, local, bias
    )
    part = exchange(part)
    part, dpre2, dwl = call(bind(back_last_body, z), backs, "back_last", 12, us=1.5)(
        mine, part, grad, a3, wlc, h2, slope2, wmh, wml
    )
    part = exchange(part)
    part = call(
        bind(grads_body, z), [((blocks, z.piece_rows, LANES), F32)], "grads", 12,
        scratch=[
            pltpu.VMEM((256, 128), F32), pltpu.VMEM((512, 128), F32),
            pltpu.VMEM((4, LAST_ROWS, LANES), F32),
        ],
    )(part, a2, dpre2, wmh, wml, slope1, x1, y2, dwl, grad, loss)[0]
    part = exchange(part)
    own = call(bind(sum_grads_body, z), [((z.piece_rows, LANES), F32)], "sum_grads", 8)(part)[0]
    other = lax.ppermute(own, "zh", [(0, 1), (1, 0)])
    part = call(bind(share_body, z), [((4 * z.rl, z.share_rows, LANES), F32)], "share", 8)(own, other)[0]
    whole = lax.all_to_all(part, ("rl", "y", "c"), 0, 0)

    params = (w_first, w_mid, swapped(w_last), b_hidden, b_last[None])
    firsts = (m_first, m_mid, swapped(m_last), m_hidden, m_bias[None])
    seconds = (v_first, v_mid, swapped(v_last), v_hidden, v_bias[None])
    shapes = [(p.shape, F32) for p in params]
    state = (*params, *firsts, *seconds)
    outs = call(
        bind(update_body, z), shapes * 3 + [((1, 1), F32)] * 3, "update", 8
    )(whole, mine, *state)
    results = []
    for g in range(3):
        a, b, c, d, e = outs[5 * g : 5 * g + 5]
        results += [a, b, jnp.transpose(c, (1, 2, 0)), d, e[0]]
    return tuple(results) + tuple(o[0, 0] for o in outs[15:])


def solution(mesh):
    rows, cols = mesh.shape["rows"], mesh.shape["cols"]
    fine = Mesh(mesh.devices.reshape(2, rows // 2, 2, cols // 2), ("zh", "rl", "y", "c"))
    r, c = ("zh", "rl"), ("y", "c")
    weights = (P(None, c, None),) * 3 + (P(None, c), P())
    nodes = (P(None, r, None), P(None, r))
    placed = (P(None, r, c),) + nodes * 3 + (P(None, r),) + weights * 3
    return jax.shard_map(
        functools.partial(on_device, fine),
        mesh=fine,
        in_specs=placed,
        out_specs=weights * 3 + (P(), P(), P()),
        check_vma=False,
    )
```

```python
import functools

import jax
import jax.numpy as jnp
from jax import lax
from jax.experimental import pallas as pl
from jax.experimental.pallas import tpu as pltpu
from jax.sharding import Mesh
from jax.sharding import PartitionSpec as P

STEP = 5
F32 = jnp.float32
BF16 = jnp.bfloat16
I32 = jnp.int32
LANES = 128
CLASS_ROWS = 48
LAST_ROWS = 64
ROW_HIDDEN = 48
ROW_LAST = 50
LANE_LOSS = 47
MIB = 1 << 20


def dims(left, right):
    return (((left,), (right,)), ((), ()))


NN, NT = dims(1, 0), dims(1, 1)


def dot(left, right, form):
    return lax.dot_general(left, right, form, preferred_element_type=F32)


def halves(value):
    high = value.astype(BF16)
    return high, (value - high.astype(F32)).astype(BF16)


def dot_split(left, right, form):
    (lh, ll), (rh, rl) = left, right
    return dot(lh, rh, form) + dot(lh, rl, form) + dot(ll, rh, form)


def dot_full(left, right, form):
    return dot_split(halves(left), halves(right), form)


def sigmoid(value):
    return 1.0 / (1.0 + jnp.exp(-value))


VMEM = pl.BlockSpec(memory_space=pltpu.VMEM)
HBM = pl.BlockSpec(memory_space=pltpu.HBM)


AXES = ("zh", "rl", "y", "c")


def call(body, outs, name, vmem, scratch=(), where=VMEM, us=1.0):
    def placed(*refs):
        body([lax.axis_index(a) for a in AXES], *refs)

    def run(*args):
        return pl.pallas_call(
            placed,
            out_shape=[jax.ShapeDtypeStruct(s, d) for s, d in outs],
            in_specs=[where] * len(args),
            out_specs=[VMEM] * len(outs),
            scratch_shapes=list(scratch),
            name=name,
            compiler_params=pltpu.CompilerParams(vmem_limit_bytes=vmem * MIB),
            cost_estimate=pl.CostEstimate(flops=0, bytes_accessed=int(us * 3.6e6), transcendentals=0),
        )(*args)

    return run


def fetch(sources, targets, sems):
    copies = [pltpu.make_async_copy(s, t, sems.at[i]) for i, (s, t) in enumerate(zip(sources, targets))]
    for copy in copies:
        copy.start()
    for copy in copies:
        copy.wait()


def like(*arrays):
    return [pltpu.VMEM(a.shape, a.dtype) for a in arrays] + [pltpu.SemaphoreType.DMA((len(arrays),))]


class Sizes:
    def __init__(self, mesh, features, neigh_first, neigh_mid, neigh_last):
        self.ranks = mesh.shape["zh"] * mesh.shape["rl"]
        self.rl = mesh.shape["rl"]
        self.s1, self.t1 = features.shape[1], neigh_first.shape[1]
        self.t2, self.t3 = neigh_mid.shape[1], neigh_last.shape[1]
        self.f1, self.f2, self.f3 = neigh_first.shape[2], neigh_mid.shape[2], neigh_last.shape[2]
        l1, l2, l3 = self.t1 // LANES, self.t2 // LANES, self.t3 // LANES
        self.l1, self.l2, self.l3 = l1, l2, l3
        self.at_first = 0
        self.at_mid = self.at_first + self.f1 * l1
        self.at_last = self.at_mid + self.f2 * l2
        self.at_label = self.at_last + self.f3 * l3
        self.at_c1 = self.at_label + 2 * l3
        self.at_c2 = self.at_c1 + l1
        self.at_c3 = self.at_c2 + l2
        self.id_rows = -(-(self.at_c3 + l3) // 32) * 32
        self.id_part = self.id_rows // 4
        self.blocks = 2 * self.rl
        self.nf, self.nm, self.nl = 64 // self.blocks, 128 // self.blocks, LAST_ROWS // self.blocks
        self.pair = self.nl // 2
        self.at_m, self.at_l, self.piece_rows = 4 * self.nf, 4 * (self.nf + self.nm), 4 * (self.nf + self.nm + self.pair)
        self.share_rows = -(-(self.nf + self.nm + self.pair + 1) // 8) * 8


def ids_body(z, pos, *refs):
    ids, rows = refs[7:9]
    nf, cf, nm, cm, nl, cl, labels = refs[9:16]
    fetch(refs[:7], refs[9:16], refs[16])

    def put(mb, at, value):
        for j in range(value.shape[1] // LANES):
            rows[mb, at + j : at + j + 1, :] = value[:, j * LANES : (j + 1) * LANES]

    for mb in range(2):
        for fan, nb, cnt, at, at_c in (
            (z.f1, nf, cf, z.at_first, z.at_c1),
            (z.f2, nm, cm, z.at_mid, z.at_c2),
            (z.f3, nl, cl, z.at_last, z.at_c3),
        ):
            count = cnt[mb : mb + 1, :]
            lanes = count.shape[1] // LANES
            for k in range(fan):
                put(mb, at + k * lanes, jnp.where(count > k, nb[k, mb : mb + 1, :], -1))
            put(mb, at_c, count)
        for other in range(2):
            put(mb, z.at_label + other * z.l3, labels[other : other + 1, :])
        end = z.at_c3 + z.l3
        if end < z.id_rows:
            rows[mb, end:, :] = jnp.zeros((z.id_rows - end, LANES), I32)
    part = pl.ds(pl.multiple_of((2 * pos[2] + pos[3]) * z.id_part, 8), z.id_part)
    for mb in range(2):
        mine = rows[mb, part]
        for s in range(4):
            for lead in range(z.rl):
                ids[(2 * s + mb) * z.rl + lead] = mine


def prep_body(z, pos, *refs):
    f0, f1, wmsg = refs[5:8]
    feats, wf, wm, wl, bh = refs[8:13]
    fetch(refs[:5], refs[8:13], refs[13])
    y = pos[2]
    f0[...] = feats[y]
    f1[...] = feats[1 - y]
    for j in range(2):
        wmsg[32 * j : 32 * j + 32, :] = wf[j]
        wmsg[64 + 64 * j : 128 + 64 * j, :] = wm[j]
    wmsg[192:248, :] = jnp.zeros((56, 256), F32)
    for j in range(2):
        wmsg[192 : 192 + 47, 64 * j : 64 * j + 64] = wl[:, j, :]
        wmsg[240:241, 64 * j : 64 * j + 64] = bh[j : j + 1, :]


def weights_body(pos, own, acr, dia, cor, blast, after, w1h, w1l, w2h, w2l, wmh, wml, wlt, wlc, bias, wall, f32a, f32b):
    s = 2 * pos[2] + pos[3]
    for at, part in ((s, own), (s ^ 2, acr), (s ^ 3, dia), (s ^ 1, cor)):
        wall[at] = part[...]
    for s in range(4):
        for j in range(2):
            f32a[128 * j + 32 * s : 128 * j + 32 * s + 32, :] = wall[s, 32 * j : 32 * j + 32, :]
            f32b[256 * j + 64 * s : 256 * j + 64 * s + 64, :] = wall[s, 64 + 64 * j : 128 + 64 * j, :]
            wlt[j, :, 64 * s : 64 * s + 64] = wall[s, 192 : 192 + CLASS_ROWS, 64 * j : 64 * j + 64]
    w1h[...], w1l[...] = halves(f32a[...].T)
    w2h[...], w2l[...] = halves(f32b[...].T)
    for j in range(2):
        wmh[j], wml[j] = halves(f32b[256 * j : 256 * j + 256, :])
        wlc[j] = jnp.concatenate([wlt[j], jnp.zeros((128 - CLASS_ROWS, 256), F32)], axis=0).T
    rows = [jnp.concatenate([wall[s, 240:241, 64 * j : 64 * j + 64] for s in range(4)], axis=1) for j in range(2)]
    last = jnp.concatenate([blast[...], jnp.zeros((1, 256 - 47), F32)], axis=1)
    packed = jnp.concatenate(rows + [last, jnp.zeros((125, 256), F32)], axis=0)
    bias[...] = packed.T


PIECE = 256


def all_rows(z, ids, row, zs):
    first = (row // z.id_part * 2 + zs) * z.rl
    return ids[first : first + z.rl, row % z.id_part, :]


def distinct(z, ids, at, fan, lanes, size, base, local, times):
    for zs in range(2):
        for j in range(lanes):
            rows = [all_rows(z, ids, at + k * lanes + j, zs) for k in range(fan)]
            count = [jnp.ones(rows[0].shape, F32) for _ in range(fan)]
            seen = [None] * fan
            for a in range(fan):
                for b in range(a + 1, fan):
                    same = rows[a] == rows[b]
                    count[a] = count[a] + jnp.where(same, 1.0, 0.0)
                    seen[b] = same if seen[b] is None else jnp.logical_or(seen[b], same)
            for k in range(fan):
                times[zs * lanes + j, k] = count[k]
                rel = rows[k] - base
                for g in range(size // PIECE):
                    inside = jnp.logical_and(rel >= g * PIECE, rel < (g + 1) * PIECE)
                    if seen[k] is not None:
                        inside = jnp.logical_and(inside, jnp.logical_not(seen[k]))
                    local[zs * lanes + j, g * fan + k] = jnp.where(inside, rel - g * PIECE, -1).astype(F32)


def adjacency_block(z, zs, lead, fan, lanes, size, local, times, at, out, column):
    for j in range(lanes):
        row = pl.ds(lead, 1)
        many = [jnp.broadcast_to(times[zs * lanes + j, k, row], (PIECE, LANES)).astype(BF16) for k in range(fan)]
        for g in range(size // PIECE):
            total = jnp.zeros((PIECE, LANES), BF16)
            for k in range(fan):
                name = jnp.broadcast_to(local[zs * lanes + j, g * fan + k, row], (PIECE, LANES)).astype(BF16)
                total = jnp.where(at == name, many[k], total)
            out[g * PIECE : (g + 1) * PIECE, column(j)] = total


def numbers():
    return lax.broadcasted_iota(I32, (PIECE, LANES), 0).astype(F32).astype(BF16)


def tables(z, fan, lanes, size):
    return [
        pltpu.VMEM((2 * lanes, size // PIECE * fan, z.rl, LANES), F32),
        pltpu.VMEM((2 * lanes, fan, z.rl, LANES), F32),
    ]


def adjacency_all(z, ids, first, fan, lanes, size, base, local, times, out):
    distinct(z, ids, first, fan, lanes, size, base, local, times)
    at = numbers()
    for zs in range(2):

        def block(lead, carry):
            def column(j):
                return pl.ds(pl.multiple_of(((zs * z.rl + lead) * lanes + j) * LANES, LANES), LANES)

            adjacency_block(z, zs, lead, fan, lanes, size, local, times, at, out, column)
            return carry

        lax.fori_loop(0, z.rl, block, 0)


def adjacency_first_body(z, pos, ids, adj, small, local, times):
    me = pos[2] * z.rl + pos[1]
    for q in range(4):
        small[q * z.id_part : (q + 1) * z.id_part] = ids[2 * q * z.rl + me].astype(F32)
    weight, total = class_weights(z, ids)
    n = z.id_rows
    small[n : n + CLASS_ROWS] = jnp.broadcast_to(weight, (CLASS_ROWS, LANES))
    small[n + CLASS_ROWS :] = jnp.broadcast_to(total, (8, LANES))
    adjacency_all(z, ids, z.at_first, z.f1, z.l1, z.s1, me * z.s1, local, times, adj)


def adjacency_mid_body(z, pos, ids, after, a2, local, times):
    me = pos[2] * z.rl + pos[1]
    adjacency_all(z, ids, z.at_mid, z.f2, z.l2, z.t1, me * z.t1, local, times, a2)


def adjacency_last_body(z, pos, ids, after, a3, local, times):
    me = pos[2] * z.rl + pos[1]
    adjacency_all(z, ids, z.at_last, z.f3, z.l3, z.t2, me * z.t2, local, times, a3)


def class_weights(z, ids):
    classes = lax.broadcasted_iota(I32, (CLASS_ROWS, LANES), 0)
    total = jnp.zeros((CLASS_ROWS, LANES), F32)
    for zs in range(2):
        for other in range(2 * z.l3):
            rows = all_rows(z, ids, z.at_label + other, zs)
            for lead in range(z.rl):
                total = total + jnp.where(classes == rows[lead : lead + 1], 1.0, 0.0)
    counts = jnp.sum(total, axis=1, keepdims=True)
    weight = 1.0 / jnp.maximum(counts, 1.0)
    return weight, jnp.sum(counts * weight, axis=0, keepdims=True)


def columns(pos, got0, got1, lanes):
    swap = pos[0] == 1
    a, b = got0[:, :lanes], got1[:, :lanes]
    return jnp.where(swap, b, a), jnp.where(swap, a, b)


def first_table(z, pos, got0, got1, table):
    width = 2 * got0.shape[0]
    rows = jnp.concatenate(columns(pos, got0, got1, z.s1), axis=0)
    table[:width], table[width:] = halves(rows)


def first_body(z, pos, adj, got0, got1, after, out, table):
    first_table(z, pos, got0, got1, table)
    for r in range(z.blocks):
        both = dot(table[...], adj[:, r * z.t1 : (r + 1) * z.t1], NN)
        out[r] = both[: both.shape[0] // 2] + both[both.shape[0] // 2 :]


def inverse(z, mine, at, lanes):
    row = jnp.concatenate([mine[at + j : at + j + 1, :] for j in range(lanes)], axis=1)
    return 1.0 / row


def sum_first_body(z, pos, mine, part, got0, got1, out):
    half = got0.shape[0]
    out[:half], out[half : 2 * half] = columns(pos, got0, got1, z.t1)
    total = part[0]
    for r in range(1, 2 * z.rl):
        total = total + part[r]
    out[2 * half :] = total * inverse(z, mine, z.at_c1, z.l1)


def put_columns(pos, own, other, out):
    c = pos[3]
    for j in range(2):
        for y in range(2):
            at = 128 * j + 64 * y
            out[pl.ds(pl.multiple_of(at + 32 * c, 32), 32)] = own[64 * j + 32 * y : 64 * j + 32 * y + 32]
            out[pl.ds(pl.multiple_of(at + 32 * (1 - c), 32), 32)] = other[64 * j + 32 * y : 64 * j + 32 * y + 32]


def hidden_one_body(z, pos, own, other, w1h, w1l, bias, a2, out, x1, h1, slope):
    c = pos[3]
    put_columns(pos, own, other, x1)
    high, low = halves(x1[...])

    def layer(rows, lanes):
        pre = dot_split((w1h[rows, :], w1l[rows, :]), (high[:, :lanes], low[:, :lanes]), NN) + bias[rows, 0:1]
        sigma = sigmoid(pre)
        return pre, sigma

    mine = pl.ds(pl.multiple_of(c * 128, 128), 128)
    rest = pl.ds(pl.multiple_of((1 - c) * 128, 128), 128)
    pre, sigma = layer(mine, z.t1)
    hidden = pre * sigma
    slope[...] = sigma * (1.0 + pre * (1.0 - sigma))
    h1[mine] = hidden[:, : z.t2]
    table = jnp.concatenate(halves(hidden), axis=0)
    pre, sigma = layer(rest, z.t2)
    h1[rest] = pre * sigma
    for r in range(2 * z.rl):
        both = dot(table, a2[:, r * z.t2 : (r + 1) * z.t2], NN)
        out[r] = both[:128] + both[128:]


def sum_mid_body(z, pos, mine, part, out):
    total = part[0]
    for r in range(1, 2 * z.rl):
        total = total + part[r]
    out[...] = total * inverse(z, mine, z.at_c2, z.l2)


def hidden_two_body(z, pos, own, other, h1, w2h, w2l, bias, wlt, a3, out, y2, h2, slope, local):
    c = pos[3]
    y2[:256] = h1[...]
    y2[pl.ds(pl.multiple_of(256 + c * 128, 128), 128)] = own[...]
    y2[pl.ds(pl.multiple_of(256 + (1 - c) * 128, 128), 128)] = other[...]
    pre = dot_split((w2h[...], w2l[...]), halves(y2[...]), NN) + bias[:, 1:2]
    sigma = sigmoid(pre)
    hidden = pre * sigma
    h2[...] = hidden
    slope[...] = sigma * (1.0 + pre * (1.0 - sigma))
    split = halves(hidden)
    local[...] = dot_split(halves(wlt[0]), (split[0][:, : z.t3], split[1][:, : z.t3]), NN)
    for_mean = dot_split(halves(wlt[1]), split, NN)
    table = jnp.concatenate(halves(for_mean), axis=0)
    for r in range(z.blocks):
        both = dot(table, a3[:, r * z.t3 : (r + 1) * z.t3], NN)
        out[r] = both[:CLASS_ROWS] + both[CLASS_ROWS:]


def logits_body(z, pos, mine, part, local, bias, out, grad, loss):
    total = part[0]
    for r in range(1, 2 * z.rl):
        total = total + part[r]
    recip = inverse(z, mine, z.at_c3, z.l3)
    logits = total * recip + local[...] + bias[:CLASS_ROWS, 2:3]
    classes = lax.broadcasted_iota(I32, logits.shape, 0)
    logits = jnp.where(classes < 47, logits, -jnp.inf)
    label = jnp.where(
        pos[0] == 0,
        mine[z.at_label : z.at_label + 1, :],
        mine[z.at_label + z.l3 : z.at_label + z.l3 + 1, :],
    ).astype(I32)
    onehot = jnp.where(classes == label, 1.0, 0.0)
    top = jnp.max(logits, axis=0, keepdims=True)
    powers = jnp.exp(logits - top)
    norm = jnp.sum(powers, axis=0, keepdims=True)
    weight = jnp.sum(onehot * mine[z.id_rows : z.id_rows + CLASS_ROWS], axis=0, keepdims=True)
    target = jnp.sum(jnp.where(classes == label, logits, 0.0), axis=0, keepdims=True)
    each = weight * (jnp.log(norm) + top - target)
    loss[...] = jnp.broadcast_to(jnp.sum(each, axis=1, keepdims=True), loss.shape)
    dlogits = weight * (powers / norm - onehot) / mine[z.id_rows + CLASS_ROWS : z.id_rows + CLASS_ROWS + 1, :]
    grad[...] = dlogits
    scaled = dlogits * recip
    for r in range(2 * z.rl):
        out[r] = scaled


def back_last_body(z, pos, mine, gall, grad, a3, wlc, h2, slope, wmh, wml, out, dpre2, dwl):
    both = None
    for r in range(2 * z.rl):
        table = jnp.concatenate(halves(gall[r]), axis=0)
        term = dot(table, a3[:, r * z.t3 : (r + 1) * z.t3], NT)
        both = term if both is None else both + term
    spread = both[:CLASS_ROWS] + both[CLASS_ROWS:]
    dh = dot_full(wlc[1][:, :CLASS_ROWS], spread, NN)
    own = dot_full(wlc[0][:, :CLASS_ROWS], grad[...], NN)
    dh = dh + jnp.concatenate([own, jnp.zeros((256, z.t2 - z.t3), F32)], axis=1)
    dpre2[...] = dh * slope[...]
    rows = pl.ds(pl.multiple_of(pos[3] * 128, 128), 128)
    scaled = dot_split((wmh[1, rows, :], wml[1, rows, :]), halves(dpre2[...]), NN) * inverse(z, mine, z.at_c2, z.l2)
    for r in range(2 * z.rl):
        out[r] = scaled
    dwl[0] = dot_full(grad[...], h2[:, : z.t3], NT)
    dwl[1] = dot_full(spread, h2[...], NT)


def row_sums(value):
    ones = jnp.ones((8, value.shape[1]), BF16)
    high, low = halves(value)
    return dot(ones, high, NT) + dot(ones, low, NT)


def grads_body(z, pos, gall, a2, dpre2, wmh, wml, slope, x1, y2, dwl, grad, loss, out, first, mid, last):
    c = pos[3]
    mine = pl.ds(pl.multiple_of(c * 128, 128), 128)
    both = None
    for r in range(z.blocks):
        table = jnp.concatenate(halves(gall[r]), axis=0)
        term = dot(table, a2[:, r * z.t2 : (r + 1) * z.t2], NT)
        both = term if both is None else both + term
    dh = both[:128] + both[128:]
    at_own = dot_split((wmh[0, mine, :], wml[0, mine, :]), halves(dpre2[...]), NN)
    dh = dh + jnp.concatenate([at_own, jnp.zeros((128, z.t1 - z.t2), F32)], axis=1)
    dpre1 = dh * slope[...]
    half2 = dpre2[mine]
    first[...] = dot_full(x1[...], dpre1, NT)
    mid[...] = dot_full(y2[...], half2, NT)
    b1, b2, b3 = row_sums(dpre1), row_sums(half2), row_sums(grad[...])
    last[...] = jnp.zeros_like(last)
    core0 = jnp.where(c == 0, 1.0, 0.0)
    for s in range(4):
        last[s, :CLASS_ROWS, :64] = dwl[c, :, 64 * s : 64 * s + 64]
        here = jnp.where(c == s // 2, 1.0, 0.0)
        at = 64 * (s % 2)
        last[s, ROW_HIDDEN : ROW_HIDDEN + 1, :64] = b1[0:1, at : at + 64] * here
        last[s, ROW_HIDDEN + 1 : ROW_HIDDEN + 2, :64] = b2[0:1, at : at + 64] * here
        last[s, ROW_LAST : ROW_LAST + 1, :LANE_LOSS] = b3[0:1, :LANE_LOSS] * core0
        last[s, ROW_LAST : ROW_LAST + 1, LANE_LOSS : LANE_LOSS + 1] = loss[0:1, 0:1] * core0
    for p in range(z.blocks):
        for s in range(4):
            e = z.nf * p
            at = 128 * (e // 32) + 32 * s + e % 32
            out[p, s * z.nf : (s + 1) * z.nf] = first[at : at + z.nf]
            e = z.nm * p
            at = 256 * (e // 64) + 64 * s + e % 64
            out[p, z.at_m + s * z.nm : z.at_m + (s + 1) * z.nm] = mid[at : at + z.nm]
            e = z.nl * p
            two = [last[s, e + h * z.pair : e + (h + 1) * z.pair, :64] for h in range(2)]
            out[p, z.at_l + s * z.pair : z.at_l + (s + 1) * z.pair] = jnp.concatenate(two, axis=1)


def sum_grads_body(z, pos, part, out):
    total = part[0]
    for r in range(1, z.blocks):
        total = total + part[r]
    out[...] = total


def share_body(z, pos, own, other, out):
    nf, nm, pair = z.nf, z.nm, z.pair
    total = own[...] + other[...]
    piece = pos[2] * z.rl + pos[1]
    lane = lax.broadcasted_iota(I32, (1, LANES), 1)
    squares = jnp.sum(total[: z.at_l] * total[: z.at_l], axis=0, keepdims=True)
    for s in range(4):
        for i in range(pair):
            row = total[z.at_l + s * pair + i : z.at_l + s * pair + i + 1]
            at = piece * z.nl + i + jnp.where(lane < 64, 0, pair)
            keep = at < ROW_LAST
            if s == 0:
                keep = jnp.logical_or(keep, jnp.logical_and(at == ROW_LAST, lane % 64 < 47))
            squares = squares + jnp.where(keep, row * row, 0.0)
    squares = jnp.broadcast_to(jnp.sum(squares, axis=1, keepdims=True), (1, LANES))
    pad = z.share_rows - nf - nm - pair - 1
    for s in range(4):
        rows = [
            total[s * nf : (s + 1) * nf],
            total[z.at_m + s * nm : z.at_m + (s + 1) * nm],
            total[z.at_l + s * pair : z.at_l + (s + 1) * pair],
            squares,
        ]
        if pad:
            rows.append(jnp.zeros((pad, LANES), F32))
        rows = jnp.concatenate(rows, axis=0)
        for lead in range(z.rl):
            out[4 * lead + s] = rows


def update_body(z, pos, whole, mine, *refs):
    w, m, v = refs[0:5], refs[5:10], refs[10:15]
    new, moment, square = refs[15:20], refs[20:25], refs[25:30]
    loss, weight_sum, norm = refs[30:33]
    nf, nm, nl, pair = z.nf, z.nm, z.nl, z.pair
    h = nf + nm
    total = whole[0, h + pair : h + pair + 1, 0:1]
    for p in range(1, 4 * z.rl):
        total = total + whole[p, h + pair : h + pair + 1, 0:1]
    root = jnp.sqrt(total)
    scale = jnp.minimum(1.0, 0.01 / root)
    norm[...] = root
    weight_sum[...] = mine[z.id_rows + CLASS_ROWS : z.id_rows + CLASS_ROWS + 1, 0:1]

    def adamw(weight, grad, first, second):
        grad = grad * scale
        mo = 0.9 * first + 0.1 * grad
        sq = 0.999 * second + 0.001 * grad * grad
        corrected = mo / (1.0 - 0.9**STEP)
        rt = jnp.sqrt(sq / (1.0 - 0.999**STEP))
        return (weight - 0.05 * (corrected / (rt + 1e-08) + 0.01 * weight), mo, sq)

    def put(i, at, grad):
        outs = adamw(w[i][at], grad, m[i][at], v[i][at])
        new[i][at], moment[i][at], square[i][at] = outs

    def source(p, c):
        return 4 * (p % z.rl) + 2 * (p // z.rl) + c

    def class_row(row, c):
        p, i = row // nl, row % nl
        at, lane = h + i % pair, 64 * (i // pair)
        return whole[source(p, c), at : at + 1, lane : lane + 64]

    for p in range(z.blocks):
        a, b = source(p, 0), source(p, 1)
        e = nf * p
        g = jnp.concatenate([whole[a, :nf], whole[b, :nf]], axis=1)
        put(0, (e // 32, slice(e % 32, e % 32 + nf), slice(None)), g)
        e = nm * p
        g = jnp.concatenate([whole[a, nf:h], whole[b, nf:h]], axis=1)
        put(1, (e // 64, slice(e % 64, e % 64 + nm), slice(None)), g)
        for j, src in enumerate((a, b)):
            for half in range(2):
                at = nl * p + half * pair
                end = min(at + pair, 47)
                if at < end:
                    g = whole[src, h : h + end - at, 64 * half : 64 * half + 64]
                    put(2, (slice(at, end), j, slice(None)), g)
    for j in range(2):
        g = jnp.where(pos[2] == 0, class_row(ROW_HIDDEN + j, 0), class_row(ROW_HIDDEN + j, 1))
        put(3, (slice(j, j + 1), slice(None)), g)
    row = class_row(ROW_LAST, 0)
    put(4, (slice(None), slice(None)), row[:, :47])
    loss[...] = row[:, LANE_LOSS : LANE_LOSS + 1]


def on_device(
    mesh, features, neigh_first, count_first, neigh_mid, count_mid, neigh_last, count_last, labels,
    w_first, w_mid, w_last, b_hidden, b_last,
    m_first, m_mid, m_last, m_hidden, m_bias,
    v_first, v_mid, v_last, v_hidden, v_bias,
):
    z = Sizes(mesh, features, neigh_first, neigh_mid, neigh_last)
    bind = functools.partial
    blocks = z.blocks

    def flip(value):
        return lax.ppermute(value, "c", [(0, 1), (1, 0)])

    def exchange(value):
        return lax.all_to_all(value, ("y", "rl"), 0, 0)

    def swapped(value):
        return jnp.transpose(value, (2, 0, 1))

    raw = (
        swapped(neigh_first), count_first, swapped(neigh_mid), count_mid, swapped(neigh_last), count_last, labels,
    )
    ids = call(
        bind(ids_body, z), [((4 * z.ranks, z.id_part, LANES), I32)], "ids", 58,
        scratch=[pltpu.VMEM((2, z.id_rows, LANES), I32), *like(*raw)], where=HBM,
    )(*raw)[0]
    raw = (jnp.transpose(features, (0, 2, 1)), w_first, w_mid, swapped(w_last), b_hidden)
    f0, f1, wmsg = call(
        bind(prep_body, z), [((32, z.s1), F32), ((32, z.s1), F32), ((248, 256), F32)], "prep", 58, scratch=like(*raw),
        where=HBM,
    )(*raw)
    got0, got1 = (
        lax.ppermute(f, ("zh", "y"), [(2 * zh + y, 2 * (y ^ j) + zh) for zh in range(2) for y in range(2)])
        for j, f in enumerate((f0, f1))
    )
    ids = lax.all_to_all(ids, ("y", "c", "zh", "rl"), 0, 0)
    w_across = lax.ppermute(wmsg, "y", [(0, 1), (1, 0)])
    a1, mine = call(
        bind(adjacency_first_body, z),
        [
            ((z.s1, blocks * z.t1), BF16), ((z.id_rows + CLASS_ROWS + 8, LANES), F32),
        ],
        "adjacency_first", 4 + blocks, us=6.0, scratch=tables(z, z.f1, z.l1, z.s1),
    )(ids)
    part = call(
        bind(first_body, z), [((blocks, 64, z.t1), F32)], "first", 4 + blocks, scratch=[pltpu.VMEM((128, z.s1), BF16)],
    )(a1, got0, got1, w_across)[0]
    part = exchange(part)
    half = call(bind(sum_first_body, z), [((128, z.t1), F32)], "sum_first", 8)(mine, part, got0, got1)[0]
    other = flip(half)
    walls = (wmsg, w_across, flip(w_across), flip(wmsg))
    w1h, w1l, w2h, w2l, wmh, wml, wlt, wlc, bias = call(
        weights_body,
        [
            ((256, 256), BF16), ((256, 256), BF16), ((256, 512), BF16), ((256, 512), BF16),
            ((2, 256, 256), BF16), ((2, 256, 256), BF16),
            ((2, CLASS_ROWS, 256), F32), ((2, 256, 128), F32), ((256, 128), F32),
        ],
        "weights", 8,
        scratch=[pltpu.VMEM((4, 248, 256), F32), pltpu.VMEM((256, 256), F32), pltpu.VMEM((512, 256), F32)],
    )(*walls, b_last[None], half)
    a2 = call(
        bind(adjacency_mid_body, z), [((z.t1, blocks * z.t2), BF16)], "adjacency_mid", 4, us=3.0,
        scratch=tables(z, z.f2, z.l2, z.t1),
    )(ids, half)[0]
    part, x1, h1, slope1 = call(
        bind(hidden_one_body, z),
        [((blocks, 128, z.t2), F32), ((256, z.t1), F32), ((256, z.t2), F32), ((128, z.t1), F32)],
        "hidden_one", 16,
    )(half, other, w1h, w1l, bias, a2)
    part = exchange(part)
    half = call(bind(sum_mid_body, z), [((128, z.t2), F32)], "sum_mid", 8)(mine, part)[0]
    other = flip(half)
    a3 = call(
        bind(adjacency_last_body, z), [((z.t2, blocks * z.t3), BF16)], "adjacency_last", 4, us=1.0,
        scratch=tables(z, z.f3, z.l3, z.t2),
    )(ids, half)[0]
    part, y2, h2, slope2, local = call(
        bind(hidden_two_body, z),
        [
            ((blocks, CLASS_ROWS, z.t3), F32),
            ((512, z.t2), F32), ((256, z.t2), F32), ((256, z.t2), F32), ((CLASS_ROWS, z.t3), F32),
        ],
        "hidden_two", 12,
    )(half, other, h1, w2h, w2l, bias, wlt, a3)
    part = exchange(part)
    backs = [((blocks, 128, z.t2), F32), ((256, z.t2), F32), ((2, CLASS_ROWS, 256), F32)]
    ends = [((CLASS_ROWS, z.t3), F32), ((8, LANES), F32)]
    part, grad, loss = call(bind(logits_body, z), [((blocks, CLASS_ROWS, z.t3), F32), *ends], "logits", 8)(
        mine, part, local, bias
    )
    part = exchange(part)
    part, dpre2, dwl = call(bind(back_last_body, z), backs, "back_last", 12, us=1.5)(
        mine, part, grad, a3, wlc, h2, slope2, wmh, wml
    )
    part = exchange(part)
    part = call(
        bind(grads_body, z), [((blocks, z.piece_rows, LANES), F32)], "grads", 12,
        scratch=[
            pltpu.VMEM((256, 128), F32), pltpu.VMEM((512, 128), F32),
            pltpu.VMEM((4, LAST_ROWS, LANES), F32),
        ],
    )(part, a2, dpre2, wmh, wml, slope1, x1, y2, dwl, grad, loss)[0]
    part = exchange(part)
    own = call(bind(sum_grads_body, z), [((z.piece_rows, LANES), F32)], "sum_grads", 8)(part)[0]
    other = lax.ppermute(own, "zh", [(0, 1), (1, 0)])
    part = call(bind(share_body, z), [((4 * z.rl, z.share_rows, LANES), F32)], "share", 8)(own, other)[0]
    whole = lax.all_to_all(part, ("rl", "y", "c"), 0, 0)

    params = (w_first, w_mid, swapped(w_last), b_hidden, b_last[None])
    firsts = (m_first, m_mid, swapped(m_last), m_hidden, m_bias[None])
    seconds = (v_first, v_mid, swapped(v_last), v_hidden, v_bias[None])
    shapes = [(p.shape, F32) for p in params]
    state = (*params, *firsts, *seconds)
    outs = call(
        bind(update_body, z), shapes * 3 + [((1, 1), F32)] * 3, "update", 8
    )(whole, mine, *state)
    results = []
    for g in range(3):
        a, b, c, d, e = outs[5 * g : 5 * g + 5]
        results += [a, b, jnp.transpose(c, (1, 2, 0)), d, e[0]]
    return tuple(results) + tuple(o[0, 0] for o in outs[15:])


def solution(mesh):
    rows, cols = mesh.shape["rows"], mesh.shape["cols"]
    fine = Mesh(mesh.devices.reshape(2, rows // 2, 2, cols // 2), ("zh", "rl", "y", "c"))
    r, c = ("zh", "rl"), ("y", "c")
    weights = (P(None, c, None),) * 3 + (P(None, c), P())
    nodes = (P(None, r, None), P(None, r))
    placed = (P(None, r, c),) + nodes * 3 + (P(None, r),) + weights * 3
    return jax.shard_map(
        functools.partial(on_device, fine),
        mesh=fine,
        in_specs=placed,
        out_specs=weights * 3 + (P(), P(), P()),
        check_vma=False,
    )
```
